128 devices in a mesh: blk: 32 (over z, y, core), sub: 4 (over x).
Axes of the slice: x: 4, y: 4, z: 4, core: 2. Of those that a mesh axis runs over, the one named last changes fastest.
Arguments:
- gcm_state: float32 [6, 32, 64, 512], P(None, None, 'blk', 'sub'), may hold values from -6 to 6
- crm_state: bfloat16 [2, 32, 64, 32768], P(None, None, None, ('blk', 'sub')), may hold values from -6 to 6
- owner: int32 [64, 512], P('blk', 'sub'), may hold values from 0 to 127, as said below
- branch: int32 [64, 512], P('blk', 'sub'), may hold values 0 or 1
- diffusion: float32 [6, 32], replicated, may hold values from 0.03 to 0.24
Outputs:
- gcm_next: float32 [6, 32, 64, 512], P(None, None, 'blk', 'sub')
- crm_stats: float32 [2, 32, 64, 512], P(None, None, 'blk', 'sub')
The draws below stay inside these ranges and needn't reach their ends.
Inputs may be any that keep to these rules, and one draw needn't show every extreme that they name: Every device sends exactly 2 of its columns to each device (itself included); every owner receives exactly 256 columns.
All inputs are finite; a program needn't handle non-finite values. No bound on the sum of `branch` on one device may be relied on, other than what follows from the above.
Results may differ from the reference program's by a relative error of at most 0.0003.
Values sent between devices are 32-bit elements; how exact they have to be, the bound alone decides.
No kernel may reach another device: no remote copies, remote signals or barrier semaphores. Data moves between devices by JAX's collectives and lax.ppermute only.
A program may use at most 64 MiB of HBM per device.

```python
import math
import jax
import jax.numpy as jnp
from jax import lax

LEV = 32
NXC = 64
SUBSTEPS = 4
CX = 128
CY = 2
COLS_DEV = 256
NY = 64
NX = 512
TOTAL = 32768
N_BLK = 32
N_SUB = 4


def draw_owner(key, part):
    key = jax.random.fold_in(key, 11)
    key_label, key_offset = jax.random.split(key, 2)
    devices = N_BLK * N_SUB
    capacity = COLS_DEV // devices
    scores = jax.random.randint(key_label, (devices, COLS_DEV), 0, 1 << 20) * COLS_DEV + jnp.arange(COLS_DEV, dtype=jnp.int32)[None, :]
    labels = jnp.argsort(scores, axis=1, stable=True).astype(jnp.int32) // capacity
    offsets = jax.random.randint(key_offset, (devices, 1), 0, devices)
    owners = (labels + offsets) % devices
    owners = owners.reshape(N_BLK, N_SUB, CY, CX).transpose(0, 2, 1, 3).reshape(NY, NX)
    return owners.astype(jnp.int32)


def with_ends(array, key, smallest, high):
    spot = [jax.random.randint(jax.random.fold_in(key, axis), (), 0, length) for axis, length in enumerate(array.shape)]
    main_axis = array.shape.index(max(array.shape))
    next_to = spot[:main_axis] + [(spot[main_axis] + 1) % array.shape[main_axis]] + spot[main_axis + 1:]
    return array.at[tuple(spot)].set(smallest).at[tuple(next_to)].set(high)


def block_scale(rng, extent, shards, smallest, top_value):
    def one(axis_at, shards_of):
        draws = jax.random.uniform(jax.random.fold_in(jax.random.fold_in(rng, 6), axis_at), (shards_of,), jnp.float32, smallest / len(shards), top_value / len(shards))
        return jnp.repeat(jnp.exp(draws), extent[axis_at] // shards_of).reshape((-1,) + (1,) * (len(extent) - axis_at - 1))

    loudness = one(*shards[0])
    for cut in shards[1:]:
        loudness = loudness * one(*cut)
    return loudness


def gaussian(key, shape, scale, bound, cuts=(), kind=jnp.bfloat16):
    values = jax.random.normal(key, shape, jnp.float32) * scale
    if len(cuts) > 0:
        values = block_scale(key, shape, cuts, -0.22, 0.18) * values
    return jnp.clip(values, min=-bound, max=bound).astype(kind)


def setup_inputs(seed: int = 0) -> dict:
    keys = jax.random.split(jax.random.key(seed), 6)
    return {
        "gcm_state": gaussian(keys[0], (6, LEV, NY, NX), 1.0, 6.0, ((2, 32), (3, 4)), jnp.float32),
        "crm_state": gaussian(keys[1], (2, LEV, NXC, TOTAL), 1.0, 6.0, ((3, 128),)),
        "owner": draw_owner(jax.random.fold_in(keys[5], 71), 0),
        "branch": with_ends((jax.random.randint(keys[3], (NY, NX), 0, 3) < 1).astype(jnp.int32), jax.random.fold_in(keys[3], 1), 0, 1),
        "diffusion": jnp.clip(jnp.exp(jax.random.uniform(keys[4], (6, LEV), jnp.float32, math.log(0.03), math.log(0.24))), 0.03, 0.24),
    }


def advect(field, horizontal, vertical):
    right_flux = jnp.maximum(horizontal, 0.0) * field + jnp.minimum(horizontal, 0.0) * jnp.roll(field, -1, axis=1)
    field = field - (right_flux - jnp.roll(right_flux, 1, axis=1))
    inner = jnp.maximum(vertical, 0.0) * field[:-1] + jnp.minimum(vertical, 0.0) * field[1:]
    border = jnp.zeros_like(field[:1])
    upward = jnp.concatenate([inner, border], axis=0)
    downward = jnp.concatenate([border, inner], axis=0)
    return field - (upward - downward)


def cloud_model(crm_fields, forcing, branch_value):
    temper = crm_fields[0].astype(jnp.float32)
    moisture = crm_fields[1].astype(jnp.float32)
    horizontal = (0.45 * jnp.tanh(forcing[2]))[:, None, :]
    tilted = jnp.tanh(forcing[3])
    vertical = (0.15 * (tilted[:-1] + tilted[1:]))[:, None, :]
    cond_rate = jnp.where(branch_value > 0.5, 0.6, 0.2)[None, None, :]
    rainfall = jnp.zeros_like(temper)
    for substep in range(SUBSTEPS):
        temper = advect(temper, horizontal, vertical)
        moisture = advect(moisture, horizontal, vertical)
        temper = temper + 0.25 * (forcing[0][:, None, :] - jnp.mean(temper, axis=1, keepdims=True)) + 0.2 * forcing[4][:, None, :]
        moisture = moisture + 0.25 * (forcing[1][:, None, :] - jnp.mean(moisture, axis=1, keepdims=True)) + 0.2 * forcing[5][:, None, :]
        saturation = 0.5 * jnp.exp(0.3 * temper)
        condensed = cond_rate * jnp.maximum(moisture - saturation, 0.0)
        moisture = moisture - condensed
        temper = temper + 1.5 * condensed
        rainfall = rainfall + condensed
    mean_temp = jnp.mean(temper, axis=1)
    spread = jnp.mean((temper - mean_temp[:, None, :]) ** 2, axis=1)
    return jnp.stack([mean_temp, jnp.mean(moisture, axis=1), jnp.mean(rainfall, axis=1), spread])


def reference(gcm_state, crm_state, owner, branch, diffusion):
    neighbours = jnp.roll(gcm_state, 1, axis=2) + jnp.roll(gcm_state, -1, axis=2)
    neighbours = neighbours + jnp.roll(gcm_state, 1, axis=3) + jnp.roll(gcm_state, -1, axis=3)
    advanced = gcm_state + diffusion[:, :, None, None] * (neighbours - 4.0 * gcm_state)
    devices = N_BLK * N_SUB
    row_index = jnp.arange(NY, dtype=jnp.int32)[:, None]
    col_index = jnp.arange(NX, dtype=jnp.int32)[None, :]
    device_index = (row_index // CY) * N_SUB + col_index // CX
    local_index = (row_index % CY) * CX + col_index % CX
    sort_key = ((owner * devices + device_index) * COLS_DEV + local_index).reshape(-1)
    ordering = jnp.argsort(sort_key).astype(jnp.int32)
    forcing_all = advanced.reshape(6, LEV, NY * NX)[:, :, ordering]
    flags_all = branch.reshape(-1)[ordering].astype(jnp.float32)

    def one_owner(block):
        start = block * COLS_DEV
        return cloud_model(lax.dynamic_slice_in_dim(crm_state, start, COLS_DEV, 3),
                           lax.dynamic_slice_in_dim(forcing_all, start, COLS_DEV, 2),
                           lax.dynamic_slice_in_dim(flags_all, start, COLS_DEV, 0))

    profiles = lax.map(one_owner, jnp.arange(devices, dtype=jnp.int32))
    profiles = profiles.transpose(1, 2, 0, 3).reshape(4, LEV, NY * NX)
    placed = jnp.zeros_like(profiles).at[:, :, ordering].set(profiles)
    placed = placed.reshape(4, LEV, NY, NX)
    return jnp.concatenate([placed[:2], advanced[2:]], axis=0), placed[2:]
```

```python
import math

import jax
import jax.numpy as jnp
from jax import lax
from jax.experimental import pallas as pl
from jax.experimental.pallas import tpu as pltpu
from jax.sharding import PartitionSpec as P

SUBSTEPS = 4
LEV = 32
NXC = 64
LANES = 128
DEVICES = 128
COLS = 256
FIELDS = 6
SUB = 8
INNER = NXC // SUB
GCM_ROWS = FIELDS * LEV * 2
ALPHA = 0.3 * math.log2(math.e)
BETA = 1.5 * ALPHA
SHIFT = math.log2(0.5 * BETA)
MIB = 1 << 20


def pieces(x):
    first = x.astype(jnp.bfloat16)
    rest = x - first.astype(jnp.float32)
    second = rest.astype(jnp.bfloat16)
    third = (rest - second.astype(jnp.float32)).astype(jnp.bfloat16)
    return first, second, third


def select_dot(x, chosen, dims, x_first):
    total = None
    for part in pieces(x):
        pair = (part, chosen) if x_first else (chosen, part)
        term = lax.dot_general(*pair, (dims, ((), ())), preferred_element_type=jnp.float32)
        total = term if total is None else total + term
    return total


def prepare_kernel(
    gcm, above, below, left, right, owner, branch, diffusion, advanced, outgoing, routes
):
    number = diffusion[...]
    lane = lax.broadcasted_iota(jnp.int32, (FIELDS * LEV, LANES), 1)
    level = lax.broadcasted_iota(jnp.int32, (LEV, LANES), 0)

    def rows(ref, y):
        return ref[pl.ds(y, FIELDS * LEV, stride=2), :]

    own = [rows(gcm, 0), rows(gcm, 1)]
    vertical = [rows(above, 1) + own[1], own[0] + rows(below, 0)]
    values = []
    for y in range(2):
        before = pltpu.roll(jnp.where(lane == LANES - 1, rows(left, y), own[y]), 1, axis=1)
        after = pltpu.roll(jnp.where(lane == 0, rows(right, y), own[y]), LANES - 1, axis=1)
        around = vertical[y] + after + before
        state = own[y] + number * (around - 4.0 * own[y])
        advanced[pl.ds(2 * 2 * LEV + y, 4 * LEV, stride=2), :] = state[2 * LEV :]
        field = [state[f * LEV : (f + 1) * LEV] for f in range(FIELDS)]
        warm = ALPHA * (0.25 * field[0] + 0.2 * field[4])
        wet = BETA * (0.25 * field[1] + 0.2 * field[5])
        drift = 0.45 * jnp.tanh(field[2])
        tilt = jnp.tanh(field[3])
        rise = 0.15 * (tilt + pltpu.roll(tilt, LEV - 1, axis=0))
        rate = jnp.where(branch[y : y + 1, :] == 1, 0.6, 0.2)
        rise = jnp.where(level == LEV - 1, rate, rise)
        values.append(jnp.concatenate([warm, wet, drift, rise], axis=0))
    values = jnp.concatenate(values, axis=1)

    device = lax.broadcasted_iota(jnp.int32, (DEVICES, LANES), 0)
    target = jnp.concatenate(
        [(device == owner[y : y + 1, :]).astype(jnp.float32) for y in range(2)], axis=1
    )
    earlier = (
        lax.broadcasted_iota(jnp.int32, (COLS, COLS), 0)
        < lax.broadcasted_iota(jnp.int32, (COLS, COLS), 1)
    ).astype(jnp.bfloat16)
    count = jnp.dot(target.astype(jnp.bfloat16), earlier, preferred_element_type=jnp.float32)
    for slot in range(2):
        here = jnp.where(count < 0.5, 1.0 - slot, 0.0 + slot)
        route = (target * here).astype(jnp.bfloat16)
        routes[slot] = route
        outgoing[pl.ds(slot, DEVICES, stride=2), :] = select_dot(
            values, route, ((1,), (1,)), False
        )


def spread_kernel(crm, state, sums):
    levels = crm.shape[1]
    moist = pl.program_id(0)
    scale = jnp.where(moist == 1, BETA, ALPHA)
    shift = jnp.where(moist == 1, 0.0, SHIFT)

    def level(k, carry):
        for half in range(2):
            x = crm[0, k, :, half * LANES : (half + 1) * LANES].astype(jnp.float32)
            x = x * scale + shift
            total = None
            for part in range(SUB):
                block = x[part * INNER : (part + 1) * INNER]
                state[0, half, pl.ds(k * NXC + part, INNER, stride=SUB), :] = block
                total = block if total is None else total + block
            sums[0, half, pl.ds(pl.multiple_of(k * SUB, SUB), SUB), :] = total
        return carry

    lax.fori_loop(0, levels, level, 0, unroll=4)


def cloud_kernel(incoming, start, sums, outgoing, state, coef, mean, total, square):
    level = lax.broadcasted_iota(jnp.int32, (LEV, LANES), 0)
    top = level == LEV - 1
    rates = []

    def up(x):
        return pltpu.roll(x, LEV - 1, axis=0)

    def down(x):
        return pltpu.roll(x, 1, axis=0)

    def folded(ref, *lead):
        out = None
        for part in range(SUB):
            x = ref[(*lead, pl.ds(part, LEV, stride=SUB), slice(None))]
            out = x if out is None else out + x
        return out

    for half in range(2):
        values = jnp.transpose(incoming[half * LANES : (half + 1) * LANES, :])
        rise = values[3 * LEV :]
        rates.append(rise[LEV - 1 :])
        rise = jnp.where(top, 0.0, rise)
        base = SHIFT * (1.0 - rise + down(rise))
        coef[0, half] = values[:LEV] + SHIFT - 0.75 * base
        coef[1, half] = values[LEV : 2 * LEV]
        coef[2, half] = values[2 * LEV : 3 * LEV]
        coef[3, half] = rise
        coef[7, half] = jnp.broadcast_to(rates[half], (LEV, LANES))
        for f in range(2):
            mean[f, half] = folded(sums, f, half) * (1.0 / NXC)

    def relax():
        for half in range(2):
            rise = coef[3, half]
            for f in range(2):
                now = mean[f, half]
                flux = rise * jnp.where(rise > 0.0, now, up(now))
                now = now - flux + down(flux)
                add = coef[f, half] - 0.25 * now
                coef[4 + f, half] = add
                mean[f, half] = now + add
                if f == 0:
                    coef[6, half] = now + add

    def settle():
        for half in range(2):
            rain = folded(total, half) * (1.0 / NXC)
            mean[0, half] = mean[0, half] + rain
            mean[1, half] = mean[1, half] - rain
            mean[2, half] = mean[2, half] + rain

    def sweep(source, half, last):
        rate = jnp.broadcast_to(coef[7, half, 0:1, :], (SUB, LANES))

        def row(index, k):
            return jnp.broadcast_to(coef[index, half, k : k + 1, :], (SUB, LANES))

        def drifted(f, k, size, positive):
            cells = [
                source[f, half, k * NXC + j * SUB : k * NXC + (j + 1) * SUB, :]
                for j in range(INNER)
            ]
            before = [pltpu.roll(cells[-1], 1, axis=0)] + cells[:-1]
            after = cells[1:] + [pltpu.roll(cells[0], SUB - 1, axis=0)]
            return [
                c + size * (jnp.where(positive, b, a) - c)
                for c, b, a in zip(cells, before, after)
            ]

        def level_of(k):
            drift = row(2, k)
            size, positive = jnp.abs(drift), drift > 0.0
            return [drifted(f, k, size, positive) for f in range(2)]

        now = level_of(0)
        below = None
        for k in range(LEV):
            add = [row(4, k), row(5, k)]
            if k < LEV - 1:
                after = level_of(k + 1)
                rise = row(3, k)
                upward = rise > 0.0
                flux = [
                    [rise * jnp.where(upward, a, b) for a, b in zip(now[f], after[f])]
                    for f in range(2)
                ]
            rained = None
            spread = None
            if last:
                middle = row(6, k)
            for j in range(INNER):
                new = []
                for f in range(2):
                    x = now[f][j]
                    if k < LEV - 1:
                        x = x - flux[f][j]
                    if k > 0:
                        x = x + below[f][j]
                    new.append(x + add[f])
                temper, moisture = new
                rain = rate * jnp.maximum(moisture - jnp.exp2(temper), 0.0)
                temper = temper + rain
                rained = rain if rained is None else rained + rain
                if last:
                    away = temper - middle
                    spread = away * away if spread is None else spread + away * away
                else:
                    at = slice(k * NXC + j * SUB, k * NXC + (j + 1) * SUB)
                    state[0, half, at, :] = temper
                    state[1, half, at, :] = moisture - rain
            total[half, k * SUB : (k + 1) * SUB, :] = rained
            if last:
                square[half, k * SUB : (k + 1) * SUB, :] = spread
            if k < LEV - 1:
                below, now = flux, after

    def substep(source, last):
        relax()

        def half_of(half, carry):
            sweep(source, half, last)
            return carry

        lax.fori_loop(0, 2, half_of, 0)
        if not last:
            settle()

    for half in range(2):
        mean[2, half] = jnp.zeros((LEV, LANES), jnp.float32)
    substep(start, False)

    def middle_step(step, carry):
        substep(state, False)
        return carry

    lax.fori_loop(0, SUBSTEPS - 2, middle_step, 0)
    substep(state, True)
    settle()
    for half in range(2):
        warm, wet, rain = mean[0, half], mean[1, half], mean[2, half]
        gap = warm - coef[6, half]
        spread = folded(square, half) * (1.0 / NXC) - gap * gap
        result = [
            (warm - SHIFT) * (1.0 / ALPHA),
            wet * (1.0 / BETA),
            rain * (1.0 / BETA),
            spread * (1.0 / (ALPHA * ALPHA)),
        ]
        outgoing[half * LANES : (half + 1) * LANES, :] = jnp.transpose(
            jnp.concatenate(result, axis=0)
        )


def home_kernel(returned, routes, advanced, gcm_next, stats):
    del advanced
    home = None
    for slot in range(2):
        back = returned[pl.ds(slot, DEVICES, stride=2), :]
        term = select_dot(jnp.transpose(back), routes[slot], ((1,), (0,)), True)
        home = term if home is None else home + term
    for y in range(2):
        part = home[:, y * LANES : (y + 1) * LANES]
        gcm_next[pl.ds(y, 2 * LEV, stride=2), :] = part[: 2 * LEV]
        stats[pl.ds(y, 2 * LEV, stride=2), :] = part[2 * LEV :]


def whole(shape):
    return pl.BlockSpec(shape, lambda *_: (0,) * len(shape))


def f32(*shape):
    return jax.ShapeDtypeStruct(shape, jnp.float32)


def transfer(rows):
    moved = lax.all_to_all(
        rows.reshape(DEVICES, 2, LANES), ("blk", "sub"), split_axis=0, concat_axis=0, tiled=True
    )
    return moved.reshape(COLS, LANES)


def body(gcm_state, crm_state, owner, branch, diffusion):
    gcm = gcm_state.reshape(GCM_ROWS, LANES)
    n_blk, n_sub = lax.axis_size("blk"), lax.axis_size("sub")

    def ring(n, step):
        return [(i, (i + step) % n) for i in range(n)]

    left = lax.ppermute(gcm, "sub", ring(n_sub, 1))
    right = lax.ppermute(gcm, "sub", ring(n_sub, -1))
    above = lax.ppermute(gcm, "blk", ring(n_blk, 1))
    below = lax.ppermute(gcm, "blk", ring(n_blk, -1))
    number = jnp.broadcast_to(diffusion.reshape(FIELDS * LEV, 1), (FIELDS * LEV, LANES))
    advanced, outgoing, routes = pl.pallas_call(
        prepare_kernel,
        out_shape=(
            f32(GCM_ROWS, LANES),
            f32(COLS, LANES),
            jax.ShapeDtypeStruct((2, DEVICES, COLS), jnp.bfloat16),
        ),
        compiler_params=pltpu.CompilerParams(vmem_limit_bytes=32 * MIB),
        name="prepare",
    )(gcm, above, below, left, right, owner, branch, number)

    chunk = 8
    state, sums = pl.pallas_call(
        spread_kernel,
        grid=(2, LEV // chunk),
        in_specs=[pl.BlockSpec((1, chunk, NXC, COLS), lambda f, k: (f, k, 0, 0))],
        out_specs=(
            pl.BlockSpec((1, 2, chunk * NXC, LANES), lambda f, k: (f, 0, k, 0)),
            pl.BlockSpec((1, 2, chunk * SUB, LANES), lambda f, k: (f, 0, k, 0)),
        ),
        out_shape=(f32(2, 2, LEV * NXC, LANES), f32(2, 2, LEV * SUB, LANES)),
        compiler_params=pltpu.CompilerParams(vmem_limit_bytes=16 * MIB),
        cost_estimate=pl.CostEstimate(
            flops=4 * 2 * LEV * NXC * COLS, bytes_accessed=6 * 2 * LEV * NXC * COLS, transcendentals=0
        ),
        name="spread",
    )(crm_state)

    incoming = transfer(outgoing)
    profiles = pl.pallas_call(
        cloud_kernel,
        out_shape=f32(COLS, LANES),
        scratch_shapes=[
            pltpu.VMEM((2, 2, LEV * NXC, LANES), jnp.float32),
            pltpu.VMEM((8, 2, LEV, LANES), jnp.float32),
            pltpu.VMEM((3, 2, LEV, LANES), jnp.float32),
            pltpu.VMEM((2, LEV * SUB, LANES), jnp.float32),
            pltpu.VMEM((2, LEV * SUB, LANES), jnp.float32),
        ],
        compiler_params=pltpu.CompilerParams(vmem_limit_bytes=32 * MIB),
        name="cloud",
    )(incoming, state, sums)
    returned = transfer(profiles)

    gcm_next, stats = pl.pallas_call(
        home_kernel,
        grid=(1,),
        in_specs=[
            whole((COLS, LANES)),
            whole((2, DEVICES, COLS)),
            pl.BlockSpec(memory_space=pl.ANY),
        ],
        out_specs=(whole((4 * LEV, LANES)), whole((4 * LEV, LANES))),
        out_shape=(f32(GCM_ROWS, LANES), f32(4 * LEV, LANES)),
        input_output_aliases={2: 0},
        compiler_params=pltpu.CompilerParams(vmem_limit_bytes=32 * MIB),
        name="home",
    )(returned, routes, advanced)
    return gcm_next.reshape(gcm_state.shape), stats.reshape(2, LEV, 2, LANES)


def solution(mesh):
    grid = P(None, None, "blk", "sub")
    return jax.shard_map(
        body,
        mesh=mesh,
        in_specs=(grid, P(None, None, None, ("blk", "sub")), P("blk", "sub"), P("blk", "sub"), P()),
        out_specs=(grid, grid),
        check_vma=False,
    )
```

```python
import math

import jax
import jax.numpy as jnp
from jax import lax
from jax.experimental import pallas as pl
from jax.experimental.pallas import tpu as pltpu
from jax.sharding import PartitionSpec as P

SUBSTEPS = 4
LEV = 32
NXC = 64
LANES = 128
DEVICES = 128
COLS = 256
FIELDS = 6
SUB = 8
INNER = NXC // SUB
GCM_ROWS = FIELDS * LEV * 2
CRM_CHUNK = 8
ALPHA = 0.3 * math.log2(math.e)
BETA = 1.5 * ALPHA
SHIFT = math.log2(0.5 * BETA)
MIB = 1 << 20


def pieces(x):
    first = x.astype(jnp.bfloat16)
    rest = x - first.astype(jnp.float32)
    second = rest.astype(jnp.bfloat16)
    third = (rest - second.astype(jnp.float32)).astype(jnp.bfloat16)
    return first, second, third


def select_dot(x, chosen, dims, x_first):
    total = None
    for part in pieces(x):
        pair = (part, chosen) if x_first else (chosen, part)
        term = lax.dot_general(*pair, (dims, ((), ())), preferred_element_type=jnp.float32)
        total = term if total is None else total + term
    return total


def rows_of(ref, y):
    return ref[pl.ds(y, FIELDS * LEV, stride=2), :]


def edge_kernel(gcm_hbm, first, last, gcm, arrival):
    copy = pltpu.make_async_copy(gcm_hbm, gcm, arrival)
    copy.start()
    first[...] = jnp.zeros_like(first)
    last[...] = jnp.zeros_like(last)
    copy.wait()
    rows = jnp.concatenate([rows_of(gcm, 0), rows_of(gcm, 1)], axis=0)
    for part in range(GCM_ROWS // LANES):
        turned = jnp.transpose(rows[part * LANES : (part + 1) * LANES])
        first[part : part + 1, :] = turned[:1]
        last[part : part + 1, :] = turned[LANES - 1 :]


def early_kernel(
    gcm_hbm, crm_hbm, owner_hbm, branch_hbm, diffusion_hbm,
    state, sums, partial, number, routes, rates,
    gcm, crm, owner, branch, diffusion, arrival, crm_arrival,
):
    loads = [
        pltpu.make_async_copy(source, target, arrival.at[n])
        for n, (source, target) in enumerate(
            [(owner_hbm, owner), (branch_hbm, branch), (diffusion_hbm, diffusion), (gcm_hbm, gcm)]
        )
    ]
    crm_loads = [
        pltpu.make_async_copy(
            crm_hbm.at[f, pl.ds(part * CRM_CHUNK, CRM_CHUNK)],
            crm.at[f, pl.ds(part * CRM_CHUNK, CRM_CHUNK)],
            crm_arrival.at[f, part],
        )
        for f in range(2)
        for part in range(LEV // CRM_CHUNK)
    ]
    for copy in loads + crm_loads:
        copy.start()

    for copy in loads[:3]:
        copy.wait()
    device = lax.broadcasted_iota(jnp.int32, (DEVICES, LANES), 0)
    target = jnp.concatenate(
        [(device == owner[y : y + 1, :]).astype(jnp.float32) for y in range(2)], axis=1
    )
    earlier = (
        lax.broadcasted_iota(jnp.int32, (COLS, COLS), 0)
        < lax.broadcasted_iota(jnp.int32, (COLS, COLS), 1)
    ).astype(jnp.bfloat16)
    count = jnp.dot(target.astype(jnp.bfloat16), earlier, preferred_element_type=jnp.float32)
    for slot in range(2):
        here = jnp.where(count < 0.5, 1.0 - slot, 0.0 + slot)
        routes[slot] = (target * here).astype(jnp.bfloat16)
    rates[...] = jnp.where(branch[...] == 1, 0.6, 0.2)
    for f in range(FIELDS):
        spread = jnp.broadcast_to(diffusion[f : f + 1, :], (LANES, LEV))
        number[f * LEV : (f + 1) * LEV, :] = jnp.transpose(spread)

    loads[3].wait()
    lane = lax.broadcasted_iota(jnp.int32, (FIELDS * LEV, LANES), 1)
    own = [rows_of(gcm, 0), rows_of(gcm, 1)]
    for y in range(2):
        before = jnp.where(lane == 0, 0.0, pltpu.roll(own[y], 1, axis=1))
        after = jnp.where(lane == LANES - 1, 0.0, pltpu.roll(own[y], LANES - 1, axis=1))
        around = own[1 - y] + after + before
        partial[y] = own[y] + number[...] * (around - 4.0 * own[y])

    for f, (scale, shift) in enumerate([(ALPHA, SHIFT), (BETA, 0.0)]):
        for part in range(LEV // CRM_CHUNK):
            crm_loads[f * (LEV // CRM_CHUNK) + part].wait()

            def level(n, carry):
                k = part * CRM_CHUNK + n
                for half in range(2):
                    x = crm[f, k, :, half * LANES : (half + 1) * LANES].astype(jnp.float32)
                    x = x * scale + shift
                    total = None
                    for row in range(SUB):
                        block = x[row * INNER : (row + 1) * INNER]
                        state[f, half, pl.ds(k * NXC + row, INNER, stride=SUB), :] = block
                        total = block if total is None else total + block
                    sums[f, half, pl.ds(pl.multiple_of(k * SUB, SUB), SUB), :] = total
                return carry

            lax.fori_loop(0, CRM_CHUNK, level, 0, unroll=4)


def prepare_kernel(partial, number, above, below, left, right, routes, rates, advanced, outgoing):
    lane = lax.broadcasted_iota(jnp.int32, (FIELDS * LEV, LANES), 1)
    level = lax.broadcasted_iota(jnp.int32, (LEV, LANES), 0)

    def columns(ref):
        turned = jnp.transpose(ref[...])
        column = jnp.concatenate([turned[:, n : n + 1] for n in range(GCM_ROWS // LANES)], axis=0)
        return column[: FIELDS * LEV], column[FIELDS * LEV :]

    vertical = [rows_of(above, 1), rows_of(below, 0)]
    west, east = columns(left), columns(right)
    values = []
    for y in range(2):
        side = jnp.where(lane == 0, west[y], jnp.where(lane == LANES - 1, east[y], 0.0))
        state = partial[y] + number[...] * (vertical[y] + side)
        advanced[pl.ds(2 * 2 * LEV + y, 4 * LEV, stride=2), :] = state[2 * LEV :]
        field = [state[f * LEV : (f + 1) * LEV] for f in range(FIELDS)]
        warm = ALPHA * (0.25 * field[0] + 0.2 * field[4])
        wet = BETA * (0.25 * field[1] + 0.2 * field[5])
        drift = 0.45 * jnp.tanh(field[2])
        tilt = jnp.tanh(field[3])
        rise = 0.15 * (tilt + pltpu.roll(tilt, LEV - 1, axis=0))
        rise = jnp.where(level == LEV - 1, rates[y : y + 1, :], rise)
        values.append(jnp.concatenate([warm, wet, drift, rise], axis=0))
    values = jnp.concatenate(values, axis=1)
    for slot in range(2):
        outgoing[pl.ds(slot, DEVICES, stride=2), :] = select_dot(
            values, routes[slot], ((1,), (1,)), False
        )


def cloud_kernel(incoming, start, sums, outgoing, state, coef, mean, total, square):
    level = lax.broadcasted_iota(jnp.int32, (LEV, LANES), 0)
    top = level == LEV - 1
    rates = []

    def up(x):
        return pltpu.roll(x, LEV - 1, axis=0)

    def down(x):
        return pltpu.roll(x, 1, axis=0)

    def folded(ref, *lead):
        out = None
        for part in range(SUB):
            x = ref[(*lead, pl.ds(part, LEV, stride=SUB), slice(None))]
            out = x if out is None else out + x
        return out

    for half in range(2):
        values = jnp.transpose(incoming[half * LANES : (half + 1) * LANES, :])
        rise = values[3 * LEV :]
        rates.append(rise[LEV - 1 :])
        rise = jnp.where(top, 0.0, rise)
        base = SHIFT * (1.0 - rise + down(rise))
        coef[0, half] = values[:LEV] + SHIFT - 0.75 * base
        coef[1, half] = values[LEV : 2 * LEV]
        coef[2, half] = values[2 * LEV : 3 * LEV]
        coef[3, half] = rise
        coef[7, half] = jnp.broadcast_to(rates[half], (LEV, LANES))
        for f in range(2):
            mean[f, half] = folded(sums, f, half) * (1.0 / NXC)

    def relax():
        for half in range(2):
            rise = coef[3, half]
            for f in range(2):
                now = mean[f, half]
                flux = rise * jnp.where(rise > 0.0, now, up(now))
                now = now - flux + down(flux)
                add = coef[f, half] - 0.25 * now
                coef[4 + f, half] = add
                mean[f, half] = now + add
                if f == 0:
                    coef[6, half] = now + add

    def settle():
        for half in range(2):
            rain = folded(total, half) * (1.0 / NXC)
            mean[0, half] = mean[0, half] + rain
            mean[1, half] = mean[1, half] - rain
            mean[2, half] = mean[2, half] + rain

    def sweep(source, half, last):
        rate = jnp.broadcast_to(coef[7, half, 0:1, :], (SUB, LANES))

        def row(index, k):
            return jnp.broadcast_to(coef[index, half, k : k + 1, :], (SUB, LANES))

        def drifted(f, k, size, positive):
            cells = [
                source[f, half, k * NXC + j * SUB : k * NXC + (j + 1) * SUB, :]
                for j in range(INNER)
            ]
            before = [pltpu.roll(cells[-1], 1, axis=0)] + cells[:-1]
            after = cells[1:] + [pltpu.roll(cells[0], SUB - 1, axis=0)]
            return [
                c + size * (jnp.where(positive, b, a) - c)
                for c, b, a in zip(cells, before, after)
            ]

        def level_of(k):
            drift = row(2, k)
            size, positive = jnp.abs(drift), drift > 0.0
            return [drifted(f, k, size, positive) for f in range(2)]

        now = level_of(0)
        below = None
        for k in range(LEV):
            add = [row(4, k), row(5, k)]
            if k < LEV - 1:
                after = level_of(k + 1)
                rise = row(3, k)
                upward = rise > 0.0
                flux = [
                    [rise * jnp.where(upward, a, b) for a, b in zip(now[f], after[f])]
                    for f in range(2)
                ]
            rained = None
            spread = None
            if last:
                middle = row(6, k)
            for j in range(INNER):
                new = []
                for f in range(2):
                    x = now[f][j]
                    if k < LEV - 1:
                        x = x - flux[f][j]
                    if k > 0:
                        x = x + below[f][j]
                    new.append(x + add[f])
                temper, moisture = new
                rain = rate * jnp.maximum(moisture - jnp.exp2(temper), 0.0)
                temper = temper + rain
                rained = rain if rained is None else rained + rain
                if last:
                    away = temper - middle
                    spread = away * away if spread is None else spread + away * away
                else:
                    at = slice(k * NXC + j * SUB, k * NXC + (j + 1) * SUB)
                    state[0, half, at, :] = temper
                    state[1, half, at, :] = moisture - rain
            total[half, k * SUB : (k + 1) * SUB, :] = rained
            if last:
                square[half, k * SUB : (k + 1) * SUB, :] = spread
            if k < LEV - 1:
                below, now = flux, after

    def substep(source, last):
        relax()

        def half_of(half, carry):
            sweep(source, half, last)
            return carry

        lax.fori_loop(0, 2, half_of, 0)
        if not last:
            settle()

    for half in range(2):
        mean[2, half] = jnp.zeros((LEV, LANES), jnp.float32)
    substep(start, False)

    def middle_step(step, carry):
        substep(state, False)
        return carry

    lax.fori_loop(0, SUBSTEPS - 2, middle_step, 0)
    substep(state, True)
    settle()
    for half in range(2):
        warm, wet, rain = mean[0, half], mean[1, half], mean[2, half]
        gap = warm - coef[6, half]
        spread = folded(square, half) * (1.0 / NXC) - gap * gap
        result = [
            (warm - SHIFT) * (1.0 / ALPHA),
            wet * (1.0 / BETA),
            rain * (1.0 / BETA),
            spread * (1.0 / (ALPHA * ALPHA)),
        ]
        outgoing[half * LANES : (half + 1) * LANES, :] = jnp.transpose(
            jnp.concatenate(result, axis=0)
        )


def home_kernel(returned, routes, advanced, gcm_next, stats):
    del advanced
    home = None
    for slot in range(2):
        back = returned[pl.ds(slot, DEVICES, stride=2), :]
        term = select_dot(jnp.transpose(back), routes[slot], ((1,), (0,)), True)
        home = term if home is None else home + term
    for y in range(2):
        part = home[:, y * LANES : (y + 1) * LANES]
        gcm_next[pl.ds(y, 2 * LEV, stride=2), :] = part[: 2 * LEV]
        stats[pl.ds(y, 2 * LEV, stride=2), :] = part[2 * LEV :]


def whole(shape):
    return pl.BlockSpec(shape, lambda *_: (0,) * len(shape))


def f32(*shape):
    return jax.ShapeDtypeStruct(shape, jnp.float32)


def transfer(rows):
    moved = lax.all_to_all(
        rows.reshape(DEVICES, 2, LANES), ("blk", "sub"), split_axis=0, concat_axis=0, tiled=True
    )
    return moved.reshape(COLS, LANES)


def body(gcm_state, crm_state, owner, branch, diffusion):
    gcm = gcm_state.reshape(GCM_ROWS, LANES)
    n_blk, n_sub = lax.axis_size("blk"), lax.axis_size("sub")

    def ring(n, step):
        return [(i, (i + step) % n) for i in range(n)]

    below = lax.ppermute(gcm, "blk", ring(n_blk, -1))
    above = lax.ppermute(gcm, "blk", ring(n_blk, 1))
    hbm = pl.BlockSpec(memory_space=pltpu.HBM)
    first, last = pl.pallas_call(
        edge_kernel,
        in_specs=[hbm],
        out_shape=(f32(SUB, LANES), f32(SUB, LANES)),
        scratch_shapes=[pltpu.VMEM((GCM_ROWS, LANES), jnp.float32), pltpu.SemaphoreType.DMA(())],
        compiler_params=pltpu.CompilerParams(vmem_limit_bytes=4 * MIB),
        name="edges",
    )(gcm)
    right = lax.ppermute(first, "sub", ring(n_sub, -1))
    left = lax.ppermute(last, "sub", ring(n_sub, 1))
    cells = 2 * LEV * NXC * COLS
    state, sums, partial, number, routes, rates = pl.pallas_call(
        early_kernel,
        in_specs=[hbm] * 5,
        out_shape=(
            f32(2, 2, LEV * NXC, LANES),
            f32(2, 2, LEV * SUB, LANES),
            f32(2, FIELDS * LEV, LANES),
            f32(FIELDS * LEV, LANES),
            jax.ShapeDtypeStruct((2, DEVICES, COLS), jnp.bfloat16),
            f32(2, LANES),
        ),
        scratch_shapes=[
            pltpu.VMEM((GCM_ROWS, LANES), jnp.float32),
            pltpu.VMEM((2, LEV, NXC, COLS), jnp.bfloat16),
            pltpu.VMEM((2, LANES), jnp.int32),
            pltpu.VMEM((2, LANES), jnp.int32),
            pltpu.VMEM((FIELDS, LEV), jnp.float32),
            pltpu.SemaphoreType.DMA((4,)),
            pltpu.SemaphoreType.DMA((2, LEV // CRM_CHUNK)),
        ],
        compiler_params=pltpu.CompilerParams(vmem_limit_bytes=16 * MIB),
        cost_estimate=pl.CostEstimate(flops=4 * cells, bytes_accessed=6 * cells, transcendentals=0),
        name="early",
    )(gcm, crm_state, owner, branch, diffusion)
    advanced, outgoing = pl.pallas_call(
        prepare_kernel,
        out_shape=(f32(GCM_ROWS, LANES), f32(COLS, LANES)),
        compiler_params=pltpu.CompilerParams(vmem_limit_bytes=8 * MIB),
        name="prepare",
    )(partial, number, above, below, left, right, routes, rates)

    incoming = transfer(outgoing)
    profiles = pl.pallas_call(
        cloud_kernel,
        out_shape=f32(COLS, LANES),
        scratch_shapes=[
            pltpu.VMEM((2, 2, LEV * NXC, LANES), jnp.float32),
            pltpu.VMEM((8, 2, LEV, LANES), jnp.float32),
            pltpu.VMEM((3, 2, LEV, LANES), jnp.float32),
            pltpu.VMEM((2, LEV * SUB, LANES), jnp.float32),
            pltpu.VMEM((2, LEV * SUB, LANES), jnp.float32),
        ],
        compiler_params=pltpu.CompilerParams(vmem_limit_bytes=12 * MIB),
        name="cloud",
    )(incoming, state, sums)
    returned = transfer(profiles)

    gcm_next, stats = pl.pallas_call(
        home_kernel,
        grid=(1,),
        in_specs=[
            whole((COLS, LANES)),
            whole((2, DEVICES, COLS)),
            pl.BlockSpec(memory_space=pl.ANY),
        ],
        out_specs=(whole((4 * LEV, LANES)), whole((4 * LEV, LANES))),
        out_shape=(f32(GCM_ROWS, LANES), f32(4 * LEV, LANES)),
        input_output_aliases={2: 0},
        compiler_params=pltpu.CompilerParams(vmem_limit_bytes=8 * MIB),
        name="home",
    )(returned, routes, advanced)
    return gcm_next.reshape(gcm_state.shape), stats.reshape(2, LEV, 2, LANES)


def solution(mesh):
    grid = P(None, None, "blk", "sub")
    return jax.shard_map(
        body,
        mesh=mesh,
        in_specs=(grid, P(None, None, None, ("blk", "sub")), P("blk", "sub"), P("blk", "sub"), P()),
        out_specs=(grid, grid),
        check_vma=False,
    )
```

```python
import math

import jax
import jax.numpy as jnp
from jax import lax
from jax.experimental import pallas as pl
from jax.experimental.pallas import tpu as pltpu
from jax.sharding import PartitionSpec as P

SUBSTEPS = 4
LEV = 32
NXC = 64
LANES = 128
DEVICES = 128
COLS = 256
FIELDS = 6
SUB = 8
INNER = NXC // SUB
GCM_ROWS = FIELDS * LEV * 2
CRM_CHUNK = 8
ALPHA = 0.3 * math.log2(math.e)
BETA = 1.5 * ALPHA
SHIFT = math.log2(0.5 * BETA)
MIB = 1 << 20


def pieces(x):
    first = x.astype(jnp.bfloat16)
    rest = x - first.astype(jnp.float32)
    second = rest.astype(jnp.bfloat16)
    third = (rest - second.astype(jnp.float32)).astype(jnp.bfloat16)
    return first, second, third


def select_dot(x, chosen, dims, x_first):
    total = None
    for part in pieces(x):
        pair = (part, chosen) if x_first else (chosen, part)
        term = lax.dot_general(*pair, (dims, ((), ())), preferred_element_type=jnp.float32)
        total = term if total is None else total + term
    return total


def rows_of(ref, y):
    return ref[pl.ds(y, FIELDS * LEV, stride=2), :]


def edge_kernel(gcm_hbm, first, last, gcm, arrival):
    copy = pltpu.make_async_copy(gcm_hbm, gcm, arrival)
    copy.start()
    first[...] = jnp.zeros_like(first)
    last[...] = jnp.zeros_like(last)
    copy.wait()
    rows = jnp.concatenate([rows_of(gcm, 0), rows_of(gcm, 1)], axis=0)
    for part in range(GCM_ROWS // LANES):
        turned = jnp.transpose(rows[part * LANES : (part + 1) * LANES])
        first[part : part + 1, :] = turned[:1]
        last[part : part + 1, :] = turned[LANES - 1 :]


def early_kernel(
    gcm_hbm, crm_hbm, owner_hbm, branch_hbm, diffusion_hbm,
    state, sums, partial, number, routes, rates,
    gcm, crm, owner, branch, diffusion, arrival, crm_arrival,
):
    loads = [
        pltpu.make_async_copy(source, target, arrival.at[n])
        for n, (source, target) in enumerate(
            [(owner_hbm, owner), (branch_hbm, branch), (diffusion_hbm, diffusion), (gcm_hbm, gcm)]
        )
    ]
    crm_loads = [
        pltpu.make_async_copy(
            crm_hbm.at[f, pl.ds(part * CRM_CHUNK, CRM_CHUNK)],
            crm.at[f, pl.ds(part * CRM_CHUNK, CRM_CHUNK)],
            crm_arrival.at[f, part],
        )
        for f in range(2)
        for part in range(LEV // CRM_CHUNK)
    ]
    for copy in loads + crm_loads:
        copy.start()

    for copy in loads[:3]:
        copy.wait()
    device = lax.broadcasted_iota(jnp.int32, (DEVICES, LANES), 0)
    target = jnp.concatenate(
        [(device == owner[y : y + 1, :]).astype(jnp.float32) for y in range(2)], axis=1
    )
    earlier = (
        lax.broadcasted_iota(jnp.int32, (COLS, COLS), 0)
        < lax.broadcasted_iota(jnp.int32, (COLS, COLS), 1)
    ).astype(jnp.bfloat16)
    count = jnp.dot(target.astype(jnp.bfloat16), earlier, preferred_element_type=jnp.float32)
    for slot in range(2):
        here = jnp.where(count < 0.5, 1.0 - slot, 0.0 + slot)
        routes[slot] = (target * here).astype(jnp.bfloat16)
    rates[...] = jnp.where(branch[...] == 1, 0.6, 0.2)
    for f in range(FIELDS):
        spread = jnp.broadcast_to(diffusion[f : f + 1, :], (LANES, LEV))
        number[f * LEV : (f + 1) * LEV, :] = jnp.transpose(spread)

    loads[3].wait()
    lane = lax.broadcasted_iota(jnp.int32, (FIELDS * LEV, LANES), 1)
    own = [rows_of(gcm, 0), rows_of(gcm, 1)]
    for y in range(2):
        before = jnp.where(lane == 0, 0.0, pltpu.roll(own[y], 1, axis=1))
        after = jnp.where(lane == LANES - 1, 0.0, pltpu.roll(own[y], LANES - 1, axis=1))
        around = own[1 - y] + after + before
        partial[y] = own[y] + number[...] * (around - 4.0 * own[y])

    for f, (scale, shift) in enumerate([(ALPHA, SHIFT), (BETA, 0.0)]):
        for part in range(LEV // CRM_CHUNK):
            crm_loads[f * (LEV // CRM_CHUNK) + part].wait()

            def level(n, carry):
                k = part * CRM_CHUNK + n
                for half in range(2):
                    x = crm[f, k, :, half * LANES : (half + 1) * LANES].astype(jnp.float32)
                    x = x * scale + shift
                    total = None
                    for row in range(SUB):
                        block = x[row * INNER : (row + 1) * INNER]
                        state[f, half, pl.ds(k * NXC + row, INNER, stride=SUB), :] = block
                        total = block if total is None else total + block
                    sums[f, half, pl.ds(pl.multiple_of(k * SUB, SUB), SUB), :] = total
                return carry

            lax.fori_loop(0, CRM_CHUNK, level, 0, unroll=4)


def prepare_kernel(partial, number, below, above, left, right, routes, rates, advanced, outgoing):
    lane = lax.broadcasted_iota(jnp.int32, (FIELDS * LEV, LANES), 1)
    level = lax.broadcasted_iota(jnp.int32, (LEV, LANES), 0)

    def columns(ref):
        turned = jnp.transpose(ref[...])
        column = jnp.concatenate([turned[:, n : n + 1] for n in range(GCM_ROWS // LANES)], axis=0)
        return column[: FIELDS * LEV], column[FIELDS * LEV :]

    vertical = [rows_of(above, 1), rows_of(below, 0)]
    west, east = columns(left), columns(right)
    values = []
    for y in range(2):
        side = jnp.where(lane == 0, west[y], jnp.where(lane == LANES - 1, east[y], 0.0))
        state = partial[y] + number[...] * (vertical[y] + side)
        advanced[pl.ds(2 * 2 * LEV + y, 4 * LEV, stride=2), :] = state[2 * LEV :]
        field = [state[f * LEV : (f + 1) * LEV] for f in range(FIELDS)]
        warm = ALPHA * (0.25 * field[0] + 0.2 * field[4])
        wet = BETA * (0.25 * field[1] + 0.2 * field[5])
        drift = 0.45 * jnp.tanh(field[2])
        tilt = jnp.tanh(field[3])
        rise = 0.15 * (tilt + pltpu.roll(tilt, LEV - 1, axis=0))
        rise = jnp.where(level == LEV - 1, rates[y : y + 1, :], rise)
        values.append(jnp.concatenate([warm, wet, drift, rise], axis=0))
    values = jnp.concatenate(values, axis=1)
    for slot in range(2):
        outgoing[pl.ds(slot, DEVICES, stride=2), :] = select_dot(
            values, routes[slot], ((1,), (1,)), False
        )


def cloud_kernel(incoming, start, sums, outgoing, state, coef, mean, total, square):
    level = lax.broadcasted_iota(jnp.int32, (LEV, LANES), 0)
    top = level == LEV - 1
    rates = []

    def up(x):
        return pltpu.roll(x, LEV - 1, axis=0)

    def down(x):
        return pltpu.roll(x, 1, axis=0)

    def folded(ref, *lead):
        out = None
        for part in range(SUB):
            x = ref[(*lead, pl.ds(part, LEV, stride=SUB), slice(None))]
            out = x if out is None else out + x
        return out

    for half in range(2):
        values = jnp.transpose(incoming[half * LANES : (half + 1) * LANES, :])
        rise = values[3 * LEV :]
        rates.append(rise[LEV - 1 :])
        rise = jnp.where(top, 0.0, rise)
        base = SHIFT * (1.0 - rise + down(rise))
        coef[0, half] = values[:LEV] + SHIFT - 0.75 * base
        coef[1, half] = values[LEV : 2 * LEV]
        coef[2, half] = values[2 * LEV : 3 * LEV]
        coef[3, half] = rise
        coef[7, half] = jnp.broadcast_to(rates[half], (LEV, LANES))
        for f in range(2):
            mean[f, half] = folded(sums, f, half) * (1.0 / NXC)

    def relax():
        for half in range(2):
            rise = coef[3, half]
            for f in range(2):
                now = mean[f, half]
                flux = rise * jnp.where(rise > 0.0, now, up(now))
                now = now - flux + down(flux)
                add = coef[f, half] - 0.25 * now
                coef[4 + f, half] = add
                mean[f, half] = now + add
                if f == 0:
                    coef[6, half] = now + add

    def settle():
        for half in range(2):
            rain = folded(total, half) * (1.0 / NXC)
            mean[0, half] = mean[0, half] + rain
            mean[1, half] = mean[1, half] - rain
            mean[2, half] = mean[2, half] + rain

    def sweep(source, half, last):
        rate = jnp.broadcast_to(coef[7, half, 0:1, :], (SUB, LANES))

        def row(index, k):
            return jnp.broadcast_to(coef[index, half, k : k + 1, :], (SUB, LANES))

        def drifted(f, k, size, positive):
            cells = [
                source[f, half, k * NXC + j * SUB : k * NXC + (j + 1) * SUB, :]
                for j in range(INNER)
            ]
            before = [pltpu.roll(cells[-1], 1, axis=0)] + cells[:-1]
            after = cells[1:] + [pltpu.roll(cells[0], SUB - 1, axis=0)]
            return [
                c + size * (jnp.where(positive, b, a) - c)
                for c, b, a in zip(cells, before, after)
            ]

        def level_of(k):
            drift = row(2, k)
            size, positive = jnp.abs(drift), drift > 0.0
            return [drifted(f, k, size, positive) for f in range(2)]

        now = level_of(0)
        below = None
        for k in range(LEV):
            add = [row(4, k), row(5, k)]
            if k < LEV - 1:
                after = level_of(k + 1)
                rise = row(3, k)
                upward = rise > 0.0
                flux = [
                    [rise * jnp.where(upward, a, b) for a, b in zip(now[f], after[f])]
                    for f in range(2)
                ]
            rained = None
            spread = None
            if last:
                middle = row(6, k)
            for j in range(INNER):
                new = []
                for f in range(2):
                    x = now[f][j]
                    if k < LEV - 1:
                        x = x - flux[f][j]
                    if k > 0:
                        x = x + below[f][j]
                    new.append(x + add[f])
                temper, moisture = new
                rain = rate * jnp.maximum(moisture - jnp.exp2(temper), 0.0)
                temper = temper + rain
                rained = rain if rained is None else rained + rain
                if last:
                    away = temper - middle
                    spread = away * away if spread is None else spread + away * away
                else:
                    at = slice(k * NXC + j * SUB, k * NXC + (j + 1) * SUB)
                    state[0, half, at, :] = temper
                    state[1, half, at, :] = moisture - rain
            total[half, k * SUB : (k + 1) * SUB, :] = rained
            if last:
                square[half, k * SUB : (k + 1) * SUB, :] = spread
            if k < LEV - 1:
                below, now = flux, after

    def substep(source, last):
        relax()

        def half_of(half, carry):
            sweep(source, half, last)
            return carry

        lax.fori_loop(0, 2, half_of, 0)
        if not last:
            settle()

    for half in range(2):
        mean[2, half] = jnp.zeros((LEV, LANES), jnp.float32)
    substep(start, False)

    def middle_step(step, carry):
        substep(state, False)
        return carry

    lax.fori_loop(0, SUBSTEPS - 2, middle_step, 0)
    substep(state, True)
    settle()
    for half in range(2):
        warm, wet, rain = mean[0, half], mean[1, half], mean[2, half]
        gap = warm - coef[6, half]
        spread = folded(square, half) * (1.0 / NXC) - gap * gap
        result = [
            (warm - SHIFT) * (1.0 / ALPHA),
            wet * (1.0 / BETA),
            rain * (1.0 / BETA),
            spread * (1.0 / (ALPHA * ALPHA)),
        ]
        outgoing[half * LANES : (half + 1) * LANES, :] = jnp.transpose(
            jnp.concatenate(result, axis=0)
        )


def home_kernel(returned, routes, advanced, gcm_next, stats):
    del advanced
    home = None
    for slot in range(2):
        back = returned[pl.ds(slot, DEVICES, stride=2), :]
        term = select_dot(jnp.transpose(back), routes[slot], ((1,), (0,)), True)
        home = term if home is None else home + term
    for y in range(2):
        part = home[:, y * LANES : (y + 1) * LANES]
        gcm_next[pl.ds(y, 2 * LEV, stride=2), :] = part[: 2 * LEV]
        stats[pl.ds(y, 2 * LEV, stride=2), :] = part[2 * LEV :]


def whole(shape):
    return pl.BlockSpec(shape, lambda *_: (0,) * len(shape))


def f32(*shape):
    return jax.ShapeDtypeStruct(shape, jnp.float32)


def in_hbm(x):
    return pltpu.with_memory_space_constraint(x, pltpu.HBM)


def transfer(rows):
    moved = lax.all_to_all(
        rows.reshape(DEVICES, 2, LANES), ("blk", "sub"), split_axis=0, concat_axis=0, tiled=True
    )
    return moved.reshape(COLS, LANES)


def body(gcm_state, crm_state, owner, branch, diffusion):
    gcm = gcm_state.reshape(GCM_ROWS, LANES)
    n_blk, n_sub = lax.axis_size("blk"), lax.axis_size("sub")

    def ring(n, step):
        return [(i, (i + step) % n) for i in range(n)]

    above = lax.ppermute(gcm, "blk", ring(n_blk, 1))
    below = lax.ppermute(gcm, "blk", ring(n_blk, -1))
    hbm = pl.BlockSpec(memory_space=pltpu.HBM)
    first, last = pl.pallas_call(
        edge_kernel,
        in_specs=[hbm],
        out_shape=(f32(SUB, LANES), f32(SUB, LANES)),
        scratch_shapes=[pltpu.VMEM((GCM_ROWS, LANES), jnp.float32), pltpu.SemaphoreType.DMA(())],
        compiler_params=pltpu.CompilerParams(vmem_limit_bytes=4 * MIB),
        name="edges",
    )(in_hbm(gcm))
    right = lax.ppermute(first, "sub", ring(n_sub, -1))
    left = lax.ppermute(last, "sub", ring(n_sub, 1))
    cells = 2 * LEV * NXC * COLS
    state, sums, partial, number, routes, rates = pl.pallas_call(
        early_kernel,
        in_specs=[hbm] * 5,
        out_shape=(
            f32(2, 2, LEV * NXC, LANES),
            f32(2, 2, LEV * SUB, LANES),
            f32(2, FIELDS * LEV, LANES),
            f32(FIELDS * LEV, LANES),
            jax.ShapeDtypeStruct((2, DEVICES, COLS), jnp.bfloat16),
            f32(2, LANES),
        ),
        scratch_shapes=[
            pltpu.VMEM((GCM_ROWS, LANES), jnp.float32),
            pltpu.VMEM((2, LEV, NXC, COLS), jnp.bfloat16),
            pltpu.VMEM((2, LANES), jnp.int32),
            pltpu.VMEM((2, LANES), jnp.int32),
            pltpu.VMEM((FIELDS, LEV), jnp.float32),
            pltpu.SemaphoreType.DMA((4,)),
            pltpu.SemaphoreType.DMA((2, LEV // CRM_CHUNK)),
        ],
        compiler_params=pltpu.CompilerParams(vmem_limit_bytes=16 * MIB),
        cost_estimate=pl.CostEstimate(flops=4 * cells, bytes_accessed=6 * cells, transcendentals=0),
        name="early",
    )(*map(in_hbm, (gcm, crm_state, owner, branch, diffusion)))
    advanced, outgoing = pl.pallas_call(
        prepare_kernel,
        out_shape=(f32(GCM_ROWS, LANES), f32(COLS, LANES)),
        compiler_params=pltpu.CompilerParams(vmem_limit_bytes=8 * MIB),
        name="prepare",
    )(partial, number, below, above, left, right, routes, rates)

    incoming = transfer(outgoing)
    profiles = pl.pallas_call(
        cloud_kernel,
        out_shape=f32(COLS, LANES),
        scratch_shapes=[
            pltpu.VMEM((2, 2, LEV * NXC, LANES), jnp.float32),
            pltpu.VMEM((8, 2, LEV, LANES), jnp.float32),
            pltpu.VMEM((3, 2, LEV, LANES), jnp.float32),
            pltpu.VMEM((2, LEV * SUB, LANES), jnp.float32),
            pltpu.VMEM((2, LEV * SUB, LANES), jnp.float32),
        ],
        compiler_params=pltpu.CompilerParams(vmem_limit_bytes=12 * MIB),
        name="cloud",
    )(incoming, state, sums)
    returned = transfer(profiles)

    gcm_next, stats = pl.pallas_call(
        home_kernel,
        grid=(1,),
        in_specs=[
            whole((COLS, LANES)),
            whole((2, DEVICES, COLS)),
            pl.BlockSpec(memory_space=pl.ANY),
        ],
        out_specs=(whole((4 * LEV, LANES)), whole((4 * LEV, LANES))),
        out_shape=(f32(GCM_ROWS, LANES), f32(4 * LEV, LANES)),
        input_output_aliases={2: 0},
        compiler_params=pltpu.CompilerParams(vmem_limit_bytes=8 * MIB),
        name="home",
    )(returned, routes, advanced)
    return gcm_next.reshape(gcm_state.shape), stats.reshape(2, LEV, 2, LANES)


def solution(mesh):
    grid = P(None, None, "blk", "sub")
    return jax.shard_map(
        body,
        mesh=mesh,
        in_specs=(grid, P(None, None, None, ("blk", "sub")), P("blk", "sub"), P("blk", "sub"), P()),
        out_specs=(grid, grid),
        check_vma=False,
    )
```

```python
import math

import jax
import jax.numpy as jnp
from jax import lax
from jax.experimental import pallas as pl
from jax.experimental.pallas import tpu as pltpu
from jax.sharding import PartitionSpec as P

SUBSTEPS = 4
LEV = 32
NXC = 64
LANES = 128
DEVICES = 128
COLS = 256
FIELDS = 6
SUB = 8
INNER = NXC // SUB
GCM_ROWS = FIELDS * LEV * 2
CRM_CHUNK = 8
ALPHA = 0.3 * math.log2(math.e)
BETA = 1.5 * ALPHA
SHIFT = math.log2(0.5 * BETA)
MIB = 1 << 20


def pieces(x):
    first = x.astype(jnp.bfloat16)
    rest = x - first.astype(jnp.float32)
    second = rest.astype(jnp.bfloat16)
    third = (rest - second.astype(jnp.float32)).astype(jnp.bfloat16)
    return first, second, third


def select_dot(x, chosen, dims, x_first):
    total = None
    for part in pieces(x):
        pair = (part, chosen) if x_first else (chosen, part)
        term = lax.dot_general(*pair, (dims, ((), ())), preferred_element_type=jnp.float32)
        total = term if total is None else total + term
    return total


def rows_of(ref, y):
    return ref[pl.ds(y, FIELDS * LEV, stride=2), :]


def edge_kernel(
    gcm_hbm, owner_hbm, branch_hbm, diffusion_hbm,
    gcm, to_chip_mate, to_other, routes, rates, number,
    owner, branch, diffusion, arrival,
):
    loads = [
        pltpu.make_async_copy(source, target, arrival.at[n])
        for n, (source, target) in enumerate(
            [(owner_hbm, owner), (branch_hbm, branch), (diffusion_hbm, diffusion), (gcm_hbm, gcm)]
        )
    ]
    for copy in loads:
        copy.start()
    to_chip_mate[...] = jnp.zeros_like(to_chip_mate)
    to_other[...] = jnp.zeros_like(to_other)
    for copy in loads[:3]:
        copy.wait()
    device = lax.broadcasted_iota(jnp.int32, (DEVICES, LANES), 0)
    target = jnp.concatenate(
        [(device == owner[y : y + 1, :]).astype(jnp.float32) for y in range(2)], axis=1
    )
    earlier = (
        lax.broadcasted_iota(jnp.int32, (COLS, COLS), 0)
        < lax.broadcasted_iota(jnp.int32, (COLS, COLS), 1)
    ).astype(jnp.bfloat16)
    count = jnp.dot(target.astype(jnp.bfloat16), earlier, preferred_element_type=jnp.float32)
    for slot in range(2):
        here = jnp.where(count < 0.5, 1.0 - slot, 0.0 + slot)
        routes[slot] = (target * here).astype(jnp.bfloat16)
    rates[...] = jnp.where(branch[...] == 1, 0.6, 0.2)
    for f in range(FIELDS):
        spread = jnp.broadcast_to(diffusion[f : f + 1, :], (LANES, LEV))
        number[f * LEV : (f + 1) * LEV, :] = jnp.transpose(spread)

    loads[3].wait()
    even = lax.rem(lax.axis_index("sub"), 2) == 0
    rows = jnp.concatenate([rows_of(gcm, 0), rows_of(gcm, 1)], axis=0)
    for part in range(GCM_ROWS // LANES):
        turned = jnp.transpose(rows[part * LANES : (part + 1) * LANES])
        first, last = turned[:1], turned[LANES - 1 :]
        to_chip_mate[part : part + 1, :] = jnp.where(even, last, first)
        to_other[part : part + 1, :] = jnp.where(even, first, last)


def early_kernel(crm_hbm, gcm, number, state, sums, partial, crm, arrival):
    loads = [
        pltpu.make_async_copy(
            crm_hbm.at[f, pl.ds(part * CRM_CHUNK, CRM_CHUNK)],
            crm.at[f, pl.ds(part * CRM_CHUNK, CRM_CHUNK)],
            arrival.at[f, part],
        )
        for f in range(2)
        for part in range(LEV // CRM_CHUNK)
    ]
    for copy in loads:
        copy.start()
    lane = lax.broadcasted_iota(jnp.int32, (FIELDS * LEV, LANES), 1)
    own = [rows_of(gcm, 0), rows_of(gcm, 1)]
    for y in range(2):
        before = jnp.where(lane == 0, 0.0, pltpu.roll(own[y], 1, axis=1))
        after = jnp.where(lane == LANES - 1, 0.0, pltpu.roll(own[y], LANES - 1, axis=1))
        around = own[1 - y] + after + before
        partial[y] = own[y] + number[...] * (around - 4.0 * own[y])

    for f, (scale, shift) in enumerate([(ALPHA, SHIFT), (BETA, 0.0)]):
        for part in range(LEV // CRM_CHUNK):
            loads[f * (LEV // CRM_CHUNK) + part].wait()

            def level(n, carry):
                k = part * CRM_CHUNK + n
                for half in range(2):
                    x = crm[f, k, :, half * LANES : (half + 1) * LANES].astype(jnp.float32)
                    x = x * scale + shift
                    total = None
                    for row in range(SUB):
                        block = x[row * INNER : (row + 1) * INNER]
                        state[f, half, pl.ds(k * NXC + row, INNER, stride=SUB), :] = block
                        total = block if total is None else total + block
                    sums[f, half, pl.ds(pl.multiple_of(k * SUB, SUB), SUB), :] = total
                return carry

            lax.fori_loop(0, CRM_CHUNK, level, 0, unroll=4)


def prepare_kernel(
    partial, number, core_mate, neighbour, chip_mate, other, routes, rates, advanced, outgoing
):
    lane = lax.broadcasted_iota(jnp.int32, (FIELDS * LEV, LANES), 1)
    level = lax.broadcasted_iota(jnp.int32, (LEV, LANES), 0)

    def columns(ref):
        turned = jnp.transpose(ref)
        column = jnp.concatenate([turned[:, n : n + 1] for n in range(GCM_ROWS // LANES)], axis=0)
        return column[: FIELDS * LEV], column[FIELDS * LEV :]

    core = lax.rem(lax.axis_index("blk"), 2)
    inside, outside = rows_of(core_mate, core), rows_of(neighbour, 1 - core)
    vertical = [
        jnp.where(core == 0, outside, inside),
        jnp.where(core == 0, inside, outside),
    ]
    even = lax.rem(lax.axis_index("sub"), 2) == 0
    near, far = chip_mate[...], other[...]
    west, east = columns(jnp.where(even, far, near)), columns(jnp.where(even, near, far))
    values = []
    for y in range(2):
        side = jnp.where(lane == 0, west[y], jnp.where(lane == LANES - 1, east[y], 0.0))
        state = partial[y] + number[...] * (vertical[y] + side)
        advanced[pl.ds(y, 4 * LEV, stride=2), :] = state[2 * LEV :]
        field = [state[f * LEV : (f + 1) * LEV] for f in range(FIELDS)]
        warm = ALPHA * (0.25 * field[0] + 0.2 * field[4])
        wet = BETA * (0.25 * field[1] + 0.2 * field[5])
        drift = 0.45 * jnp.tanh(field[2])
        tilt = jnp.tanh(field[3])
        rise = 0.15 * (tilt + pltpu.roll(tilt, LEV - 1, axis=0))
        rise = jnp.where(level == LEV - 1, rates[y : y + 1, :], rise)
        values.append(jnp.concatenate([warm, wet, drift, rise], axis=0))
    values = jnp.concatenate(values, axis=1)
    for slot in range(2):
        outgoing[pl.ds(slot, DEVICES, stride=2), :] = select_dot(
            values, routes[slot], ((1,), (1,)), False
        )


def cloud_kernel(
    incoming, start, sums, advanced, outgoing, gcm_next,
    state, coef, mean, total, square, departure,
):
    leaving = pltpu.make_async_copy(
        advanced, gcm_next.at[pl.ds(2 * 2 * LEV, 4 * 2 * LEV)], departure
    )
    leaving.start()
    level = lax.broadcasted_iota(jnp.int32, (LEV, LANES), 0)
    top = level == LEV - 1
    rates = []

    def up(x):
        return pltpu.roll(x, LEV - 1, axis=0)

    def down(x):
        return pltpu.roll(x, 1, axis=0)

    def folded(ref, *lead):
        out = None
        for part in range(SUB):
            x = ref[(*lead, pl.ds(part, LEV, stride=SUB), slice(None))]
            out = x if out is None else out + x
        return out

    for half in range(2):
        values = jnp.transpose(incoming[half * LANES : (half + 1) * LANES, :])
        rise = values[3 * LEV :]
        rates.append(rise[LEV - 1 :])
        rise = jnp.where(top, 0.0, rise)
        base = SHIFT * (1.0 - rise + down(rise))
        coef[0, half] = values[:LEV] + SHIFT - 0.75 * base
        coef[1, half] = values[LEV : 2 * LEV]
        coef[2, half] = values[2 * LEV : 3 * LEV]
        coef[3, half] = rise
        coef[7, half] = jnp.broadcast_to(rates[half], (LEV, LANES))
        for f in range(2):
            mean[f, half] = folded(sums, f, half) * (1.0 / NXC)

    def relax():
        for half in range(2):
            rise = coef[3, half]
            for f in range(2):
                now = mean[f, half]
                flux = rise * jnp.where(rise > 0.0, now, up(now))
                now = now - flux + down(flux)
                add = coef[f, half] - 0.25 * now
                coef[4 + f, half] = add
                mean[f, half] = now + add
                if f == 0:
                    coef[6, half] = now + add

    def settle():
        for half in range(2):
            rain = folded(total, half) * (1.0 / NXC)
            mean[0, half] = mean[0, half] + rain
            mean[1, half] = mean[1, half] - rain
            mean[2, half] = mean[2, half] + rain

    def sweep(source, half, last):
        rate = jnp.broadcast_to(coef[7, half, 0:1, :], (SUB, LANES))

        def row(index, k):
            return jnp.broadcast_to(coef[index, half, k : k + 1, :], (SUB, LANES))

        def drifted(f, k, size, positive):
            cells = [
                source[f, half, k * NXC + j * SUB : k * NXC + (j + 1) * SUB, :]
                for j in range(INNER)
            ]
            before = [pltpu.roll(cells[-1], 1, axis=0)] + cells[:-1]
            after = cells[1:] + [pltpu.roll(cells[0], SUB - 1, axis=0)]
            return [
                c + size * (jnp.where(positive, b, a) - c)
                for c, b, a in zip(cells, before, after)
            ]

        def level_of(k):
            drift = row(2, k)
            size, positive = jnp.abs(drift), drift > 0.0
            return [drifted(f, k, size, positive) for f in range(2)]

        now = level_of(0)
        below = None
        for k in range(LEV):
            add = [row(4, k), row(5, k)]
            if k < LEV - 1:
                after = level_of(k + 1)
                rise = row(3, k)
                upward = rise > 0.0
                flux = [
                    [rise * jnp.where(upward, a, b) for a, b in zip(now[f], after[f])]
                    for f in range(2)
                ]
            rained = None
            spread = None
            if last:
                middle = row(6, k)
            for j in range(INNER):
                new = []
                for f in range(2):
                    x = now[f][j]
                    if k < LEV - 1:
                        x = x - flux[f][j]
                    if k > 0:
                        x = x + below[f][j]
                    new.append(x + add[f])
                temper, moisture = new
                rain = rate * jnp.maximum(moisture - jnp.exp2(temper), 0.0)
                temper = temper + rain
                rained = rain if rained is None else rained + rain
                if last:
                    away = temper - middle
                    spread = away * away if spread is None else spread + away * away
                else:
                    at = slice(k * NXC + j * SUB, k * NXC + (j + 1) * SUB)
                    state[0, half, at, :] = temper
                    state[1, half, at, :] = moisture - rain
            total[half, k * SUB : (k + 1) * SUB, :] = rained
            if last:
                square[half, k * SUB : (k + 1) * SUB, :] = spread
            if k < LEV - 1:
                below, now = flux, after

    def substep(source, last):
        relax()

        def half_of(half, carry):
            sweep(source, half, last)
            return carry

        lax.fori_loop(0, 2, half_of, 0)
        if not last:
            settle()

    for half in range(2):
        mean[2, half] = jnp.zeros((LEV, LANES), jnp.float32)
    substep(start, False)

    def middle_step(step, carry):
        substep(state, False)
        return carry

    lax.fori_loop(0, SUBSTEPS - 2, middle_step, 0)
    substep(state, True)
    settle()
    for half in range(2):
        warm, wet, rain = mean[0, half], mean[1, half], mean[2, half]
        gap = warm - coef[6, half]
        spread = folded(square, half) * (1.0 / NXC) - gap * gap
        result = [
            (warm - SHIFT) * (1.0 / ALPHA),
            wet * (1.0 / BETA),
            rain * (1.0 / BETA),
            spread * (1.0 / (ALPHA * ALPHA)),
        ]
        outgoing[half * LANES : (half + 1) * LANES, :] = jnp.transpose(
            jnp.concatenate(result, axis=0)
        )
    leaving.wait()


def home_kernel(returned, routes, begun, gcm_next, stats):
    del begun
    home = None
    for slot in range(2):
        back = returned[pl.ds(slot, DEVICES, stride=2), :]
        term = select_dot(jnp.transpose(back), routes[slot], ((1,), (0,)), True)
        home = term if home is None else home + term
    for y in range(2):
        part = home[:, y * LANES : (y + 1) * LANES]
        gcm_next[pl.ds(y, 2 * LEV, stride=2), :] = part[: 2 * LEV]
        stats[pl.ds(y, 2 * LEV, stride=2), :] = part[2 * LEV :]


def whole(shape):
    return pl.BlockSpec(shape, lambda *_: (0,) * len(shape))


def f32(*shape):
    return jax.ShapeDtypeStruct(shape, jnp.float32)


def in_hbm(x):
    return pltpu.with_memory_space_constraint(x, pltpu.HBM)


def transfer(rows):
    moved = lax.all_to_all(
        rows.reshape(DEVICES, 2, LANES), ("blk", "sub"), split_axis=0, concat_axis=0, tiled=True
    )
    return moved.reshape(COLS, LANES)


def body(gcm_state, crm_state, owner, branch, diffusion):
    gcm = gcm_state.reshape(GCM_ROWS, LANES)

    def pairs(n, first):
        ahead = [(i, (i + 1) % n) for i in range(first, n, 2)]
        return ahead + [(j, i) for i, j in ahead]

    n_blk, n_sub = lax.axis_size("blk"), lax.axis_size("sub")
    neighbour = lax.ppermute(gcm, "blk", pairs(n_blk, 1))
    core_mate = lax.ppermute(gcm, "blk", pairs(n_blk, 0))
    hbm = pl.BlockSpec(memory_space=pltpu.HBM)
    gcm_here, to_chip_mate, to_other, routes, rates, number = pl.pallas_call(
        edge_kernel,
        in_specs=[hbm] * 4,
        out_shape=(
            f32(GCM_ROWS, LANES),
            f32(SUB, LANES),
            f32(SUB, LANES),
            jax.ShapeDtypeStruct((2, DEVICES, COLS), jnp.bfloat16),
            f32(2, LANES),
            f32(FIELDS * LEV, LANES),
        ),
        scratch_shapes=[
            pltpu.VMEM((2, LANES), jnp.int32),
            pltpu.VMEM((2, LANES), jnp.int32),
            pltpu.VMEM((FIELDS, LEV), jnp.float32),
            pltpu.SemaphoreType.DMA((4,)),
        ],
        compiler_params=pltpu.CompilerParams(vmem_limit_bytes=4 * MIB),
        name="edges",
    )(*map(in_hbm, (gcm, owner, branch, diffusion)))
    chip_mate = lax.ppermute(to_chip_mate, "sub", pairs(n_sub, 0))
    other = lax.ppermute(to_other, "sub", pairs(n_sub, 1))
    cells = 2 * LEV * NXC * COLS
    state, sums, partial = pl.pallas_call(
        early_kernel,
        in_specs=[hbm, whole((GCM_ROWS, LANES)), whole((FIELDS * LEV, LANES))],
        out_shape=(
            f32(2, 2, LEV * NXC, LANES),
            f32(2, 2, LEV * SUB, LANES),
            f32(2, FIELDS * LEV, LANES),
        ),
        scratch_shapes=[
            pltpu.VMEM((2, LEV, NXC, COLS), jnp.bfloat16),
            pltpu.SemaphoreType.DMA((2, LEV // CRM_CHUNK)),
        ],
        compiler_params=pltpu.CompilerParams(vmem_limit_bytes=16 * MIB),
        cost_estimate=pl.CostEstimate(flops=4 * cells, bytes_accessed=6 * cells, transcendentals=0),
        name="early",
    )(in_hbm(crm_state), gcm_here, number)
    advanced, outgoing = pl.pallas_call(
        prepare_kernel,
        out_shape=(f32(4 * 2 * LEV, LANES), f32(COLS, LANES)),
        compiler_params=pltpu.CompilerParams(vmem_limit_bytes=8 * MIB),
        name="prepare",
    )(partial, number, core_mate, neighbour, chip_mate, other, routes, rates)

    incoming = transfer(outgoing)
    profiles, gcm_next = pl.pallas_call(
        cloud_kernel,
        out_specs=(whole((COLS, LANES)), hbm),
        out_shape=(f32(COLS, LANES), f32(GCM_ROWS, LANES)),
        scratch_shapes=[
            pltpu.VMEM((2, 2, LEV * NXC, LANES), jnp.float32),
            pltpu.VMEM((8, 2, LEV, LANES), jnp.float32),
            pltpu.VMEM((3, 2, LEV, LANES), jnp.float32),
            pltpu.VMEM((2, LEV * SUB, LANES), jnp.float32),
            pltpu.VMEM((2, LEV * SUB, LANES), jnp.float32),
            pltpu.SemaphoreType.DMA(()),
        ],
        compiler_params=pltpu.CompilerParams(vmem_limit_bytes=12 * MIB),
        name="cloud",
    )(incoming, state, sums, advanced)
    returned = transfer(profiles)

    gcm_next, stats = pl.pallas_call(
        home_kernel,
        grid=(1,),
        in_specs=[
            whole((COLS, LANES)),
            whole((2, DEVICES, COLS)),
            pl.BlockSpec(memory_space=pl.ANY),
        ],
        out_specs=(whole((4 * LEV, LANES)), whole((4 * LEV, LANES))),
        out_shape=(f32(GCM_ROWS, LANES), f32(4 * LEV, LANES)),
        input_output_aliases={2: 0},
        compiler_params=pltpu.CompilerParams(vmem_limit_bytes=8 * MIB),
        name="home",
    )(returned, routes, gcm_next)
    return gcm_next.reshape(gcm_state.shape), stats.reshape(2, LEV, 2, LANES)


def solution(mesh):
    grid = P(None, None, "blk", "sub")
    return jax.shard_map(
        body,
        mesh=mesh,
        in_specs=(grid, P(None, None, None, ("blk", "sub")), P("blk", "sub"), P("blk", "sub"), P()),
        out_specs=(grid, grid),
        check_vma=False,
    )
```

```python
import math

import jax
import jax.numpy as jnp
from jax import lax
from jax.experimental import pallas as pl
from jax.experimental.pallas import tpu as pltpu
from jax.sharding import PartitionSpec as P

SUBSTEPS = 4
LEV = 32
NXC = 64
LANES = 128
DEVICES = 128
COLS = 256
FIELDS = 6
SUB = 8
INNER = NXC // SUB
GCM_ROWS = FIELDS * LEV * 2
CRM_CHUNK = 8
PLANE = 8
ALPHA = 0.3 * math.log2(math.e)
BETA = 1.5 * ALPHA
SHIFT = math.log2(0.5 * BETA)
MIB = 1 << 20


def pieces(x):
    first = x.astype(jnp.bfloat16)
    rest = x - first.astype(jnp.float32)
    second = rest.astype(jnp.bfloat16)
    third = (rest - second.astype(jnp.float32)).astype(jnp.bfloat16)
    return first, second, third


def select_dot(x, chosen, dims, x_first):
    total = None
    for part in pieces(x):
        pair = (part, chosen) if x_first else (chosen, part)
        term = lax.dot_general(*pair, (dims, ((), ())), preferred_element_type=jnp.float32)
        total = term if total is None else total + term
    return total


def rows_of(ref, y):
    return ref[pl.ds(y, FIELDS * LEV, stride=2), :]


def cut_kernel(gcm_hbm, row, gcm, arrival):
    @pl.when(lax.rem(lax.axis_index("blk"), PLANE) == 0)
    def _():
        copy = pltpu.make_async_copy(gcm_hbm, gcm, arrival)
        copy.start()
        copy.wait()
        row[: FIELDS * LEV, :] = rows_of(gcm, 0)
        row[FIELDS * LEV :, :] = jnp.zeros((SUB, LANES), jnp.float32)


def edge_kernel(
    cut_first, gcm_hbm, owner_hbm, branch_hbm, diffusion_hbm,
    gcm, to_core_mate, to_chip_mate, to_other, routes, rates, number,
    owner, branch, diffusion, arrival,
):
    del cut_first
    loads = [
        pltpu.make_async_copy(source, target, arrival.at[n])
        for n, (source, target) in enumerate(
            [(owner_hbm, owner), (branch_hbm, branch), (diffusion_hbm, diffusion), (gcm_hbm, gcm)]
        )
    ]
    for copy in loads:
        copy.start()
    to_chip_mate[...] = jnp.zeros_like(to_chip_mate)
    to_other[...] = jnp.zeros_like(to_other)
    for copy in loads[:3]:
        copy.wait()
    device = lax.broadcasted_iota(jnp.int32, (DEVICES, LANES), 0)
    target = jnp.concatenate(
        [(device == owner[y : y + 1, :]).astype(jnp.float32) for y in range(2)], axis=1
    )
    earlier = (
        lax.broadcasted_iota(jnp.int32, (COLS, COLS), 0)
        < lax.broadcasted_iota(jnp.int32, (COLS, COLS), 1)
    ).astype(jnp.bfloat16)
    count = jnp.dot(target.astype(jnp.bfloat16), earlier, preferred_element_type=jnp.float32)
    for slot in range(2):
        here = jnp.where(count < 0.5, 1.0 - slot, 0.0 + slot)
        routes[slot] = (target * here).astype(jnp.bfloat16)
    rates[...] = jnp.where(branch[...] == 1, 0.6, 0.2)
    for f in range(FIELDS):
        spread = jnp.broadcast_to(diffusion[f : f + 1, :], (LANES, LEV))
        number[f * LEV : (f + 1) * LEV, :] = jnp.transpose(spread)

    loads[3].wait()
    to_core_mate[...] = rows_of(gcm, 1 - lax.rem(lax.axis_index("blk"), 2))
    even = lax.rem(lax.axis_index("sub"), 2) == 0
    rows = jnp.concatenate([rows_of(gcm, 0), rows_of(gcm, 1)], axis=0)
    for part in range(GCM_ROWS // LANES):
        turned = jnp.transpose(rows[part * LANES : (part + 1) * LANES])
        first, last = turned[:1], turned[LANES - 1 :]
        to_chip_mate[part : part + 1, :] = jnp.where(even, last, first)
        to_other[part : part + 1, :] = jnp.where(even, first, last)


def early_kernel(crm_hbm, gcm, number, state, sums, partial, crm, arrival):
    loads = [
        pltpu.make_async_copy(
            crm_hbm.at[f, pl.ds(part * CRM_CHUNK, CRM_CHUNK)],
            crm.at[f, pl.ds(part * CRM_CHUNK, CRM_CHUNK)],
            arrival.at[f, part],
        )
        for f in range(2)
        for part in range(LEV // CRM_CHUNK)
    ]
    for copy in loads:
        copy.start()
    lane = lax.broadcasted_iota(jnp.int32, (FIELDS * LEV, LANES), 1)
    own = [rows_of(gcm, 0), rows_of(gcm, 1)]
    for y in range(2):
        before = jnp.where(lane == 0, 0.0, pltpu.roll(own[y], 1, axis=1))
        after = jnp.where(lane == LANES - 1, 0.0, pltpu.roll(own[y], LANES - 1, axis=1))
        around = own[1 - y] + after + before
        partial[y] = own[y] + number[...] * (around - 4.0 * own[y])

    for f, (scale, shift) in enumerate([(ALPHA, SHIFT), (BETA, 0.0)]):
        for part in range(LEV // CRM_CHUNK):
            loads[f * (LEV // CRM_CHUNK) + part].wait()

            def level(n, carry):
                k = part * CRM_CHUNK + n
                for half in range(2):
                    x = crm[f, k, :, half * LANES : (half + 1) * LANES].astype(jnp.float32)
                    x = x * scale + shift
                    total = None
                    for row in range(SUB):
                        block = x[row * INNER : (row + 1) * INNER]
                        state[f, half, pl.ds(k * NXC + row, INNER, stride=SUB), :] = block
                        total = block if total is None else total + block
                    sums[f, half, pl.ds(pl.multiple_of(k * SUB, SUB), SUB), :] = total
                return carry

            lax.fori_loop(0, CRM_CHUNK, level, 0, unroll=4)


def prepare_kernel(
    partial, number, core_mate, other, chip_mate, neighbour, across, routes, rates,
    advanced, outgoing,
):
    lane = lax.broadcasted_iota(jnp.int32, (FIELDS * LEV, LANES), 1)
    level = lax.broadcasted_iota(jnp.int32, (LEV, LANES), 0)

    def columns(ref):
        turned = jnp.transpose(ref)
        column = jnp.concatenate([turned[:, n : n + 1] for n in range(GCM_ROWS // LANES)], axis=0)
        return column[: FIELDS * LEV], column[FIELDS * LEV :]

    core = lax.rem(lax.axis_index("blk"), 2)
    inside = core_mate[...]
    border = lax.rem(lax.axis_index("blk"), PLANE) == PLANE - 1
    outside = jnp.where(border, across[: FIELDS * LEV, :], rows_of(neighbour, 1 - core))
    vertical = [
        jnp.where(core == 0, outside, inside),
        jnp.where(core == 0, inside, outside),
    ]
    even = lax.rem(lax.axis_index("sub"), 2) == 0
    near, far = chip_mate[...], other[...]
    west, east = columns(jnp.where(even, far, near)), columns(jnp.where(even, near, far))
    values = []
    for y in range(2):
        side = jnp.where(lane == 0, west[y], jnp.where(lane == LANES - 1, east[y], 0.0))
        state = partial[y] + number[...] * (vertical[y] + side)
        advanced[pl.ds(y, 4 * LEV, stride=2), :] = state[2 * LEV :]
        field = [state[f * LEV : (f + 1) * LEV] for f in range(FIELDS)]
        warm = ALPHA * (0.25 * field[0] + 0.2 * field[4])
        wet = BETA * (0.25 * field[1] + 0.2 * field[5])
        drift = 0.45 * jnp.tanh(field[2])
        tilt = jnp.tanh(field[3])
        rise = 0.15 * (tilt + pltpu.roll(tilt, LEV - 1, axis=0))
        rise = jnp.where(level == LEV - 1, rates[y : y + 1, :], rise)
        values.append(jnp.concatenate([warm, wet, drift, rise], axis=0))
    values = jnp.concatenate(values, axis=1)
    for slot in range(2):
        outgoing[pl.ds(slot, DEVICES, stride=2), :] = select_dot(
            values, routes[slot], ((1,), (1,)), False
        )


def cloud_kernel(
    incoming, start, sums, advanced, outgoing, gcm_next,
    state, coef, mean, total, square, departure,
):
    leaving = pltpu.make_async_copy(
        advanced, gcm_next.at[pl.ds(2 * 2 * LEV, 4 * 2 * LEV)], departure
    )
    leaving.start()
    level = lax.broadcasted_iota(jnp.int32, (LEV, LANES), 0)
    top = level == LEV - 1
    rates = []

    def up(x):
        return pltpu.roll(x, LEV - 1, axis=0)

    def down(x):
        return pltpu.roll(x, 1, axis=0)

    def folded(ref, *lead):
        out = None
        for part in range(SUB):
            x = ref[(*lead, pl.ds(part, LEV, stride=SUB), slice(None))]
            out = x if out is None else out + x
        return out

    for half in range(2):
        values = jnp.transpose(incoming[half * LANES : (half + 1) * LANES, :])
        rise = values[3 * LEV :]
        rates.append(rise[LEV - 1 :])
        rise = jnp.where(top, 0.0, rise)
        base = SHIFT * (1.0 - rise + down(rise))
        coef[0, half] = values[:LEV] + SHIFT - 0.75 * base
        coef[1, half] = values[LEV : 2 * LEV]
        coef[2, half] = values[2 * LEV : 3 * LEV]
        coef[3, half] = rise
        coef[7, half] = jnp.broadcast_to(rates[half], (LEV, LANES))
        for f in range(2):
            mean[f, half] = folded(sums, f, half) * (1.0 / NXC)

    def relax():
        for half in range(2):
            rise = coef[3, half]
            for f in range(2):
                now = mean[f, half]
                flux = rise * jnp.where(rise > 0.0, now, up(now))
                now = now - flux + down(flux)
                add = coef[f, half] - 0.25 * now
                coef[4 + f, half] = add
                mean[f, half] = now + add
                if f == 0:
                    coef[6, half] = now + add

    def settle():
        for half in range(2):
            rain = folded(total, half) * (1.0 / NXC)
            mean[0, half] = mean[0, half] + rain
            mean[1, half] = mean[1, half] - rain
            mean[2, half] = mean[2, half] + rain

    def sweep(source, half, last):
        rate = jnp.broadcast_to(coef[7, half, 0:1, :], (SUB, LANES))

        def row(index, k):
            return jnp.broadcast_to(coef[index, half, k : k + 1, :], (SUB, LANES))

        def drifted(f, k, size, positive):
            cells = [
                source[f, half, k * NXC + j * SUB : k * NXC + (j + 1) * SUB, :]
                for j in range(INNER)
            ]
            before = [pltpu.roll(cells[-1], 1, axis=0)] + cells[:-1]
            after = cells[1:] + [pltpu.roll(cells[0], SUB - 1, axis=0)]
            return [
                c + size * (jnp.where(positive, b, a) - c)
                for c, b, a in zip(cells, before, after)
            ]

        def level_of(k):
            drift = row(2, k)
            size, positive = jnp.abs(drift), drift > 0.0
            return [drifted(f, k, size, positive) for f in range(2)]

        now = level_of(0)
        below = None
        for k in range(LEV):
            add = [row(4, k), row(5, k)]
            if k < LEV - 1:
                after = level_of(k + 1)
                rise = row(3, k)
                upward = rise > 0.0
                flux = [
                    [rise * jnp.where(upward, a, b) for a, b in zip(now[f], after[f])]
                    for f in range(2)
                ]
            rained = None
            spread = None
            if last:
                middle = row(6, k)
            for j in range(INNER):
                new = []
                for f in range(2):
                    x = now[f][j]
                    if k < LEV - 1:
                        x = x - flux[f][j]
                    if k > 0:
                        x = x + below[f][j]
                    new.append(x + add[f])
                temper, moisture = new
                rain = rate * jnp.maximum(moisture - jnp.exp2(temper), 0.0)
                temper = temper + rain
                rained = rain if rained is None else rained + rain
                if last:
                    away = temper - middle
                    spread = away * away if spread is None else spread + away * away
                else:
                    at = slice(k * NXC + j * SUB, k * NXC + (j + 1) * SUB)
                    state[0, half, at, :] = temper
                    state[1, half, at, :] = moisture - rain
            total[half, k * SUB : (k + 1) * SUB, :] = rained
            if last:
                square[half, k * SUB : (k + 1) * SUB, :] = spread
            if k < LEV - 1:
                below, now = flux, after

    def substep(source, last):
        relax()

        def half_of(half, carry):
            sweep(source, half, last)
            return carry

        lax.fori_loop(0, 2, half_of, 0)
        if not last:
            settle()

    for half in range(2):
        mean[2, half] = jnp.zeros((LEV, LANES), jnp.float32)
    substep(start, False)

    def middle_step(step, carry):
        substep(state, False)
        return carry

    lax.fori_loop(0, SUBSTEPS - 2, middle_step, 0)
    substep(state, True)
    settle()
    for half in range(2):
        warm, wet, rain = mean[0, half], mean[1, half], mean[2, half]
        gap = warm - coef[6, half]
        spread = folded(square, half) * (1.0 / NXC) - gap * gap
        result = [
            (warm - SHIFT) * (1.0 / ALPHA),
            wet * (1.0 / BETA),
            rain * (1.0 / BETA),
            spread * (1.0 / (ALPHA * ALPHA)),
        ]
        outgoing[half * LANES : (half + 1) * LANES, :] = jnp.transpose(
            jnp.concatenate(result, axis=0)
        )
    leaving.wait()


def home_kernel(returned, routes, begun, gcm_next, stats):
    del begun
    home = None
    for slot in range(2):
        back = returned[pl.ds(slot, DEVICES, stride=2), :]
        term = select_dot(jnp.transpose(back), routes[slot], ((1,), (0,)), True)
        home = term if home is None else home + term
    for y in range(2):
        part = home[:, y * LANES : (y + 1) * LANES]
        gcm_next[pl.ds(y, 2 * LEV, stride=2), :] = part[: 2 * LEV]
        stats[pl.ds(y, 2 * LEV, stride=2), :] = part[2 * LEV :]


def whole(shape):
    return pl.BlockSpec(shape, lambda *_: (0,) * len(shape))


def f32(*shape):
    return jax.ShapeDtypeStruct(shape, jnp.float32)


def in_hbm(x):
    return pltpu.with_memory_space_constraint(x, pltpu.HBM)


def transfer(rows):
    moved = lax.all_to_all(
        rows.reshape(DEVICES, 2, LANES), ("blk", "sub"), split_axis=0, concat_axis=0, tiled=True
    )
    return moved.reshape(COLS, LANES)


def body(gcm_state, crm_state, owner, branch, diffusion):
    gcm = gcm_state.reshape(GCM_ROWS, LANES)

    def pairs(n, first):
        ahead = [(i, (i + 1) % n) for i in range(first, n, 2)]
        return ahead + [(j, i) for i, j in ahead]

    n_blk, n_sub = lax.axis_size("blk"), lax.axis_size("sub")
    hbm = pl.BlockSpec(memory_space=pltpu.HBM)
    row = pl.pallas_call(
        cut_kernel,
        in_specs=[hbm],
        out_shape=f32(FIELDS * LEV + SUB, LANES),
        scratch_shapes=[pltpu.VMEM((GCM_ROWS, LANES), jnp.float32), pltpu.SemaphoreType.DMA(())],
        compiler_params=pltpu.CompilerParams(vmem_limit_bytes=4 * MIB),
        name="cut",
    )(in_hbm(gcm))
    down = [(i, (i - 1) % n_blk) for i in range(0, n_blk, PLANE)]
    across = lax.ppermute(row, "blk", down)
    near = [pair for pair in pairs(n_blk, 1) if pair not in down]
    neighbour = lax.ppermute(gcm, "blk", near)
    gcm_here, to_core_mate, to_chip_mate, to_other, routes, rates, number = pl.pallas_call(
        edge_kernel,
        in_specs=[pl.BlockSpec(memory_space=pl.ANY)] + [hbm] * 4,
        out_shape=(
            f32(GCM_ROWS, LANES),
            f32(FIELDS * LEV, LANES),
            f32(SUB, LANES),
            f32(SUB, LANES),
            jax.ShapeDtypeStruct((2, DEVICES, COLS), jnp.bfloat16),
            f32(2, LANES),
            f32(FIELDS * LEV, LANES),
        ),
        scratch_shapes=[
            pltpu.VMEM((2, LANES), jnp.int32),
            pltpu.VMEM((2, LANES), jnp.int32),
            pltpu.VMEM((FIELDS, LEV), jnp.float32),
            pltpu.SemaphoreType.DMA((4,)),
        ],
        compiler_params=pltpu.CompilerParams(vmem_limit_bytes=4 * MIB),
        name="edges",
    )(row, *map(in_hbm, (gcm, owner, branch, diffusion)))
    chip_mate = lax.ppermute(to_chip_mate, "sub", pairs(n_sub, 0))
    other = lax.ppermute(to_other, "sub", pairs(n_sub, 1))
    core_mate = lax.ppermute(to_core_mate, "blk", pairs(n_blk, 0))
    cells = 2 * LEV * NXC * COLS
    state, sums, partial = pl.pallas_call(
        early_kernel,
        in_specs=[hbm, whole((GCM_ROWS, LANES)), whole((FIELDS * LEV, LANES))],
        out_shape=(
            f32(2, 2, LEV * NXC, LANES),
            f32(2, 2, LEV * SUB, LANES),
            f32(2, FIELDS * LEV, LANES),
        ),
        scratch_shapes=[
            pltpu.VMEM((2, LEV, NXC, COLS), jnp.bfloat16),
            pltpu.SemaphoreType.DMA((2, LEV // CRM_CHUNK)),
        ],
        compiler_params=pltpu.CompilerParams(vmem_limit_bytes=16 * MIB),
        cost_estimate=pl.CostEstimate(flops=4 * cells, bytes_accessed=6 * cells, transcendentals=0),
        name="early",
    )(in_hbm(crm_state), gcm_here, number)
    advanced, outgoing = pl.pallas_call(
        prepare_kernel,
        out_shape=(f32(4 * 2 * LEV, LANES), f32(COLS, LANES)),
        compiler_params=pltpu.CompilerParams(vmem_limit_bytes=8 * MIB),
        name="prepare",
    )(partial, number, core_mate, other, chip_mate, neighbour, across, routes, rates)

    incoming = transfer(outgoing)
    profiles, gcm_next = pl.pallas_call(
        cloud_kernel,
        out_specs=(whole((COLS, LANES)), hbm),
        out_shape=(f32(COLS, LANES), f32(GCM_ROWS, LANES)),
        scratch_shapes=[
            pltpu.VMEM((2, 2, LEV * NXC, LANES), jnp.float32),
            pltpu.VMEM((8, 2, LEV, LANES), jnp.float32),
            pltpu.VMEM((3, 2, LEV, LANES), jnp.float32),
            pltpu.VMEM((2, LEV * SUB, LANES), jnp.float32),
            pltpu.VMEM((2, LEV * SUB, LANES), jnp.float32),
            pltpu.SemaphoreType.DMA(()),
        ],
        compiler_params=pltpu.CompilerParams(vmem_limit_bytes=12 * MIB),
        name="cloud",
    )(incoming, state, sums, advanced)
    returned = transfer(profiles)

    gcm_next, stats = pl.pallas_call(
        home_kernel,
        grid=(1,),
        in_specs=[
            whole((COLS, LANES)),
            whole((2, DEVICES, COLS)),
            pl.BlockSpec(memory_space=pl.ANY),
        ],
        out_specs=(whole((4 * LEV, LANES)), whole((4 * LEV, LANES))),
        out_shape=(f32(GCM_ROWS, LANES), f32(4 * LEV, LANES)),
        input_output_aliases={2: 0},
        compiler_params=pltpu.CompilerParams(vmem_limit_bytes=8 * MIB),
        name="home",
    )(returned, routes, gcm_next)
    return gcm_next.reshape(gcm_state.shape), stats.reshape(2, LEV, 2, LANES)


def solution(mesh):
    grid = P(None, None, "blk", "sub")
    return jax.shard_map(
        body,
        mesh=mesh,
        in_specs=(grid, P(None, None, None, ("blk", "sub")), P("blk", "sub"), P("blk", "sub"), P()),
        out_specs=(grid, grid),
        check_vma=False,
    )
```

```python
import math

import jax
import jax.numpy as jnp
from jax import lax
from jax.experimental import pallas as pl
from jax.experimental.pallas import tpu as pltpu
from jax.sharding import PartitionSpec as P

SUBSTEPS = 4
LEV = 32
NXC = 64
LANES = 128
DEVICES = 128
COLS = 256
FIELDS = 6
SUB = 8
INNER = NXC // SUB
GCM_ROWS = FIELDS * LEV * 2
CRM_CHUNK = 8
ALPHA = 0.3 * math.log2(math.e)
BETA = 1.5 * ALPHA
SHIFT = math.log2(0.5 * BETA)
MIB = 1 << 20


def pieces(x):
    first = x.astype(jnp.bfloat16)
    rest = x - first.astype(jnp.float32)
    second = rest.astype(jnp.bfloat16)
    third = (rest - second.astype(jnp.float32)).astype(jnp.bfloat16)
    return first, second, third


def select_dot(x, chosen, dims, x_first):
    total = None
    for part in pieces(x):
        pair = (part, chosen) if x_first else (chosen, part)
        term = lax.dot_general(*pair, (dims, ((), ())), preferred_element_type=jnp.float32)
        total = term if total is None else total + term
    return total


def rows_of(ref, y):
    return ref[pl.ds(y, FIELDS * LEV, stride=2), :]


def edge_kernel(
    gcm_hbm, owner_hbm, branch_hbm, diffusion_hbm,
    gcm, to_core_mate, to_neighbour, to_chip_mate, to_other, routes, rates, number,
    owner, branch, diffusion, arrival,
):
    loads = [
        pltpu.make_async_copy(source, target, arrival.at[n])
        for n, (source, target) in enumerate(
            [(owner_hbm, owner), (branch_hbm, branch), (diffusion_hbm, diffusion), (gcm_hbm, gcm)]
        )
    ]
    for copy in loads:
        copy.start()
    to_chip_mate[...] = jnp.zeros_like(to_chip_mate)
    to_other[...] = jnp.zeros_like(to_other)
    for copy in loads[:3]:
        copy.wait()
    device = lax.broadcasted_iota(jnp.int32, (DEVICES, LANES), 0)
    target = jnp.concatenate(
        [(device == owner[y : y + 1, :]).astype(jnp.float32) for y in range(2)], axis=1
    )
    earlier = (
        lax.broadcasted_iota(jnp.int32, (COLS, COLS), 0)
        < lax.broadcasted_iota(jnp.int32, (COLS, COLS), 1)
    ).astype(jnp.bfloat16)
    count = jnp.dot(target.astype(jnp.bfloat16), earlier, preferred_element_type=jnp.float32)
    for slot in range(2):
        here = jnp.where(count < 0.5, 1.0 - slot, 0.0 + slot)
        routes[slot] = (target * here).astype(jnp.bfloat16)
    rates[...] = jnp.where(branch[...] == 1, 0.6, 0.2)
    for f in range(FIELDS):
        spread = jnp.broadcast_to(diffusion[f : f + 1, :], (LANES, LEV))
        number[f * LEV : (f + 1) * LEV, :] = jnp.transpose(spread)

    loads[3].wait()
    core = lax.rem(lax.axis_index("blk"), 2)
    to_core_mate[...] = rows_of(gcm, 1 - core)
    to_neighbour[...] = rows_of(gcm, core)
    even = lax.rem(lax.axis_index("sub"), 2) == 0
    rows = jnp.concatenate([rows_of(gcm, 0), rows_of(gcm, 1)], axis=0)
    for part in range(GCM_ROWS // LANES):
        turned = jnp.transpose(rows[part * LANES : (part + 1) * LANES])
        first, last = turned[:1], turned[LANES - 1 :]
        to_chip_mate[part : part + 1, :] = jnp.where(even, last, first)
        to_other[part : part + 1, :] = jnp.where(even, first, last)


def early_kernel(crm_hbm, gcm, number, state, sums, partial, crm, arrival):
    loads = [
        pltpu.make_async_copy(
            crm_hbm.at[f, pl.ds(part * CRM_CHUNK, CRM_CHUNK)],
            crm.at[f, pl.ds(part * CRM_CHUNK, CRM_CHUNK)],
            arrival.at[f, part],
        )
        for f in range(2)
        for part in range(LEV // CRM_CHUNK)
    ]
    for copy in loads:
        copy.start()
    lane = lax.broadcasted_iota(jnp.int32, (FIELDS * LEV, LANES), 1)
    own = [rows_of(gcm, 0), rows_of(gcm, 1)]
    for y in range(2):
        before = jnp.where(lane == 0, 0.0, pltpu.roll(own[y], 1, axis=1))
        after = jnp.where(lane == LANES - 1, 0.0, pltpu.roll(own[y], LANES - 1, axis=1))
        around = own[1 - y] + after + before
        partial[y] = own[y] + number[...] * (around - 4.0 * own[y])

    for f, (scale, shift) in enumerate([(ALPHA, SHIFT), (BETA, 0.0)]):
        for part in range(LEV // CRM_CHUNK):
            loads[f * (LEV // CRM_CHUNK) + part].wait()

            def level(n, carry):
                k = part * CRM_CHUNK + n
                for half in range(2):
                    x = crm[f, k, :, half * LANES : (half + 1) * LANES].astype(jnp.float32)
                    x = x * scale + shift
                    total = None
                    for row in range(SUB):
                        block = x[row * INNER : (row + 1) * INNER]
                        state[f, half, pl.ds(k * NXC + row, INNER, stride=SUB), :] = block
                        total = block if total is None else total + block
                    sums[f, half, pl.ds(pl.multiple_of(k * SUB, SUB), SUB), :] = total
                return carry

            lax.fori_loop(0, CRM_CHUNK, level, 0, unroll=4)


def prepare_kernel(
    partial, number, neighbour, core_mate, other, chip_mate, routes, rates, advanced, outgoing
):
    lane = lax.broadcasted_iota(jnp.int32, (FIELDS * LEV, LANES), 1)
    level = lax.broadcasted_iota(jnp.int32, (LEV, LANES), 0)

    def columns(ref):
        turned = jnp.transpose(ref)
        column = jnp.concatenate([turned[:, n : n + 1] for n in range(GCM_ROWS // LANES)], axis=0)
        return column[: FIELDS * LEV], column[FIELDS * LEV :]

    core = lax.rem(lax.axis_index("blk"), 2)
    inside, outside = core_mate[...], neighbour[...]
    vertical = [
        jnp.where(core == 0, outside, inside),
        jnp.where(core == 0, inside, outside),
    ]
    even = lax.rem(lax.axis_index("sub"), 2) == 0
    near, far = chip_mate[...], other[...]
    west, east = columns(jnp.where(even, far, near)), columns(jnp.where(even, near, far))
    values = []
    for y in range(2):
        side = jnp.where(lane == 0, west[y], jnp.where(lane == LANES - 1, east[y], 0.0))
        state = partial[y] + number[...] * (vertical[y] + side)
        advanced[pl.ds(y, 4 * LEV, stride=2), :] = state[2 * LEV :]
        field = [state[f * LEV : (f + 1) * LEV] for f in range(FIELDS)]
        warm = ALPHA * (0.25 * field[0] + 0.2 * field[4])
        wet = BETA * (0.25 * field[1] + 0.2 * field[5])
        drift = 0.45 * jnp.tanh(field[2])
        tilt = jnp.tanh(field[3])
        rise = 0.15 * (tilt + pltpu.roll(tilt, LEV - 1, axis=0))
        rise = jnp.where(level == LEV - 1, rates[y : y + 1, :], rise)
        values.append(jnp.concatenate([warm, wet, drift, rise], axis=0))
    values = jnp.concatenate(values, axis=1)
    for slot in range(2):
        outgoing[pl.ds(slot, DEVICES, stride=2), :] = select_dot(
            values, routes[slot], ((1,), (1,)), False
        )


def cloud_kernel(
    incoming, start, sums, advanced, outgoing, gcm_next,
    state, coef, mean, total, square, departure,
):
    leaving = pltpu.make_async_copy(
        advanced, gcm_next.at[pl.ds(2 * 2 * LEV, 4 * 2 * LEV)], departure
    )
    leaving.start()
    level = lax.broadcasted_iota(jnp.int32, (LEV, LANES), 0)
    top = level == LEV - 1
    rates = []

    def up(x):
        return pltpu.roll(x, LEV - 1, axis=0)

    def down(x):
        return pltpu.roll(x, 1, axis=0)

    def folded(ref, *lead):
        out = None
        for part in range(SUB):
            x = ref[(*lead, pl.ds(part, LEV, stride=SUB), slice(None))]
            out = x if out is None else out + x
        return out

    for half in range(2):
        values = jnp.transpose(incoming[half * LANES : (half + 1) * LANES, :])
        rise = values[3 * LEV :]
        rates.append(rise[LEV - 1 :])
        rise = jnp.where(top, 0.0, rise)
        base = SHIFT * (1.0 - rise + down(rise))
        coef[0, half] = values[:LEV] + SHIFT - 0.75 * base
        coef[1, half] = values[LEV : 2 * LEV]
        coef[2, half] = values[2 * LEV : 3 * LEV]
        coef[3, half] = rise
        coef[7, half] = jnp.broadcast_to(rates[half], (LEV, LANES))
        for f in range(2):
            mean[f, half] = folded(sums, f, half) * (1.0 / NXC)

    def relax():
        for half in range(2):
            rise = coef[3, half]
            for f in range(2):
                now = mean[f, half]
                flux = rise * jnp.where(rise > 0.0, now, up(now))
                now = now - flux + down(flux)
                add = coef[f, half] - 0.25 * now
                coef[4 + f, half] = add
                mean[f, half] = now + add
                if f == 0:
                    coef[6, half] = now + add

    def settle():
        for half in range(2):
            rain = folded(total, half) * (1.0 / NXC)
            mean[0, half] = mean[0, half] + rain
            mean[1, half] = mean[1, half] - rain
            mean[2, half] = mean[2, half] + rain

    def sweep(source, half, last):
        rate = jnp.broadcast_to(coef[7, half, 0:1, :], (SUB, LANES))

        def row(index, k):
            return jnp.broadcast_to(coef[index, half, k : k + 1, :], (SUB, LANES))

        def drifted(f, k, size, positive):
            cells = [
                source[f, half, k * NXC + j * SUB : k * NXC + (j + 1) * SUB, :]
                for j in range(INNER)
            ]
            before = [pltpu.roll(cells[-1], 1, axis=0)] + cells[:-1]
            after = cells[1:] + [pltpu.roll(cells[0], SUB - 1, axis=0)]
            return [
                c + size * (jnp.where(positive, b, a) - c)
                for c, b, a in zip(cells, before, after)
            ]

        def level_of(k):
            drift = row(2, k)
            size, positive = jnp.abs(drift), drift > 0.0
            return [drifted(f, k, size, positive) for f in range(2)]

        now = level_of(0)
        below = None
        for k in range(LEV):
            add = [row(4, k), row(5, k)]
            if k < LEV - 1:
                after = level_of(k + 1)
                rise = row(3, k)
                upward = rise > 0.0
                flux = [
                    [rise * jnp.where(upward, a, b) for a, b in zip(now[f], after[f])]
                    for f in range(2)
                ]
            rained = None
            spread = None
            if last:
                middle = row(6, k)
            for j in range(INNER):
                new = []
                for f in range(2):
                    x = now[f][j]
                    if k < LEV - 1:
                        x = x - flux[f][j]
                    if k > 0:
                        x = x + below[f][j]
                    new.append(x + add[f])
                temper, moisture = new
                rain = rate * jnp.maximum(moisture - jnp.exp2(temper), 0.0)
                temper = temper + rain
                rained = rain if rained is None else rained + rain
                if last:
                    away = temper - middle
                    spread = away * away if spread is None else spread + away * away
                else:
                    at = slice(k * NXC + j * SUB, k * NXC + (j + 1) * SUB)
                    state[0, half, at, :] = temper
                    state[1, half, at, :] = moisture - rain
            total[half, k * SUB : (k + 1) * SUB, :] = rained
            if last:
                square[half, k * SUB : (k + 1) * SUB, :] = spread
            if k < LEV - 1:
                below, now = flux, after

    def substep(source, last):
        relax()

        def half_of(half, carry):
            sweep(source, half, last)
            return carry

        lax.fori_loop(0, 2, half_of, 0)
        if not last:
            settle()

    for half in range(2):
        mean[2, half] = jnp.zeros((LEV, LANES), jnp.float32)
    substep(start, False)

    def middle_step(step, carry):
        substep(state, False)
        return carry

    lax.fori_loop(0, SUBSTEPS - 2, middle_step, 0)
    substep(state, True)
    settle()
    for half in range(2):
        warm, wet, rain = mean[0, half], mean[1, half], mean[2, half]
        gap = warm - coef[6, half]
        spread = folded(square, half) * (1.0 / NXC) - gap * gap
        result = [
            (warm - SHIFT) * (1.0 / ALPHA),
            wet * (1.0 / BETA),
            rain * (1.0 / BETA),
            spread * (1.0 / (ALPHA * ALPHA)),
        ]
        outgoing[half * LANES : (half + 1) * LANES, :] = jnp.transpose(
            jnp.concatenate(result, axis=0)
        )
    leaving.wait()


def home_kernel(returned, routes, begun, gcm_next, stats):
    del begun
    home = None
    for slot in range(2):
        back = returned[pl.ds(slot, DEVICES, stride=2), :]
        term = select_dot(jnp.transpose(back), routes[slot], ((1,), (0,)), True)
        home = term if home is None else home + term
    for y in range(2):
        part = home[:, y * LANES : (y + 1) * LANES]
        gcm_next[pl.ds(y, 2 * LEV, stride=2), :] = part[: 2 * LEV]
        stats[pl.ds(y, 2 * LEV, stride=2), :] = part[2 * LEV :]


def whole(shape):
    return pl.BlockSpec(shape, lambda *_: (0,) * len(shape))


def f32(*shape):
    return jax.ShapeDtypeStruct(shape, jnp.float32)


def in_hbm(x):
    return pltpu.with_memory_space_constraint(x, pltpu.HBM)


def transfer(rows):
    moved = lax.all_to_all(
        rows.reshape(DEVICES, 2, LANES), ("blk", "sub"), split_axis=0, concat_axis=0, tiled=True
    )
    return moved.reshape(COLS, LANES)


def body(gcm_state, crm_state, owner, branch, diffusion):
    gcm = gcm_state.reshape(GCM_ROWS, LANES)

    def pairs(n, first):
        ahead = [(i, (i + 1) % n) for i in range(first, n, 2)]
        return ahead + [(j, i) for i, j in ahead]

    n_blk, n_sub = lax.axis_size("blk"), lax.axis_size("sub")
    hbm = pl.BlockSpec(memory_space=pltpu.HBM)
    gcm_here, to_core_mate, to_neighbour, to_chip_mate, to_other, routes, rates, number = pl.pallas_call(
        edge_kernel,
        in_specs=[hbm] * 4,
        out_shape=(
            f32(GCM_ROWS, LANES),
            f32(FIELDS * LEV, LANES),
            f32(FIELDS * LEV, LANES),
            f32(SUB, LANES),
            f32(SUB, LANES),
            jax.ShapeDtypeStruct((2, DEVICES, COLS), jnp.bfloat16),
            f32(2, LANES),
            f32(FIELDS * LEV, LANES),
        ),
        scratch_shapes=[
            pltpu.VMEM((2, LANES), jnp.int32),
            pltpu.VMEM((2, LANES), jnp.int32),
            pltpu.VMEM((FIELDS, LEV), jnp.float32),
            pltpu.SemaphoreType.DMA((4,)),
        ],
        compiler_params=pltpu.CompilerParams(vmem_limit_bytes=4 * MIB),
        name="edges",
    )(*map(in_hbm, (gcm, owner, branch, diffusion)))
    neighbour = lax.ppermute(to_neighbour, "blk", pairs(n_blk, 1))
    core_mate = lax.ppermute(to_core_mate, "blk", pairs(n_blk, 0))
    chip_mate = lax.ppermute(to_chip_mate, "sub", pairs(n_sub, 0))
    other = lax.ppermute(to_other, "sub", pairs(n_sub, 1))
    cells = 2 * LEV * NXC * COLS
    state, sums, partial = pl.pallas_call(
        early_kernel,
        in_specs=[hbm, whole((GCM_ROWS, LANES)), whole((FIELDS * LEV, LANES))],
        out_shape=(
            f32(2, 2, LEV * NXC, LANES),
            f32(2, 2, LEV * SUB, LANES),
            f32(2, FIELDS * LEV, LANES),
        ),
        scratch_shapes=[
            pltpu.VMEM((2, LEV, NXC, COLS), jnp.bfloat16),
            pltpu.SemaphoreType.DMA((2, LEV // CRM_CHUNK)),
        ],
        compiler_params=pltpu.CompilerParams(vmem_limit_bytes=16 * MIB),
        cost_estimate=pl.CostEstimate(flops=4 * cells, bytes_accessed=6 * cells, transcendentals=0),
        name="early",
    )(in_hbm(crm_state), gcm_here, number)
    advanced, outgoing = pl.pallas_call(
        prepare_kernel,
        out_shape=(f32(4 * 2 * LEV, LANES), f32(COLS, LANES)),
        compiler_params=pltpu.CompilerParams(vmem_limit_bytes=8 * MIB),
        name="prepare",
    )(partial, number, neighbour, core_mate, other, chip_mate, routes, rates)

    incoming = transfer(outgoing)
    profiles, gcm_next = pl.pallas_call(
        cloud_kernel,
        out_specs=(whole((COLS, LANES)), hbm),
        out_shape=(f32(COLS, LANES), f32(GCM_ROWS, LANES)),
        scratch_shapes=[
            pltpu.VMEM((2, 2, LEV * NXC, LANES), jnp.float32),
            pltpu.VMEM((8, 2, LEV, LANES), jnp.float32),
            pltpu.VMEM((3, 2, LEV, LANES), jnp.float32),
            pltpu.VMEM((2, LEV * SUB, LANES), jnp.float32),
            pltpu.VMEM((2, LEV * SUB, LANES), jnp.float32),
            pltpu.SemaphoreType.DMA(()),
        ],
        compiler_params=pltpu.CompilerParams(vmem_limit_bytes=12 * MIB),
        name="cloud",
    )(incoming, state, sums, advanced)
    returned = transfer(profiles)

    gcm_next, stats = pl.pallas_call(
        home_kernel,
        grid=(1,),
        in_specs=[
            whole((COLS, LANES)),
            whole((2, DEVICES, COLS)),
            pl.BlockSpec(memory_space=pl.ANY),
        ],
        out_specs=(whole((4 * LEV, LANES)), whole((4 * LEV, LANES))),
        out_shape=(f32(GCM_ROWS, LANES), f32(4 * LEV, LANES)),
        input_output_aliases={2: 0},
        compiler_params=pltpu.CompilerParams(vmem_limit_bytes=8 * MIB),
        name="home",
    )(returned, routes, gcm_next)
    return gcm_next.reshape(gcm_state.shape), stats.reshape(2, LEV, 2, LANES)


def solution(mesh):
    grid = P(None, None, "blk", "sub")
    return jax.shard_map(
        body,
        mesh=mesh,
        in_specs=(grid, P(None, None, None, ("blk", "sub")), P("blk", "sub"), P("blk", "sub"), P()),
        out_specs=(grid, grid),
        check_vma=False,
    )
```

```python
import math

import jax
import jax.numpy as jnp
from jax import lax
from jax.experimental import pallas as pl
from jax.experimental.pallas import tpu as pltpu
from jax.sharding import PartitionSpec as P

SUBSTEPS = 4
LEV = 32
NXC = 64
LANES = 128
DEVICES = 128
COLS = 256
FIELDS = 6
SUB = 8
INNER = NXC // SUB
GCM_ROWS = FIELDS * LEV * 2
CRM_CHUNK = 8
PLANE = 8
ALPHA = 0.3 * math.log2(math.e)
BETA = 1.5 * ALPHA
SHIFT = math.log2(0.5 * BETA)
MIB = 1 << 20


def pieces(x):
    first = x.astype(jnp.bfloat16)
    rest = x - first.astype(jnp.float32)
    second = rest.astype(jnp.bfloat16)
    third = (rest - second.astype(jnp.float32)).astype(jnp.bfloat16)
    return first, second, third


def select_dot(x, chosen, dims, x_first):
    total = None
    for part in pieces(x):
        pair = (part, chosen) if x_first else (chosen, part)
        term = lax.dot_general(*pair, (dims, ((), ())), preferred_element_type=jnp.float32)
        total = term if total is None else total + term
    return total


def rows_of(ref, y):
    return ref[pl.ds(y, FIELDS * LEV, stride=2), :]


def cut_kernel(gcm_hbm, row, gcm, arrival):
    @pl.when(lax.rem(lax.axis_index("blk"), PLANE) == 0)
    def _():
        copy = pltpu.make_async_copy(gcm_hbm, gcm, arrival)
        copy.start()
        copy.wait()
        row[: FIELDS * LEV, :] = rows_of(gcm, 0)
        row[FIELDS * LEV :, :] = jnp.zeros((SUB, LANES), jnp.float32)


def edge_kernel(
    cut_first, gcm_hbm, owner_hbm, branch_hbm, diffusion_hbm,
    gcm, to_core_mate, to_neighbour, to_chip_mate, to_other, routes, rates, number,
    owner, branch, diffusion, arrival,
):
    del cut_first
    loads = [
        pltpu.make_async_copy(source, target, arrival.at[n])
        for n, (source, target) in enumerate(
            [(owner_hbm, owner), (branch_hbm, branch), (diffusion_hbm, diffusion), (gcm_hbm, gcm)]
        )
    ]
    for copy in loads:
        copy.start()
    to_chip_mate[...] = jnp.zeros_like(to_chip_mate)
    to_other[...] = jnp.zeros_like(to_other)
    for copy in loads[:3]:
        copy.wait()
    device = lax.broadcasted_iota(jnp.int32, (DEVICES, LANES), 0)
    target = jnp.concatenate(
        [(device == owner[y : y + 1, :]).astype(jnp.float32) for y in range(2)], axis=1
    )
    earlier = (
        lax.broadcasted_iota(jnp.int32, (COLS, COLS), 0)
        < lax.broadcasted_iota(jnp.int32, (COLS, COLS), 1)
    ).astype(jnp.bfloat16)
    count = jnp.dot(target.astype(jnp.bfloat16), earlier, preferred_element_type=jnp.float32)
    for slot in range(2):
        here = jnp.where(count < 0.5, 1.0 - slot, 0.0 + slot)
        routes[slot] = (target * here).astype(jnp.bfloat16)
    rates[...] = jnp.where(branch[...] == 1, 0.6, 0.2)
    for f in range(FIELDS):
        spread = jnp.broadcast_to(diffusion[f : f + 1, :], (LANES, LEV))
        number[f * LEV : (f + 1) * LEV, :] = jnp.transpose(spread)

    loads[3].wait()
    core = lax.rem(lax.axis_index("blk"), 2)
    to_core_mate[...] = rows_of(gcm, 1 - core)
    to_neighbour[...] = rows_of(gcm, core)
    even = lax.rem(lax.axis_index("sub"), 2) == 0
    rows = jnp.concatenate([rows_of(gcm, 0), rows_of(gcm, 1)], axis=0)
    for part in range(GCM_ROWS // LANES):
        turned = jnp.transpose(rows[part * LANES : (part + 1) * LANES])
        first, last = turned[:1], turned[LANES - 1 :]
        to_chip_mate[part : part + 1, :] = jnp.where(even, last, first)
        to_other[part : part + 1, :] = jnp.where(even, first, last)


def early_kernel(crm_hbm, gcm, number, state, sums, partial, crm, arrival):
    loads = [
        pltpu.make_async_copy(
            crm_hbm.at[f, pl.ds(part * CRM_CHUNK, CRM_CHUNK)],
            crm.at[f, pl.ds(part * CRM_CHUNK, CRM_CHUNK)],
            arrival.at[f, part],
        )
        for f in range(2)
        for part in range(LEV // CRM_CHUNK)
    ]
    for copy in loads:
        copy.start()
    lane = lax.broadcasted_iota(jnp.int32, (FIELDS * LEV, LANES), 1)
    own = [rows_of(gcm, 0), rows_of(gcm, 1)]
    for y in range(2):
        before = jnp.where(lane == 0, 0.0, pltpu.roll(own[y], 1, axis=1))
        after = jnp.where(lane == LANES - 1, 0.0, pltpu.roll(own[y], LANES - 1, axis=1))
        around = own[1 - y] + after + before
        partial[y] = own[y] + number[...] * (around - 4.0 * own[y])

    for f, (scale, shift) in enumerate([(ALPHA, SHIFT), (BETA, 0.0)]):
        for part in range(LEV // CRM_CHUNK):
            loads[f * (LEV // CRM_CHUNK) + part].wait()

            def level(n, carry):
                k = part * CRM_CHUNK + n
                for half in range(2):
                    x = crm[f, k, :, half * LANES : (half + 1) * LANES].astype(jnp.float32)
                    x = x * scale + shift
                    total = None
                    for row in range(SUB):
                        block = x[row * INNER : (row + 1) * INNER]
                        state[f, half, pl.ds(k * NXC + row, INNER, stride=SUB), :] = block
                        total = block if total is None else total + block
                    sums[f, half, pl.ds(pl.multiple_of(k * SUB, SUB), SUB), :] = total
                return carry

            lax.fori_loop(0, CRM_CHUNK, level, 0, unroll=4)


def prepare_kernel(
    partial, number, neighbour, core_mate, other, chip_mate, across, routes, rates,
    advanced, outgoing,
):
    lane = lax.broadcasted_iota(jnp.int32, (FIELDS * LEV, LANES), 1)
    level = lax.broadcasted_iota(jnp.int32, (LEV, LANES), 0)

    def columns(ref):
        turned = jnp.transpose(ref)
        column = jnp.concatenate([turned[:, n : n + 1] for n in range(GCM_ROWS // LANES)], axis=0)
        return column[: FIELDS * LEV], column[FIELDS * LEV :]

    core = lax.rem(lax.axis_index("blk"), 2)
    border = lax.rem(lax.axis_index("blk"), PLANE) == PLANE - 1
    inside = core_mate[...]
    outside = jnp.where(border, across[: FIELDS * LEV, :], neighbour[...])
    vertical = [
        jnp.where(core == 0, outside, inside),
        jnp.where(core == 0, inside, outside),
    ]
    even = lax.rem(lax.axis_index("sub"), 2) == 0
    near, far = chip_mate[...], other[...]
    west, east = columns(jnp.where(even, far, near)), columns(jnp.where(even, near, far))
    values = []
    for y in range(2):
        side = jnp.where(lane == 0, west[y], jnp.where(lane == LANES - 1, east[y], 0.0))
        state = partial[y] + number[...] * (vertical[y] + side)
        advanced[pl.ds(y, 4 * LEV, stride=2), :] = state[2 * LEV :]
        field = [state[f * LEV : (f + 1) * LEV] for f in range(FIELDS)]
        warm = ALPHA * (0.25 * field[0] + 0.2 * field[4])
        wet = BETA * (0.25 * field[1] + 0.2 * field[5])
        drift = 0.45 * jnp.tanh(field[2])
        tilt = jnp.tanh(field[3])
        rise = 0.15 * (tilt + pltpu.roll(tilt, LEV - 1, axis=0))
        rise = jnp.where(level == LEV - 1, rates[y : y + 1, :], rise)
        values.append(jnp.concatenate([warm, wet, drift, rise], axis=0))
    values = jnp.concatenate(values, axis=1)
    for slot in range(2):
        outgoing[pl.ds(slot, DEVICES, stride=2), :] = select_dot(
            values, routes[slot], ((1,), (1,)), False
        )


def cloud_kernel(
    incoming, start, sums, advanced, outgoing, gcm_next,
    state, coef, mean, total, square, departure,
):
    leaving = pltpu.make_async_copy(
        advanced, gcm_next.at[pl.ds(2 * 2 * LEV, 4 * 2 * LEV)], departure
    )
    leaving.start()
    level = lax.broadcasted_iota(jnp.int32, (LEV, LANES), 0)
    top = level == LEV - 1
    rates = []

    def up(x):
        return pltpu.roll(x, LEV - 1, axis=0)

    def down(x):
        return pltpu.roll(x, 1, axis=0)

    def folded(ref, *lead):
        out = None
        for part in range(SUB):
            x = ref[(*lead, pl.ds(part, LEV, stride=SUB), slice(None))]
            out = x if out is None else out + x
        return out

    for half in range(2):
        values = jnp.transpose(incoming[half * LANES : (half + 1) * LANES, :])
        rise = values[3 * LEV :]
        rates.append(rise[LEV - 1 :])
        rise = jnp.where(top, 0.0, rise)
        base = SHIFT * (1.0 - rise + down(rise))
        coef[0, half] = values[:LEV] + SHIFT - 0.75 * base
        coef[1, half] = values[LEV : 2 * LEV]
        coef[2, half] = values[2 * LEV : 3 * LEV]
        coef[3, half] = rise
        coef[7, half] = jnp.broadcast_to(rates[half], (LEV, LANES))
        for f in range(2):
            mean[f, half] = folded(sums, f, half) * (1.0 / NXC)

    def relax():
        for half in range(2):
            rise = coef[3, half]
            for f in range(2):
                now = mean[f, half]
                flux = rise * jnp.where(rise > 0.0, now, up(now))
                now = now - flux + down(flux)
                add = coef[f, half] - 0.25 * now
                coef[4 + f, half] = add
                mean[f, half] = now + add
                if f == 0:
                    coef[6, half] = now + add

    def settle():
        for half in range(2):
            rain = folded(total, half) * (1.0 / NXC)
            mean[0, half] = mean[0, half] + rain
            mean[1, half] = mean[1, half] - rain
            mean[2, half] = mean[2, half] + rain

    def sweep(source, half, last):
        rate = jnp.broadcast_to(coef[7, half, 0:1, :], (SUB, LANES))

        def row(index, k):
            return jnp.broadcast_to(coef[index, half, k : k + 1, :], (SUB, LANES))

        def drifted(f, k, size, positive):
            cells = [
                source[f, half, k * NXC + j * SUB : k * NXC + (j + 1) * SUB, :]
                for j in range(INNER)
            ]
            before = [pltpu.roll(cells[-1], 1, axis=0)] + cells[:-1]
            after = cells[1:] + [pltpu.roll(cells[0], SUB - 1, axis=0)]
            return [
                c + size * (jnp.where(positive, b, a) - c)
                for c, b, a in zip(cells, before, after)
            ]

        def level_of(k):
            drift = row(2, k)
            size, positive = jnp.abs(drift), drift > 0.0
            return [drifted(f, k, size, positive) for f in range(2)]

        now = level_of(0)
        below = None
        for k in range(LEV):
            add = [row(4, k), row(5, k)]
            if k < LEV - 1:
                after = level_of(k + 1)
                rise = row(3, k)
                upward = rise > 0.0
                flux = [
                    [rise * jnp.where(upward, a, b) for a, b in zip(now[f], after[f])]
                    for f in range(2)
                ]
            rained = None
            spread = None
            if last:
                middle = row(6, k)
            for j in range(INNER):
                new = []
                for f in range(2):
                    x = now[f][j]
                    if k < LEV - 1:
                        x = x - flux[f][j]
                    if k > 0:
                        x = x + below[f][j]
                    new.append(x + add[f])
                temper, moisture = new
                rain = rate * jnp.maximum(moisture - jnp.exp2(temper), 0.0)
                temper = temper + rain
                rained = rain if rained is None else rained + rain
                if last:
                    away = temper - middle
                    spread = away * away if spread is None else spread + away * away
                else:
                    at = slice(k * NXC + j * SUB, k * NXC + (j + 1) * SUB)
                    state[0, half, at, :] = temper
                    state[1, half, at, :] = moisture - rain
            total[half, k * SUB : (k + 1) * SUB, :] = rained
            if last:
                square[half, k * SUB : (k + 1) * SUB, :] = spread
            if k < LEV - 1:
                below, now = flux, after

    def substep(source, last):
        relax()

        def half_of(half, carry):
            sweep(source, half, last)
            return carry

        lax.fori_loop(0, 2, half_of, 0)
        if not last:
            settle()

    for half in range(2):
        mean[2, half] = jnp.zeros((LEV, LANES), jnp.float32)
    substep(start, False)

    def middle_step(step, carry):
        substep(state, False)
        return carry

    lax.fori_loop(0, SUBSTEPS - 2, middle_step, 0)
    substep(state, True)
    settle()
    for half in range(2):
        warm, wet, rain = mean[0, half], mean[1, half], mean[2, half]
        gap = warm - coef[6, half]
        spread = folded(square, half) * (1.0 / NXC) - gap * gap
        result = [
            (warm - SHIFT) * (1.0 / ALPHA),
            wet * (1.0 / BETA),
            rain * (1.0 / BETA),
            spread * (1.0 / (ALPHA * ALPHA)),
        ]
        outgoing[half * LANES : (half + 1) * LANES, :] = jnp.transpose(
            jnp.concatenate(result, axis=0)
        )
    leaving.wait()


def home_kernel(returned, routes, begun, gcm_next, stats):
    del begun
    home = None
    for slot in range(2):
        back = returned[pl.ds(slot, DEVICES, stride=2), :]
        term = select_dot(jnp.transpose(back), routes[slot], ((1,), (0,)), True)
        home = term if home is None else home + term
    for y in range(2):
        part = home[:, y * LANES : (y + 1) * LANES]
        gcm_next[pl.ds(y, 2 * LEV, stride=2), :] = part[: 2 * LEV]
        stats[pl.ds(y, 2 * LEV, stride=2), :] = part[2 * LEV :]


def whole(shape):
    return pl.BlockSpec(shape, lambda *_: (0,) * len(shape))


def f32(*shape):
    return jax.ShapeDtypeStruct(shape, jnp.float32)


def in_hbm(x):
    return pltpu.with_memory_space_constraint(x, pltpu.HBM)


def transfer(rows):
    moved = lax.all_to_all(
        rows.reshape(DEVICES, 2, LANES), ("blk", "sub"), split_axis=0, concat_axis=0, tiled=True
    )
    return moved.reshape(COLS, LANES)


def body(gcm_state, crm_state, owner, branch, diffusion):
    gcm = gcm_state.reshape(GCM_ROWS, LANES)

    def pairs(n, first):
        ahead = [(i, (i + 1) % n) for i in range(first, n, 2)]
        return ahead + [(j, i) for i, j in ahead]

    n_blk, n_sub = lax.axis_size("blk"), lax.axis_size("sub")
    hbm = pl.BlockSpec(memory_space=pltpu.HBM)
    row = pl.pallas_call(
        cut_kernel,
        in_specs=[hbm],
        out_shape=f32(FIELDS * LEV + SUB, LANES),
        scratch_shapes=[pltpu.VMEM((GCM_ROWS, LANES), jnp.float32), pltpu.SemaphoreType.DMA(())],
        compiler_params=pltpu.CompilerParams(vmem_limit_bytes=4 * MIB),
        name="cut",
    )(in_hbm(gcm))
    across = lax.ppermute(row, "blk", pairs(n_blk, 1))
    gcm_here, to_core_mate, to_neighbour, to_chip_mate, to_other, routes, rates, number = pl.pallas_call(
        edge_kernel,
        in_specs=[pl.BlockSpec(memory_space=pl.ANY)] + [hbm] * 4,
        out_shape=(
            f32(GCM_ROWS, LANES),
            f32(FIELDS * LEV, LANES),
            f32(FIELDS * LEV, LANES),
            f32(SUB, LANES),
            f32(SUB, LANES),
            jax.ShapeDtypeStruct((2, DEVICES, COLS), jnp.bfloat16),
            f32(2, LANES),
            f32(FIELDS * LEV, LANES),
        ),
        scratch_shapes=[
            pltpu.VMEM((2, LANES), jnp.int32),
            pltpu.VMEM((2, LANES), jnp.int32),
            pltpu.VMEM((FIELDS, LEV), jnp.float32),
            pltpu.SemaphoreType.DMA((4,)),
        ],
        compiler_params=pltpu.CompilerParams(vmem_limit_bytes=4 * MIB),
        name="edges",
    )(row, *map(in_hbm, (gcm, owner, branch, diffusion)))
    neighbour = lax.ppermute(to_neighbour, "blk", pairs(n_blk, 1))
    core_mate = lax.ppermute(to_core_mate, "blk", pairs(n_blk, 0))
    chip_mate = lax.ppermute(to_chip_mate, "sub", pairs(n_sub, 0))
    other = lax.ppermute(to_other, "sub", pairs(n_sub, 1))
    cells = 2 * LEV * NXC * COLS
    state, sums, partial = pl.pallas_call(
        early_kernel,
        in_specs=[hbm, whole((GCM_ROWS, LANES)), whole((FIELDS * LEV, LANES))],
        out_shape=(
            f32(2, 2, LEV * NXC, LANES),
            f32(2, 2, LEV * SUB, LANES),
            f32(2, FIELDS * LEV, LANES),
        ),
        scratch_shapes=[
            pltpu.VMEM((2, LEV, NXC, COLS), jnp.bfloat16),
            pltpu.SemaphoreType.DMA((2, LEV // CRM_CHUNK)),
        ],
        compiler_params=pltpu.CompilerParams(vmem_limit_bytes=16 * MIB),
        cost_estimate=pl.CostEstimate(flops=4 * cells, bytes_accessed=6 * cells, transcendentals=0),
        name="early",
    )(in_hbm(crm_state), gcm_here, number)
    advanced, outgoing = pl.pallas_call(
        prepare_kernel,
        out_shape=(f32(4 * 2 * LEV, LANES), f32(COLS, LANES)),
        compiler_params=pltpu.CompilerParams(vmem_limit_bytes=8 * MIB),
        name="prepare",
    )(partial, number, neighbour, core_mate, other, chip_mate, across, routes, rates)

    incoming = transfer(outgoing)
    profiles, gcm_next = pl.pallas_call(
        cloud_kernel,
        out_specs=(whole((COLS, LANES)), hbm),
        out_shape=(f32(COLS, LANES), f32(GCM_ROWS, LANES)),
        scratch_shapes=[
            pltpu.VMEM((2, 2, LEV * NXC, LANES), jnp.float32),
            pltpu.VMEM((8, 2, LEV, LANES), jnp.float32),
            pltpu.VMEM((3, 2, LEV, LANES), jnp.float32),
            pltpu.VMEM((2, LEV * SUB, LANES), jnp.float32),
            pltpu.VMEM((2, LEV * SUB, LANES), jnp.float32),
            pltpu.SemaphoreType.DMA(()),
        ],
        compiler_params=pltpu.CompilerParams(vmem_limit_bytes=12 * MIB),
        name="cloud",
    )(incoming, state, sums, advanced)
    returned = transfer(profiles)

    gcm_next, stats = pl.pallas_call(
        home_kernel,
        grid=(1,),
        in_specs=[
            whole((COLS, LANES)),
            whole((2, DEVICES, COLS)),
            pl.BlockSpec(memory_space=pl.ANY),
        ],
        out_specs=(whole((4 * LEV, LANES)), whole((4 * LEV, LANES))),
        out_shape=(f32(GCM_ROWS, LANES), f32(4 * LEV, LANES)),
        input_output_aliases={2: 0},
        compiler_params=pltpu.CompilerParams(vmem_limit_bytes=8 * MIB),
        name="home",
    )(returned, routes, gcm_next)
    return gcm_next.reshape(gcm_state.shape), stats.reshape(2, LEV, 2, LANES)


def solution(mesh):
    grid = P(None, None, "blk", "sub")
    return jax.shard_map(
        body,
        mesh=mesh,
        in_specs=(grid, P(None, None, None, ("blk", "sub")), P("blk", "sub"), P("blk", "sub"), P()),
        out_specs=(grid, grid),
        check_vma=False,
    )
```

```python
import math

import jax
import jax.numpy as jnp
from jax import lax
from jax.experimental import pallas as pl
from jax.experimental.pallas import tpu as pltpu
from jax.sharding import PartitionSpec as P

SUBSTEPS = 4
LEV = 32
NXC = 64
LANES = 128
DEVICES = 128
COLS = 256
FIELDS = 6
SUB = 8
INNER = NXC // SUB
GCM_ROWS = FIELDS * LEV * 2
CRM_CHUNK = 8
ALPHA = 0.3 * math.log2(math.e)
BETA = 1.5 * ALPHA
SHIFT = math.log2(0.5 * BETA)
MIB = 1 << 20


def pieces(x):
    first = x.astype(jnp.bfloat16)
    rest = x - first.astype(jnp.float32)
    second = rest.astype(jnp.bfloat16)
    third = (rest - second.astype(jnp.float32)).astype(jnp.bfloat16)
    return first, second, third


def select_dot(x, chosen, dims, x_first):
    total = None
    for part in pieces(x):
        pair = (part, chosen) if x_first else (chosen, part)
        term = lax.dot_general(*pair, (dims, ((), ())), preferred_element_type=jnp.float32)
        total = term if total is None else total + term
    return total


def rows_of(ref, y):
    return ref[pl.ds(y, FIELDS * LEV, stride=2), :]


def load_kernel(
    gcm_hbm, owner_hbm, branch_hbm, diffusion_hbm,
    gcm, to_core_mate, to_neighbour, owner, branch, diffusion, arrival,
):
    loads = [
        pltpu.make_async_copy(source, target, arrival.at[n])
        for n, (source, target) in enumerate(
            [(gcm_hbm, gcm), (owner_hbm, owner), (branch_hbm, branch), (diffusion_hbm, diffusion)]
        )
    ]
    for copy in loads:
        copy.start()
    for copy in loads:
        copy.wait()
    core = lax.rem(lax.axis_index("blk"), 2)
    to_core_mate[...] = rows_of(gcm, 1 - core)
    to_neighbour[...] = rows_of(gcm, core)


def edge_kernel(
    gcm, owner, branch, diffusion, to_chip_mate, to_other, routes, rates, number
):
    to_chip_mate[...] = jnp.zeros_like(to_chip_mate)
    to_other[...] = jnp.zeros_like(to_other)
    device = lax.broadcasted_iota(jnp.int32, (DEVICES, LANES), 0)
    target = jnp.concatenate(
        [(device == owner[y : y + 1, :]).astype(jnp.float32) for y in range(2)], axis=1
    )
    earlier = (
        lax.broadcasted_iota(jnp.int32, (COLS, COLS), 0)
        < lax.broadcasted_iota(jnp.int32, (COLS, COLS), 1)
    ).astype(jnp.bfloat16)
    count = jnp.dot(target.astype(jnp.bfloat16), earlier, preferred_element_type=jnp.float32)
    for slot in range(2):
        here = jnp.where(count < 0.5, 1.0 - slot, 0.0 + slot)
        routes[slot] = (target * here).astype(jnp.bfloat16)
    rates[...] = jnp.where(branch[...] == 1, 0.6, 0.2)
    for f in range(FIELDS):
        spread = jnp.broadcast_to(diffusion[f : f + 1, :], (LANES, LEV))
        number[f * LEV : (f + 1) * LEV, :] = jnp.transpose(spread)

    even = lax.rem(lax.axis_index("sub"), 2) == 0
    rows = jnp.concatenate([rows_of(gcm, 0), rows_of(gcm, 1)], axis=0)
    for part in range(GCM_ROWS // LANES):
        turned = jnp.transpose(rows[part * LANES : (part + 1) * LANES])
        first, last = turned[:1], turned[LANES - 1 :]
        to_chip_mate[part : part + 1, :] = jnp.where(even, last, first)
        to_other[part : part + 1, :] = jnp.where(even, first, last)


def early_kernel(crm_hbm, gcm, number, state, sums, partial, crm, arrival):
    loads = [
        pltpu.make_async_copy(
            crm_hbm.at[f, pl.ds(part * CRM_CHUNK, CRM_CHUNK)],
            crm.at[f, pl.ds(part * CRM_CHUNK, CRM_CHUNK)],
            arrival.at[f, part],
        )
        for f in range(2)
        for part in range(LEV // CRM_CHUNK)
    ]
    for copy in loads:
        copy.start()
    lane = lax.broadcasted_iota(jnp.int32, (FIELDS * LEV, LANES), 1)
    own = [rows_of(gcm, 0), rows_of(gcm, 1)]
    for y in range(2):
        before = jnp.where(lane == 0, 0.0, pltpu.roll(own[y], 1, axis=1))
        after = jnp.where(lane == LANES - 1, 0.0, pltpu.roll(own[y], LANES - 1, axis=1))
        around = own[1 - y] + after + before
        partial[y] = own[y] + number[...] * (around - 4.0 * own[y])

    for f, (scale, shift) in enumerate([(ALPHA, SHIFT), (BETA, 0.0)]):
        for part in range(LEV // CRM_CHUNK):
            loads[f * (LEV // CRM_CHUNK) + part].wait()

            def level(n, carry):
                k = part * CRM_CHUNK + n
                for half in range(2):
                    x = crm[f, k, :, half * LANES : (half + 1) * LANES].astype(jnp.float32)
                    x = x * scale + shift
                    total = None
                    for row in range(SUB):
                        block = x[row * INNER : (row + 1) * INNER]
                        state[f, half, pl.ds(k * NXC + row, INNER, stride=SUB), :] = block
                        total = block if total is None else total + block
                    sums[f, half, pl.ds(pl.multiple_of(k * SUB, SUB), SUB), :] = total
                return carry

            lax.fori_loop(0, CRM_CHUNK, level, 0, unroll=4)


def prepare_kernel(
    partial, number, neighbour, core_mate, other, chip_mate, routes, rates, advanced, outgoing
):
    lane = lax.broadcasted_iota(jnp.int32, (FIELDS * LEV, LANES), 1)
    level = lax.broadcasted_iota(jnp.int32, (LEV, LANES), 0)

    def columns(ref):
        turned = jnp.transpose(ref)
        column = jnp.concatenate([turned[:, n : n + 1] for n in range(GCM_ROWS // LANES)], axis=0)
        return column[: FIELDS * LEV], column[FIELDS * LEV :]

    core = lax.rem(lax.axis_index("blk"), 2)
    inside, outside = core_mate[...], neighbour[...]
    vertical = [
        jnp.where(core == 0, outside, inside),
        jnp.where(core == 0, inside, outside),
    ]
    even = lax.rem(lax.axis_index("sub"), 2) == 0
    near, far = chip_mate[...], other[...]
    west, east = columns(jnp.where(even, far, near)), columns(jnp.where(even, near, far))
    values = []
    for y in range(2):
        side = jnp.where(lane == 0, west[y], jnp.where(lane == LANES - 1, east[y], 0.0))
        state = partial[y] + number[...] * (vertical[y] + side)
        advanced[pl.ds(y, 4 * LEV, stride=2), :] = state[2 * LEV :]
        field = [state[f * LEV : (f + 1) * LEV] for f in range(FIELDS)]
        warm = ALPHA * (0.25 * field[0] + 0.2 * field[4])
        wet = BETA * (0.25 * field[1] + 0.2 * field[5])
        drift = 0.45 * jnp.tanh(field[2])
        tilt = jnp.tanh(field[3])
        rise = 0.15 * (tilt + pltpu.roll(tilt, LEV - 1, axis=0))
        rise = jnp.where(level == LEV - 1, rates[y : y + 1, :], rise)
        values.append(jnp.concatenate([warm, wet, drift, rise], axis=0))
    values = jnp.concatenate(values, axis=1)
    for slot in range(2):
        outgoing[pl.ds(slot, DEVICES, stride=2), :] = select_dot(
            values, routes[slot], ((1,), (1,)), False
        )


def cloud_kernel(
    incoming, start, sums, advanced, outgoing, gcm_next,
    state, coef, mean, total, square, departure,
):
    leaving = pltpu.make_async_copy(
        advanced, gcm_next.at[pl.ds(2 * 2 * LEV, 4 * 2 * LEV)], departure
    )
    leaving.start()
    level = lax.broadcasted_iota(jnp.int32, (LEV, LANES), 0)
    top = level == LEV - 1
    rates = []

    def up(x):
        return pltpu.roll(x, LEV - 1, axis=0)

    def down(x):
        return pltpu.roll(x, 1, axis=0)

    def folded(ref, *lead):
        out = None
        for part in range(SUB):
            x = ref[(*lead, pl.ds(part, LEV, stride=SUB), slice(None))]
            out = x if out is None else out + x
        return out

    for half in range(2):
        values = jnp.transpose(incoming[half * LANES : (half + 1) * LANES, :])
        rise = values[3 * LEV :]
        rates.append(rise[LEV - 1 :])
        rise = jnp.where(top, 0.0, rise)
        base = SHIFT * (1.0 - rise + down(rise))
        coef[0, half] = values[:LEV] + SHIFT - 0.75 * base
        coef[1, half] = values[LEV : 2 * LEV]
        coef[2, half] = values[2 * LEV : 3 * LEV]
        coef[3, half] = rise
        coef[7, half] = jnp.broadcast_to(rates[half], (LEV, LANES))
        for f in range(2):
            mean[f, half] = folded(sums, f, half) * (1.0 / NXC)

    def relax():
        for half in range(2):
            rise = coef[3, half]
            for f in range(2):
                now = mean[f, half]
                flux = rise * jnp.where(rise > 0.0, now, up(now))
                now = now - flux + down(flux)
                add = coef[f, half] - 0.25 * now
                coef[4 + f, half] = add
                mean[f, half] = now + add
                if f == 0:
                    coef[6, half] = now + add

    def settle():
        for half in range(2):
            rain = folded(total, half) * (1.0 / NXC)
            mean[0, half] = mean[0, half] + rain
            mean[1, half] = mean[1, half] - rain
            mean[2, half] = mean[2, half] + rain

    def sweep(source, half, last):
        rate = jnp.broadcast_to(coef[7, half, 0:1, :], (SUB, LANES))

        def row(index, k):
            return jnp.broadcast_to(coef[index, half, k : k + 1, :], (SUB, LANES))

        def drifted(f, k, size, positive):
            cells = [
                source[f, half, k * NXC + j * SUB : k * NXC + (j + 1) * SUB, :]
                for j in range(INNER)
            ]
            before = [pltpu.roll(cells[-1], 1, axis=0)] + cells[:-1]
            after = cells[1:] + [pltpu.roll(cells[0], SUB - 1, axis=0)]
            return [
                c + size * (jnp.where(positive, b, a) - c)
                for c, b, a in zip(cells, before, after)
            ]

        def level_of(k):
            drift = row(2, k)
            size, positive = jnp.abs(drift), drift > 0.0
            return [drifted(f, k, size, positive) for f in range(2)]

        now = level_of(0)
        below = None
        for k in range(LEV):
            add = [row(4, k), row(5, k)]
            if k < LEV - 1:
                after = level_of(k + 1)
                rise = row(3, k)
                upward = rise > 0.0
                flux = [
                    [rise * jnp.where(upward, a, b) for a, b in zip(now[f], after[f])]
                    for f in range(2)
                ]
            rained = None
            spread = None
            if last:
                middle = row(6, k)
            for j in range(INNER):
                new = []
                for f in range(2):
                    x = now[f][j]
                    if k < LEV - 1:
                        x = x - flux[f][j]
                    if k > 0:
                        x = x + below[f][j]
                    new.append(x + add[f])
                temper, moisture = new
                rain = rate * jnp.maximum(moisture - jnp.exp2(temper), 0.0)
                temper = temper + rain
                rained = rain if rained is None else rained + rain
                if last:
                    away = temper - middle
                    spread = away * away if spread is None else spread + away * away
                else:
                    at = slice(k * NXC + j * SUB, k * NXC + (j + 1) * SUB)
                    state[0, half, at, :] = temper
                    state[1, half, at, :] = moisture - rain
            total[half, k * SUB : (k + 1) * SUB, :] = rained
            if last:
                square[half, k * SUB : (k + 1) * SUB, :] = spread
            if k < LEV - 1:
                below, now = flux, after

    def substep(source, last):
        relax()

        def half_of(half, carry):
            sweep(source, half, last)
            return carry

        lax.fori_loop(0, 2, half_of, 0)
        if not last:
            settle()

    for half in range(2):
        mean[2, half] = jnp.zeros((LEV, LANES), jnp.float32)
    substep(start, False)

    def middle_step(step, carry):
        substep(state, False)
        return carry

    lax.fori_loop(0, SUBSTEPS - 2, middle_step, 0)
    substep(state, True)
    settle()
    for half in range(2):
        warm, wet, rain = mean[0, half], mean[1, half], mean[2, half]
        gap = warm - coef[6, half]
        spread = folded(square, half) * (1.0 / NXC) - gap * gap
        result = [
            (warm - SHIFT) * (1.0 / ALPHA),
            wet * (1.0 / BETA),
            rain * (1.0 / BETA),
            spread * (1.0 / (ALPHA * ALPHA)),
        ]
        outgoing[half * LANES : (half + 1) * LANES, :] = jnp.transpose(
            jnp.concatenate(result, axis=0)
        )
    leaving.wait()


def home_kernel(returned, routes, begun, gcm_next, stats, rows, departure):
    del begun
    home = None
    for slot in range(2):
        back = returned[pl.ds(slot, DEVICES, stride=2), :]
        term = select_dot(jnp.transpose(back), routes[slot], ((1,), (0,)), True)
        home = term if home is None else home + term
    for y in range(2):
        part = home[:, y * LANES : (y + 1) * LANES]
        rows[pl.ds(y, 4 * LEV, stride=2), :] = part
    copies = [
        pltpu.make_async_copy(
            rows.at[pl.ds(0, 4 * LEV)], gcm_next.at[pl.ds(0, 4 * LEV)], departure.at[0]
        ),
        pltpu.make_async_copy(rows.at[pl.ds(4 * LEV, 4 * LEV)], stats, departure.at[1]),
    ]
    for copy in copies:
        copy.start()
    for copy in copies:
        copy.wait()


def whole(shape):
    return pl.BlockSpec(shape, lambda *_: (0,) * len(shape))


def f32(*shape):
    return jax.ShapeDtypeStruct(shape, jnp.float32)


def in_hbm(x):
    return pltpu.with_memory_space_constraint(x, pltpu.HBM)


def transfer(rows):
    moved = lax.all_to_all(
        rows.reshape(DEVICES, 2, LANES), ("blk", "sub"), split_axis=0, concat_axis=0, tiled=True
    )
    return moved.reshape(COLS, LANES)


def body(gcm_state, crm_state, owner, branch, diffusion):
    gcm = gcm_state.reshape(GCM_ROWS, LANES)

    def pairs(n, first):
        ahead = [(i, (i + 1) % n) for i in range(first, n, 2)]
        return ahead + [(j, i) for i, j in ahead]

    n_blk, n_sub = lax.axis_size("blk"), lax.axis_size("sub")
    hbm = pl.BlockSpec(memory_space=pltpu.HBM)
    gcm_here, to_core_mate, to_neighbour, owner_here, branch_here, diffusion_here = pl.pallas_call(
        load_kernel,
        in_specs=[hbm] * 4,
        out_shape=(
            f32(GCM_ROWS, LANES),
            f32(FIELDS * LEV, LANES),
            f32(FIELDS * LEV, LANES),
            jax.ShapeDtypeStruct(owner.shape, owner.dtype),
            jax.ShapeDtypeStruct(branch.shape, branch.dtype),
            f32(*diffusion.shape),
        ),
        scratch_shapes=[pltpu.SemaphoreType.DMA((4,))],
        compiler_params=pltpu.CompilerParams(vmem_limit_bytes=4 * MIB),
        name="load",
    )(*map(in_hbm, (gcm, owner, branch, diffusion)))
    neighbour = lax.ppermute(to_neighbour, "blk", pairs(n_blk, 1))
    core_mate = lax.ppermute(to_core_mate, "blk", pairs(n_blk, 0))
    to_chip_mate, to_other, routes, rates, number = pl.pallas_call(
        edge_kernel,
        out_shape=(
            f32(SUB, LANES),
            f32(SUB, LANES),
            jax.ShapeDtypeStruct((2, DEVICES, COLS), jnp.bfloat16),
            f32(2, LANES),
            f32(FIELDS * LEV, LANES),
        ),
        compiler_params=pltpu.CompilerParams(vmem_limit_bytes=4 * MIB),
        name="edges",
    )(gcm_here, owner_here, branch_here, diffusion_here)
    chip_mate = lax.ppermute(to_chip_mate, "sub", pairs(n_sub, 0))
    other = lax.ppermute(to_other, "sub", pairs(n_sub, 1))
    cells = 2 * LEV * NXC * COLS
    state, sums, partial = pl.pallas_call(
        early_kernel,
        in_specs=[hbm, whole((GCM_ROWS, LANES)), whole((FIELDS * LEV, LANES))],
        out_shape=(
            f32(2, 2, LEV * NXC, LANES),
            f32(2, 2, LEV * SUB, LANES),
            f32(2, FIELDS * LEV, LANES),
        ),
        scratch_shapes=[
            pltpu.VMEM((2, LEV, NXC, COLS), jnp.bfloat16),
            pltpu.SemaphoreType.DMA((2, LEV // CRM_CHUNK)),
        ],
        compiler_params=pltpu.CompilerParams(vmem_limit_bytes=16 * MIB),
        cost_estimate=pl.CostEstimate(flops=4 * cells, bytes_accessed=6 * cells, transcendentals=0),
        name="early",
    )(in_hbm(crm_state), gcm_here, number)
    advanced, outgoing = pl.pallas_call(
        prepare_kernel,
        out_shape=(f32(4 * 2 * LEV, LANES), f32(COLS, LANES)),
        compiler_params=pltpu.CompilerParams(vmem_limit_bytes=8 * MIB),
        name="prepare",
    )(partial, number, neighbour, core_mate, other, chip_mate, routes, rates)

    incoming = transfer(outgoing)
    profiles, gcm_next = pl.pallas_call(
        cloud_kernel,
        out_specs=(whole((COLS, LANES)), hbm),
        out_shape=(f32(COLS, LANES), f32(GCM_ROWS, LANES)),
        scratch_shapes=[
            pltpu.VMEM((2, 2, LEV * NXC, LANES), jnp.float32),
            pltpu.VMEM((8, 2, LEV, LANES), jnp.float32),
            pltpu.VMEM((3, 2, LEV, LANES), jnp.float32),
            pltpu.VMEM((2, LEV * SUB, LANES), jnp.float32),
            pltpu.VMEM((2, LEV * SUB, LANES), jnp.float32),
            pltpu.SemaphoreType.DMA(()),
        ],
        compiler_params=pltpu.CompilerParams(vmem_limit_bytes=12 * MIB),
        name="cloud",
    )(incoming, state, sums, advanced)
    returned = transfer(profiles)

    gcm_next, stats = pl.pallas_call(
        home_kernel,
        in_specs=[whole((COLS, LANES)), whole((2, DEVICES, COLS)), hbm],
        out_specs=(hbm, hbm),
        out_shape=(f32(GCM_ROWS, LANES), f32(4 * LEV, LANES)),
        scratch_shapes=[
            pltpu.VMEM((8 * LEV, LANES), jnp.float32),
            pltpu.SemaphoreType.DMA((2,)),
        ],
        input_output_aliases={2: 0},
        compiler_params=pltpu.CompilerParams(vmem_limit_bytes=8 * MIB),
        name="home",
    )(returned, routes, gcm_next)
    return gcm_next.reshape(gcm_state.shape), stats.reshape(2, LEV, 2, LANES)


def solution(mesh):
    grid = P(None, None, "blk", "sub")
    return jax.shard_map(
        body,
        mesh=mesh,
        in_specs=(grid, P(None, None, None, ("blk", "sub")), P("blk", "sub"), P("blk", "sub"), P()),
        out_specs=(grid, grid),
        check_vma=False,
    )
```

```python
import math

import jax
import jax.numpy as jnp
from jax import lax
from jax.experimental import pallas as pl
from jax.experimental.pallas import tpu as pltpu
from jax.sharding import PartitionSpec as P

SUBSTEPS = 4
LEV = 32
NXC = 64
LANES = 128
DEVICES = 128
COLS = 256
FIELDS = 6
SUB = 8
INNER = NXC // SUB
GCM_ROWS = FIELDS * LEV * 2
CRM_CHUNK = 8
ALPHA = 0.3 * math.log2(math.e)
BETA = 1.5 * ALPHA
SHIFT = math.log2(0.5 * BETA)
MIB = 1 << 20


def pieces(x):
    first = x.astype(jnp.bfloat16)
    rest = x - first.astype(jnp.float32)
    second = rest.astype(jnp.bfloat16)
    third = (rest - second.astype(jnp.float32)).astype(jnp.bfloat16)
    return first, second, third


def select_dot(x, chosen, dims, x_first):
    total = None
    for part in pieces(x):
        pair = (part, chosen) if x_first else (chosen, part)
        term = lax.dot_general(*pair, (dims, ((), ())), preferred_element_type=jnp.float32)
        total = term if total is None else total + term
    return total


def rows_of(ref, y):
    return ref[pl.ds(y, FIELDS * LEV, stride=2), :]


def edge_kernel(
    gcm_hbm, owner_hbm, branch_hbm, diffusion_hbm,
    gcm, to_core_mate, to_neighbour, to_chip_mate, to_other, routes, rates, number,
    owner, branch, diffusion, arrival,
):
    loads = [
        pltpu.make_async_copy(source, target, arrival.at[n])
        for n, (source, target) in enumerate(
            [(owner_hbm, owner), (branch_hbm, branch), (diffusion_hbm, diffusion), (gcm_hbm, gcm)]
        )
    ]
    for copy in loads:
        copy.start()
    to_chip_mate[...] = jnp.zeros_like(to_chip_mate)
    to_other[...] = jnp.zeros_like(to_other)
    for copy in loads[:3]:
        copy.wait()
    device = lax.broadcasted_iota(jnp.int32, (DEVICES, LANES), 0)
    target = jnp.concatenate(
        [(device == owner[y : y + 1, :]).astype(jnp.float32) for y in range(2)], axis=1
    )
    earlier = (
        lax.broadcasted_iota(jnp.int32, (COLS, COLS), 0)
        < lax.broadcasted_iota(jnp.int32, (COLS, COLS), 1)
    ).astype(jnp.bfloat16)
    count = jnp.dot(target.astype(jnp.bfloat16), earlier, preferred_element_type=jnp.float32)
    for slot in range(2):
        here = jnp.where(count < 0.5, 1.0 - slot, 0.0 + slot)
        routes[slot] = (target * here).astype(jnp.bfloat16)
    rates[...] = jnp.where(branch[...] == 1, 0.6, 0.2)
    for f in range(FIELDS):
        spread = jnp.broadcast_to(diffusion[f : f + 1, :], (LANES, LEV))
        number[f * LEV : (f + 1) * LEV, :] = jnp.transpose(spread)

    loads[3].wait()
    core = lax.rem(lax.axis_index("blk"), 2)
    to_core_mate[...] = rows_of(gcm, 1 - core)
    to_neighbour[: FIELDS * LEV, :] = rows_of(gcm, core)
    to_neighbour[FIELDS * LEV :, :] = jnp.zeros((SUB, LANES), jnp.float32)
    even = lax.rem(lax.axis_index("sub"), 2) == 0
    rows = jnp.concatenate([rows_of(gcm, 0), rows_of(gcm, 1)], axis=0)
    for part in range(GCM_ROWS // LANES):
        turned = jnp.transpose(rows[part * LANES : (part + 1) * LANES])
        first, last = turned[:1], turned[LANES - 1 :]
        to_chip_mate[part : part + 1, :] = jnp.where(even, last, first)
        to_other[part : part + 1, :] = jnp.where(even, first, last)


def early_kernel(crm_hbm, gcm, number, state, sums, partial, crm, arrival):
    loads = [
        pltpu.make_async_copy(
            crm_hbm.at[f, pl.ds(part * CRM_CHUNK, CRM_CHUNK)],
            crm.at[f, pl.ds(part * CRM_CHUNK, CRM_CHUNK)],
            arrival.at[f, part],
        )
        for f in range(2)
        for part in range(LEV // CRM_CHUNK)
    ]
    for copy in loads:
        copy.start()
    lane = lax.broadcasted_iota(jnp.int32, (FIELDS * LEV, LANES), 1)
    own = [rows_of(gcm, 0), rows_of(gcm, 1)]
    for y in range(2):
        before = jnp.where(lane == 0, 0.0, pltpu.roll(own[y], 1, axis=1))
        after = jnp.where(lane == LANES - 1, 0.0, pltpu.roll(own[y], LANES - 1, axis=1))
        around = own[1 - y] + after + before
        partial[y] = own[y] + number[...] * (around - 4.0 * own[y])

    for f, (scale, shift) in enumerate([(ALPHA, SHIFT), (BETA, 0.0)]):
        for part in range(LEV // CRM_CHUNK):
            loads[f * (LEV // CRM_CHUNK) + part].wait()

            def level(n, carry):
                k = part * CRM_CHUNK + n
                for half in range(2):
                    x = crm[f, k, :, half * LANES : (half + 1) * LANES].astype(jnp.float32)
                    x = x * scale + shift
                    total = None
                    for row in range(SUB):
                        block = x[row * INNER : (row + 1) * INNER]
                        state[f, half, pl.ds(k * NXC + row, INNER, stride=SUB), :] = block
                        total = block if total is None else total + block
                    sums[f, half, pl.ds(pl.multiple_of(k * SUB, SUB), SUB), :] = total
                return carry

            lax.fori_loop(0, CRM_CHUNK, level, 0, unroll=4)


def column_values(state, rate):
    level = lax.broadcasted_iota(jnp.int32, (LEV, LANES), 0)
    field = [state[f * LEV : (f + 1) * LEV] for f in range(FIELDS)]
    warm = ALPHA * (0.25 * field[0] + 0.2 * field[4])
    wet = BETA * (0.25 * field[1] + 0.2 * field[5])
    drift = 0.45 * jnp.tanh(field[2])
    tilt = jnp.tanh(field[3])
    rise = 0.15 * (tilt + pltpu.roll(tilt, LEV - 1, axis=0))
    rise = jnp.where(level == LEV - 1, rate, rise)
    return jnp.concatenate([warm, wet, drift, rise], axis=0)


def placed(values, routes, slot, y):
    route = routes[slot, :, pl.ds(pl.multiple_of(y * LANES, LANES), LANES)]
    return select_dot(values, route, ((1,), (1,)), False)


def inner_kernel(
    partial, number, core_mate, other, chip_mate, routes, rates, outer, done, advanced
):
    lane = lax.broadcasted_iota(jnp.int32, (FIELDS * LEV, LANES), 1)
    core = lax.rem(lax.axis_index("blk"), 2)

    def columns(ref):
        turned = jnp.transpose(ref)
        column = jnp.concatenate([turned[:, n : n + 1] for n in range(GCM_ROWS // LANES)], axis=0)
        return column[: FIELDS * LEV], column[FIELDS * LEV :]

    even = lax.rem(lax.axis_index("sub"), 2) == 0
    near, far = chip_mate[...], other[...]
    west, east = columns(jnp.where(even, far, near)), columns(jnp.where(even, near, far))
    rows = []
    for y in range(2):
        side = jnp.where(lane == 0, west[y], jnp.where(lane == LANES - 1, east[y], 0.0))
        rows.append(partial[y] + number[...] * side)
    outer[...] = jnp.where(core == 0, rows[0], rows[1])
    state = jnp.where(core == 0, rows[1], rows[0]) + number[...] * core_mate[...]
    advanced[...] = state[2 * LEV :]
    values = column_values(state, rates[pl.ds(1 - core, 1), :])
    for slot in range(2):
        done[slot] = placed(values, routes, slot, 1 - core)


def outer_kernel(
    outer, number, neighbour, routes, rates, done, inner_advanced, advanced, outgoing
):
    core = lax.rem(lax.axis_index("blk"), 2)
    state = outer[...] + number[...] * neighbour[: FIELDS * LEV, :]
    advanced[pl.ds(core, 4 * LEV, stride=2), :] = state[2 * LEV :]
    advanced[pl.ds(1 - core, 4 * LEV, stride=2), :] = inner_advanced[...]
    values = column_values(state, rates[pl.ds(core, 1), :])
    for slot in range(2):
        outgoing[pl.ds(slot, DEVICES, stride=2), :] = done[slot] + placed(
            values, routes, slot, core
        )


def cloud_kernel(
    incoming, start, sums, advanced, outgoing, gcm_next,
    state, coef, mean, total, square, departure,
):
    leaving = pltpu.make_async_copy(
        advanced, gcm_next.at[pl.ds(2 * 2 * LEV, 4 * 2 * LEV)], departure
    )
    leaving.start()
    level = lax.broadcasted_iota(jnp.int32, (LEV, LANES), 0)
    top = level == LEV - 1
    rates = []

    def up(x):
        return pltpu.roll(x, LEV - 1, axis=0)

    def down(x):
        return pltpu.roll(x, 1, axis=0)

    def folded(ref, *lead):
        out = None
        for part in range(SUB):
            x = ref[(*lead, pl.ds(part, LEV, stride=SUB), slice(None))]
            out = x if out is None else out + x
        return out

    for half in range(2):
        values = jnp.transpose(incoming[half * LANES : (half + 1) * LANES, :])
        rise = values[3 * LEV :]
        rates.append(rise[LEV - 1 :])
        rise = jnp.where(top, 0.0, rise)
        base = SHIFT * (1.0 - rise + down(rise))
        coef[0, half] = values[:LEV] + SHIFT - 0.75 * base
        coef[1, half] = values[LEV : 2 * LEV]
        coef[2, half] = values[2 * LEV : 3 * LEV]
        coef[3, half] = rise
        coef[7, half] = jnp.broadcast_to(rates[half], (LEV, LANES))
        for f in range(2):
            mean[f, half] = folded(sums, f, half) * (1.0 / NXC)

    def relax():
        for half in range(2):
            rise = coef[3, half]
            for f in range(2):
                now = mean[f, half]
                flux = rise * jnp.where(rise > 0.0, now, up(now))
                now = now - flux + down(flux)
                add = coef[f, half] - 0.25 * now
                coef[4 + f, half] = add
                mean[f, half] = now + add
                if f == 0:
                    coef[6, half] = now + add

    def settle():
        for half in range(2):
            rain = folded(total, half) * (1.0 / NXC)
            mean[0, half] = mean[0, half] + rain
            mean[1, half] = mean[1, half] - rain
            mean[2, half] = mean[2, half] + rain

    def sweep(source, half, last):
        rate = jnp.broadcast_to(coef[7, half, 0:1, :], (SUB, LANES))

        def row(index, k):
            return jnp.broadcast_to(coef[index, half, k : k + 1, :], (SUB, LANES))

        def drifted(f, k, size, positive):
            cells = [
                source[f, half, k * NXC + j * SUB : k * NXC + (j + 1) * SUB, :]
                for j in range(INNER)
            ]
            before = [pltpu.roll(cells[-1], 1, axis=0)] + cells[:-1]
            after = cells[1:] + [pltpu.roll(cells[0], SUB - 1, axis=0)]
            return [
                c + size * (jnp.where(positive, b, a) - c)
                for c, b, a in zip(cells, before, after)
            ]

        def level_of(k):
            drift = row(2, k)
            size, positive = jnp.abs(drift), drift > 0.0
            return [drifted(f, k, size, positive) for f in range(2)]

        now = level_of(0)
        below = None
        for k in range(LEV):
            add = [row(4, k), row(5, k)]
            if k < LEV - 1:
                after = level_of(k + 1)
                rise = row(3, k)
                upward = rise > 0.0
                flux = [
                    [rise * jnp.where(upward, a, b) for a, b in zip(now[f], after[f])]
                    for f in range(2)
                ]
            rained = None
            spread = None
            if last:
                middle = row(6, k)
            for j in range(INNER):
                new = []
                for f in range(2):
                    x = now[f][j]
                    if k < LEV - 1:
                        x = x - flux[f][j]
                    if k > 0:
                        x = x + below[f][j]
                    new.append(x + add[f])
                temper, moisture = new
                rain = rate * jnp.maximum(moisture - jnp.exp2(temper), 0.0)
                temper = temper + rain
                rained = rain if rained is None else rained + rain
                if last:
                    away = temper - middle
                    spread = away * away if spread is None else spread + away * away
                else:
                    at = slice(k * NXC + j * SUB, k * NXC + (j + 1) * SUB)
                    state[0, half, at, :] = temper
                    state[1, half, at, :] = moisture - rain
            total[half, k * SUB : (k + 1) * SUB, :] = rained
            if last:
                square[half, k * SUB : (k + 1) * SUB, :] = spread
            if k < LEV - 1:
                below, now = flux, after

    def substep(source, last):
        relax()

        def half_of(half, carry):
            sweep(source, half, last)
            return carry

        lax.fori_loop(0, 2, half_of, 0)
        if not last:
            settle()

    for half in range(2):
        mean[2, half] = jnp.zeros((LEV, LANES), jnp.float32)
    substep(start, False)

    def middle_step(step, carry):
        substep(state, False)
        return carry

    lax.fori_loop(0, SUBSTEPS - 2, middle_step, 0)
    substep(state, True)
    settle()
    for half in range(2):
        warm, wet, rain = mean[0, half], mean[1, half], mean[2, half]
        gap = warm - coef[6, half]
        spread = folded(square, half) * (1.0 / NXC) - gap * gap
        result = [
            (warm - SHIFT) * (1.0 / ALPHA),
            wet * (1.0 / BETA),
            rain * (1.0 / BETA),
            spread * (1.0 / (ALPHA * ALPHA)),
        ]
        outgoing[half * LANES : (half + 1) * LANES, :] = jnp.transpose(
            jnp.concatenate(result, axis=0)
        )
    leaving.wait()


def home_kernel(returned, routes, begun, gcm_next, stats):
    del begun
    home = None
    for slot in range(2):
        back = returned[pl.ds(slot, DEVICES, stride=2), :]
        term = select_dot(jnp.transpose(back), routes[slot], ((1,), (0,)), True)
        home = term if home is None else home + term
    for y in range(2):
        part = home[:, y * LANES : (y + 1) * LANES]
        gcm_next[pl.ds(y, 2 * LEV, stride=2), :] = part[: 2 * LEV]
        stats[pl.ds(y, 2 * LEV, stride=2), :] = part[2 * LEV :]


def whole(shape):
    return pl.BlockSpec(shape, lambda *_: (0,) * len(shape))


def f32(*shape):
    return jax.ShapeDtypeStruct(shape, jnp.float32)


def in_hbm(x):
    return pltpu.with_memory_space_constraint(x, pltpu.HBM)


def transfer(rows):
    moved = lax.all_to_all(
        rows.reshape(DEVICES, 2, LANES), ("blk", "sub"), split_axis=0, concat_axis=0, tiled=True
    )
    return moved.reshape(COLS, LANES)


def body(gcm_state, crm_state, owner, branch, diffusion):
    gcm = gcm_state.reshape(GCM_ROWS, LANES)

    def pairs(n, first):
        ahead = [(i, (i + 1) % n) for i in range(first, n, 2)]
        return ahead + [(j, i) for i, j in ahead]

    n_blk, n_sub = lax.axis_size("blk"), lax.axis_size("sub")
    hbm = pl.BlockSpec(memory_space=pltpu.HBM)
    gcm_here, to_core_mate, to_neighbour, to_chip_mate, to_other, routes, rates, number = pl.pallas_call(
        edge_kernel,
        in_specs=[hbm] * 4,
        out_shape=(
            f32(GCM_ROWS, LANES),
            f32(FIELDS * LEV, LANES),
            f32(FIELDS * LEV + SUB, LANES),
            f32(SUB, LANES),
            f32(SUB, LANES),
            jax.ShapeDtypeStruct((2, DEVICES, COLS), jnp.bfloat16),
            f32(2, LANES),
            f32(FIELDS * LEV, LANES),
        ),
        scratch_shapes=[
            pltpu.VMEM((2, LANES), jnp.int32),
            pltpu.VMEM((2, LANES), jnp.int32),
            pltpu.VMEM((FIELDS, LEV), jnp.float32),
            pltpu.SemaphoreType.DMA((4,)),
        ],
        compiler_params=pltpu.CompilerParams(vmem_limit_bytes=4 * MIB),
        name="edges",
    )(*map(in_hbm, (gcm, owner, branch, diffusion)))
    neighbour = lax.ppermute(to_neighbour, "blk", pairs(n_blk, 1))
    core_mate = lax.ppermute(to_core_mate, "blk", pairs(n_blk, 0))
    chip_mate = lax.ppermute(to_chip_mate, "sub", pairs(n_sub, 0))
    other = lax.ppermute(to_other, "sub", pairs(n_sub, 1))
    cells = 2 * LEV * NXC * COLS
    state, sums, partial = pl.pallas_call(
        early_kernel,
        in_specs=[hbm, whole((GCM_ROWS, LANES)), whole((FIELDS * LEV, LANES))],
        out_shape=(
            f32(2, 2, LEV * NXC, LANES),
            f32(2, 2, LEV * SUB, LANES),
            f32(2, FIELDS * LEV, LANES),
        ),
        scratch_shapes=[
            pltpu.VMEM((2, LEV, NXC, COLS), jnp.bfloat16),
            pltpu.SemaphoreType.DMA((2, LEV // CRM_CHUNK)),
        ],
        compiler_params=pltpu.CompilerParams(vmem_limit_bytes=16 * MIB),
        cost_estimate=pl.CostEstimate(flops=4 * cells, bytes_accessed=6 * cells, transcendentals=0),
        name="early",
    )(in_hbm(crm_state), gcm_here, number)
    outer, done, inner_advanced = pl.pallas_call(
        inner_kernel,
        out_shape=(
            f32(FIELDS * LEV, LANES),
            f32(2, DEVICES, LANES),
            f32(4 * LEV, LANES),
        ),
        compiler_params=pltpu.CompilerParams(vmem_limit_bytes=8 * MIB),
        name="inner",
    )(partial, number, core_mate, other, chip_mate, routes, rates)
    advanced, outgoing = pl.pallas_call(
        outer_kernel,
        out_shape=(f32(4 * 2 * LEV, LANES), f32(COLS, LANES)),
        compiler_params=pltpu.CompilerParams(vmem_limit_bytes=8 * MIB),
        name="outer",
    )(outer, number, neighbour, routes, rates, done, inner_advanced)

    incoming = transfer(outgoing)
    profiles, gcm_next = pl.pallas_call(
        cloud_kernel,
        out_specs=(whole((COLS, LANES)), hbm),
        out_shape=(f32(COLS, LANES), f32(GCM_ROWS, LANES)),
        scratch_shapes=[
            pltpu.VMEM((2, 2, LEV * NXC, LANES), jnp.float32),
            pltpu.VMEM((8, 2, LEV, LANES), jnp.float32),
            pltpu.VMEM((3, 2, LEV, LANES), jnp.float32),
            pltpu.VMEM((2, LEV * SUB, LANES), jnp.float32),
            pltpu.VMEM((2, LEV * SUB, LANES), jnp.float32),
            pltpu.SemaphoreType.DMA(()),
        ],
        compiler_params=pltpu.CompilerParams(vmem_limit_bytes=12 * MIB),
        name="cloud",
    )(incoming, state, sums, advanced)
    returned = transfer(profiles)

    gcm_next, stats = pl.pallas_call(
        home_kernel,
        grid=(1,),
        in_specs=[
            whole((COLS, LANES)),
            whole((2, DEVICES, COLS)),
            pl.BlockSpec(memory_space=pl.ANY),
        ],
        out_specs=(whole((4 * LEV, LANES)), whole((4 * LEV, LANES))),
        out_shape=(f32(GCM_ROWS, LANES), f32(4 * LEV, LANES)),
        input_output_aliases={2: 0},
        compiler_params=pltpu.CompilerParams(vmem_limit_bytes=8 * MIB),
        name="home",
    )(returned, routes, gcm_next)
    return gcm_next.reshape(gcm_state.shape), stats.reshape(2, LEV, 2, LANES)


def solution(mesh):
    grid = P(None, None, "blk", "sub")
    return jax.shard_map(
        body,
        mesh=mesh,
        in_specs=(grid, P(None, None, None, ("blk", "sub")), P("blk", "sub"), P("blk", "sub"), P()),
        out_specs=(grid, grid),
        check_vma=False,
    )
```

```python
import math

import jax
import jax.numpy as jnp
from jax import lax
from jax.experimental import pallas as pl
from jax.experimental.pallas import tpu as pltpu
from jax.sharding import PartitionSpec as P

SUBSTEPS = 4
LEV = 32
NXC = 64
LANES = 128
DEVICES = 128
COLS = 256
FIELDS = 6
SUB = 8
INNER = NXC // SUB
GCM_ROWS = FIELDS * LEV * 2
CRM_CHUNK = 8
ALPHA = 0.3 * math.log2(math.e)
BETA = 1.5 * ALPHA
SHIFT = math.log2(0.5 * BETA)
MIB = 1 << 20


def pieces(x):
    first = x.astype(jnp.bfloat16)
    rest = x - first.astype(jnp.float32)
    second = rest.astype(jnp.bfloat16)
    third = (rest - second.astype(jnp.float32)).astype(jnp.bfloat16)
    return first, second, third


def select_dot(x, chosen, dims, x_first):
    total = None
    for part in pieces(x):
        pair = (part, chosen) if x_first else (chosen, part)
        term = lax.dot_general(*pair, (dims, ((), ())), preferred_element_type=jnp.float32)
        total = term if total is None else total + term
    return total


def rows_of(ref, y):
    return ref[pl.ds(y, FIELDS * LEV, stride=2), :]


def load_kernel(
    gcm_hbm, owner_hbm, branch_hbm, diffusion_hbm,
    gcm, to_core_mate, to_neighbour, owner, branch, diffusion, arrival,
):
    loads = [
        pltpu.make_async_copy(source, target, arrival.at[n])
        for n, (source, target) in enumerate(
            [(gcm_hbm, gcm), (owner_hbm, owner), (branch_hbm, branch), (diffusion_hbm, diffusion)]
        )
    ]
    for copy in loads:
        copy.start()
    for copy in loads:
        copy.wait()
    core = lax.rem(lax.axis_index("blk"), 2)
    to_core_mate[...] = rows_of(gcm, 1 - core)
    to_neighbour[: FIELDS * LEV, :] = rows_of(gcm, core)
    to_neighbour[FIELDS * LEV :, :] = jnp.zeros((SUB, LANES), jnp.float32)


def edge_kernel(
    gcm, owner, branch, diffusion, to_chip_mate, to_other, routes, rates, number
):
    to_chip_mate[...] = jnp.zeros_like(to_chip_mate)
    to_other[...] = jnp.zeros_like(to_other)
    device = lax.broadcasted_iota(jnp.int32, (DEVICES, LANES), 0)
    target = jnp.concatenate(
        [(device == owner[y : y + 1, :]).astype(jnp.float32) for y in range(2)], axis=1
    )
    earlier = (
        lax.broadcasted_iota(jnp.int32, (COLS, COLS), 0)
        < lax.broadcasted_iota(jnp.int32, (COLS, COLS), 1)
    ).astype(jnp.bfloat16)
    count = jnp.dot(target.astype(jnp.bfloat16), earlier, preferred_element_type=jnp.float32)
    for slot in range(2):
        here = jnp.where(count < 0.5, 1.0 - slot, 0.0 + slot)
        routes[slot] = (target * here).astype(jnp.bfloat16)
    rates[...] = jnp.where(branch[...] == 1, 0.6, 0.2)
    for f in range(FIELDS):
        spread = jnp.broadcast_to(diffusion[f : f + 1, :], (LANES, LEV))
        number[f * LEV : (f + 1) * LEV, :] = jnp.transpose(spread)

    even = lax.rem(lax.axis_index("sub"), 2) == 0
    rows = jnp.concatenate([rows_of(gcm, 0), rows_of(gcm, 1)], axis=0)
    for part in range(GCM_ROWS // LANES):
        turned = jnp.transpose(rows[part * LANES : (part + 1) * LANES])
        first, last = turned[:1], turned[LANES - 1 :]
        to_chip_mate[part : part + 1, :] = jnp.where(even, last, first)
        to_other[part : part + 1, :] = jnp.where(even, first, last)


def early_kernel(crm_hbm, gcm, number, state, sums, partial, crm, arrival):
    loads = [
        pltpu.make_async_copy(
            crm_hbm.at[f, pl.ds(part * CRM_CHUNK, CRM_CHUNK)],
            crm.at[f, pl.ds(part * CRM_CHUNK, CRM_CHUNK)],
            arrival.at[f, part],
        )
        for f in range(2)
        for part in range(LEV // CRM_CHUNK)
    ]
    for copy in loads:
        copy.start()
    lane = lax.broadcasted_iota(jnp.int32, (FIELDS * LEV, LANES), 1)
    own = [rows_of(gcm, 0), rows_of(gcm, 1)]
    for y in range(2):
        before = jnp.where(lane == 0, 0.0, pltpu.roll(own[y], 1, axis=1))
        after = jnp.where(lane == LANES - 1, 0.0, pltpu.roll(own[y], LANES - 1, axis=1))
        around = own[1 - y] + after + before
        partial[y] = own[y] + number[...] * (around - 4.0 * own[y])

    for f, (scale, shift) in enumerate([(ALPHA, SHIFT), (BETA, 0.0)]):
        for part in range(LEV // CRM_CHUNK):
            loads[f * (LEV // CRM_CHUNK) + part].wait()

            def level(n, carry):
                k = part * CRM_CHUNK + n
                for half in range(2):
                    x = crm[f, k, :, half * LANES : (half + 1) * LANES].astype(jnp.float32)
                    x = x * scale + shift
                    total = None
                    for row in range(SUB):
                        block = x[row * INNER : (row + 1) * INNER]
                        state[f, half, pl.ds(k * NXC + row, INNER, stride=SUB), :] = block
                        total = block if total is None else total + block
                    sums[f, half, pl.ds(pl.multiple_of(k * SUB, SUB), SUB), :] = total
                return carry

            lax.fori_loop(0, CRM_CHUNK, level, 0, unroll=4)


def column_values(state, rate):
    level = lax.broadcasted_iota(jnp.int32, (LEV, LANES), 0)
    field = [state[f * LEV : (f + 1) * LEV] for f in range(FIELDS)]
    warm = ALPHA * (0.25 * field[0] + 0.2 * field[4])
    wet = BETA * (0.25 * field[1] + 0.2 * field[5])
    drift = 0.45 * jnp.tanh(field[2])
    tilt = jnp.tanh(field[3])
    rise = 0.15 * (tilt + pltpu.roll(tilt, LEV - 1, axis=0))
    rise = jnp.where(level == LEV - 1, rate, rise)
    return jnp.concatenate([warm, wet, drift, rise], axis=0)


def placed(values, routes, slot, y):
    route = routes[slot, :, pl.ds(pl.multiple_of(y * LANES, LANES), LANES)]
    return select_dot(values, route, ((1,), (1,)), False)


def inner_kernel(
    partial, number, core_mate, other, chip_mate, routes, rates, outer, done, advanced
):
    lane = lax.broadcasted_iota(jnp.int32, (FIELDS * LEV, LANES), 1)
    core = lax.rem(lax.axis_index("blk"), 2)

    def columns(ref):
        turned = jnp.transpose(ref)
        column = jnp.concatenate([turned[:, n : n + 1] for n in range(GCM_ROWS // LANES)], axis=0)
        return column[: FIELDS * LEV], column[FIELDS * LEV :]

    even = lax.rem(lax.axis_index("sub"), 2) == 0
    near, far = chip_mate[...], other[...]
    west, east = columns(jnp.where(even, far, near)), columns(jnp.where(even, near, far))
    rows = []
    for y in range(2):
        side = jnp.where(lane == 0, west[y], jnp.where(lane == LANES - 1, east[y], 0.0))
        rows.append(partial[y] + number[...] * side)
    outer[...] = jnp.where(core == 0, rows[0], rows[1])
    state = jnp.where(core == 0, rows[1], rows[0]) + number[...] * core_mate[...]
    advanced[...] = state[2 * LEV :]
    values = column_values(state, rates[pl.ds(1 - core, 1), :])
    for slot in range(2):
        done[slot] = placed(values, routes, slot, 1 - core)


def outer_kernel(
    outer, number, neighbour, routes, rates, done, inner_advanced, advanced, outgoing
):
    core = lax.rem(lax.axis_index("blk"), 2)
    state = outer[...] + number[...] * neighbour[: FIELDS * LEV, :]
    advanced[pl.ds(core, 4 * LEV, stride=2), :] = state[2 * LEV :]
    advanced[pl.ds(1 - core, 4 * LEV, stride=2), :] = inner_advanced[...]
    values = column_values(state, rates[pl.ds(core, 1), :])
    for slot in range(2):
        outgoing[pl.ds(slot, DEVICES, stride=2), :] = done[slot] + placed(
            values, routes, slot, core
        )


def cloud_kernel(
    incoming, start, sums, advanced, outgoing, gcm_next,
    state, coef, mean, total, square, departure,
):
    leaving = pltpu.make_async_copy(
        advanced, gcm_next.at[pl.ds(2 * 2 * LEV, 4 * 2 * LEV)], departure
    )
    leaving.start()
    level = lax.broadcasted_iota(jnp.int32, (LEV, LANES), 0)
    top = level == LEV - 1
    rates = []

    def up(x):
        return pltpu.roll(x, LEV - 1, axis=0)

    def down(x):
        return pltpu.roll(x, 1, axis=0)

    def folded(ref, *lead):
        out = None
        for part in range(SUB):
            x = ref[(*lead, pl.ds(part, LEV, stride=SUB), slice(None))]
            out = x if out is None else out + x
        return out

    for half in range(2):
        values = jnp.transpose(incoming[half * LANES : (half + 1) * LANES, :])
        rise = values[3 * LEV :]
        rates.append(rise[LEV - 1 :])
        rise = jnp.where(top, 0.0, rise)
        base = SHIFT * (1.0 - rise + down(rise))
        coef[0, half] = values[:LEV] + SHIFT - 0.75 * base
        coef[1, half] = values[LEV : 2 * LEV]
        coef[2, half] = values[2 * LEV : 3 * LEV]
        coef[3, half] = rise
        coef[7, half] = jnp.broadcast_to(rates[half], (LEV, LANES))
        for f in range(2):
            mean[f, half] = folded(sums, f, half) * (1.0 / NXC)

    def relax():
        for half in range(2):
            rise = coef[3, half]
            for f in range(2):
                now = mean[f, half]
                flux = rise * jnp.where(rise > 0.0, now, up(now))
                now = now - flux + down(flux)
                add = coef[f, half] - 0.25 * now
                coef[4 + f, half] = add
                mean[f, half] = now + add
                if f == 0:
                    coef[6, half] = now + add

    def settle():
        for half in range(2):
            rain = folded(total, half) * (1.0 / NXC)
            mean[0, half] = mean[0, half] + rain
            mean[1, half] = mean[1, half] - rain
            mean[2, half] = mean[2, half] + rain

    def sweep(source, half, last):
        rate = jnp.broadcast_to(coef[7, half, 0:1, :], (SUB, LANES))

        def row(index, k):
            return jnp.broadcast_to(coef[index, half, k : k + 1, :], (SUB, LANES))

        def drifted(f, k, size, positive):
            cells = [
                source[f, half, k * NXC + j * SUB : k * NXC + (j + 1) * SUB, :]
                for j in range(INNER)
            ]
            before = [pltpu.roll(cells[-1], 1, axis=0)] + cells[:-1]
            after = cells[1:] + [pltpu.roll(cells[0], SUB - 1, axis=0)]
            return [
                c + size * (jnp.where(positive, b, a) - c)
                for c, b, a in zip(cells, before, after)
            ]

        def level_of(k):
            drift = row(2, k)
            size, positive = jnp.abs(drift), drift > 0.0
            return [drifted(f, k, size, positive) for f in range(2)]

        now = level_of(0)
        below = None
        for k in range(LEV):
            add = [row(4, k), row(5, k)]
            if k < LEV - 1:
                after = level_of(k + 1)
                rise = row(3, k)
                upward = rise > 0.0
                flux = [
                    [rise * jnp.where(upward, a, b) for a, b in zip(now[f], after[f])]
                    for f in range(2)
                ]
            rained = None
            spread = None
            if last:
                middle = row(6, k)
            for j in range(INNER):
                new = []
                for f in range(2):
                    x = now[f][j]
                    if k < LEV - 1:
                        x = x - flux[f][j]
                    if k > 0:
                        x = x + below[f][j]
                    new.append(x + add[f])
                temper, moisture = new
                rain = rate * jnp.maximum(moisture - jnp.exp2(temper), 0.0)
                temper = temper + rain
                rained = rain if rained is None else rained + rain
                if last:
                    away = temper - middle
                    spread = away * away if spread is None else spread + away * away
                else:
                    at = slice(k * NXC + j * SUB, k * NXC + (j + 1) * SUB)
                    state[0, half, at, :] = temper
                    state[1, half, at, :] = moisture - rain
            total[half, k * SUB : (k + 1) * SUB, :] = rained
            if last:
                square[half, k * SUB : (k + 1) * SUB, :] = spread
            if k < LEV - 1:
                below, now = flux, after

    def substep(source, last):
        relax()

        def half_of(half, carry):
            sweep(source, half, last)
            return carry

        lax.fori_loop(0, 2, half_of, 0)
        if not last:
            settle()

    for half in range(2):
        mean[2, half] = jnp.zeros((LEV, LANES), jnp.float32)
    substep(start, False)

    def middle_step(step, carry):
        substep(state, False)
        return carry

    lax.fori_loop(0, SUBSTEPS - 2, middle_step, 0)
    substep(state, True)
    settle()
    for half in range(2):
        warm, wet, rain = mean[0, half], mean[1, half], mean[2, half]
        gap = warm - coef[6, half]
        spread = folded(square, half) * (1.0 / NXC) - gap * gap
        result = [
            (warm - SHIFT) * (1.0 / ALPHA),
            wet * (1.0 / BETA),
            rain * (1.0 / BETA),
            spread * (1.0 / (ALPHA * ALPHA)),
        ]
        outgoing[half * LANES : (half + 1) * LANES, :] = jnp.transpose(
            jnp.concatenate(result, axis=0)
        )
    leaving.wait()


def home_kernel(returned, routes, begun, gcm_next, stats):
    del begun
    home = None
    for slot in range(2):
        back = returned[pl.ds(slot, DEVICES, stride=2), :]
        term = select_dot(jnp.transpose(back), routes[slot], ((1,), (0,)), True)
        home = term if home is None else home + term
    for y in range(2):
        part = home[:, y * LANES : (y + 1) * LANES]
        gcm_next[pl.ds(y, 2 * LEV, stride=2), :] = part[: 2 * LEV]
        stats[pl.ds(y, 2 * LEV, stride=2), :] = part[2 * LEV :]


def whole(shape):
    return pl.BlockSpec(shape, lambda *_: (0,) * len(shape))


def f32(*shape):
    return jax.ShapeDtypeStruct(shape, jnp.float32)


def in_hbm(x):
    return pltpu.with_memory_space_constraint(x, pltpu.HBM)


def transfer(rows):
    moved = lax.all_to_all(
        rows.reshape(DEVICES, 2, LANES), ("blk", "sub"), split_axis=0, concat_axis=0, tiled=True
    )
    return moved.reshape(COLS, LANES)


def body(gcm_state, crm_state, owner, branch, diffusion):
    gcm = gcm_state.reshape(GCM_ROWS, LANES)

    def pairs(n, first):
        ahead = [(i, (i + 1) % n) for i in range(first, n, 2)]
        return ahead + [(j, i) for i, j in ahead]

    n_blk, n_sub = lax.axis_size("blk"), lax.axis_size("sub")
    hbm = pl.BlockSpec(memory_space=pltpu.HBM)
    gcm_here, to_core_mate, to_neighbour, owner_here, branch_here, diffusion_here = pl.pallas_call(
        load_kernel,
        in_specs=[hbm] * 4,
        out_shape=(
            f32(GCM_ROWS, LANES),
            f32(FIELDS * LEV, LANES),
            f32(FIELDS * LEV + SUB, LANES),
            jax.ShapeDtypeStruct(owner.shape, owner.dtype),
            jax.ShapeDtypeStruct(branch.shape, branch.dtype),
            f32(*diffusion.shape),
        ),
        scratch_shapes=[pltpu.SemaphoreType.DMA((4,))],
        compiler_params=pltpu.CompilerParams(vmem_limit_bytes=4 * MIB),
        name="load",
    )(*map(in_hbm, (gcm, owner, branch, diffusion)))
    neighbour = lax.ppermute(to_neighbour, "blk", pairs(n_blk, 1))
    core_mate = lax.ppermute(to_core_mate, "blk", pairs(n_blk, 0))
    to_chip_mate, to_other, routes, rates, number = pl.pallas_call(
        edge_kernel,
        out_shape=(
            f32(SUB, LANES),
            f32(SUB, LANES),
            jax.ShapeDtypeStruct((2, DEVICES, COLS), jnp.bfloat16),
            f32(2, LANES),
            f32(FIELDS * LEV, LANES),
        ),
        compiler_params=pltpu.CompilerParams(vmem_limit_bytes=4 * MIB),
        name="edges",
    )(gcm_here, owner_here, branch_here, diffusion_here)
    chip_mate = lax.ppermute(to_chip_mate, "sub", pairs(n_sub, 0))
    other = lax.ppermute(to_other, "sub", pairs(n_sub, 1))
    cells = 2 * LEV * NXC * COLS
    state, sums, partial = pl.pallas_call(
        early_kernel,
        in_specs=[hbm, whole((GCM_ROWS, LANES)), whole((FIELDS * LEV, LANES))],
        out_shape=(
            f32(2, 2, LEV * NXC, LANES),
            f32(2, 2, LEV * SUB, LANES),
            f32(2, FIELDS * LEV, LANES),
        ),
        scratch_shapes=[
            pltpu.VMEM((2, LEV, NXC, COLS), jnp.bfloat16),
            pltpu.SemaphoreType.DMA((2, LEV // CRM_CHUNK)),
        ],
        compiler_params=pltpu.CompilerParams(vmem_limit_bytes=16 * MIB),
        cost_estimate=pl.CostEstimate(flops=4 * cells, bytes_accessed=6 * cells, transcendentals=0),
        name="early",
    )(in_hbm(crm_state), gcm_here, number)
    outer, done, inner_advanced = pl.pallas_call(
        inner_kernel,
        out_shape=(
            f32(FIELDS * LEV, LANES),
            f32(2, DEVICES, LANES),
            f32(4 * LEV, LANES),
        ),
        compiler_params=pltpu.CompilerParams(vmem_limit_bytes=8 * MIB),
        name="inner",
    )(partial, number, core_mate, other, chip_mate, routes, rates)
    advanced, outgoing = pl.pallas_call(
        outer_kernel,
        out_shape=(f32(4 * 2 * LEV, LANES), f32(COLS, LANES)),
        compiler_params=pltpu.CompilerParams(vmem_limit_bytes=8 * MIB),
        name="outer",
    )(outer, number, neighbour, routes, rates, done, inner_advanced)

    incoming = transfer(outgoing)
    profiles, gcm_next = pl.pallas_call(
        cloud_kernel,
        out_specs=(whole((COLS, LANES)), hbm),
        out_shape=(f32(COLS, LANES), f32(GCM_ROWS, LANES)),
        scratch_shapes=[
            pltpu.VMEM((2, 2, LEV * NXC, LANES), jnp.float32),
            pltpu.VMEM((8, 2, LEV, LANES), jnp.float32),
            pltpu.VMEM((3, 2, LEV, LANES), jnp.float32),
            pltpu.VMEM((2, LEV * SUB, LANES), jnp.float32),
            pltpu.VMEM((2, LEV * SUB, LANES), jnp.float32),
            pltpu.SemaphoreType.DMA(()),
        ],
        compiler_params=pltpu.CompilerParams(vmem_limit_bytes=12 * MIB),
        name="cloud",
    )(incoming, state, sums, advanced)
    returned = transfer(profiles)

    gcm_next, stats = pl.pallas_call(
        home_kernel,
        grid=(1,),
        in_specs=[
            whole((COLS, LANES)),
            whole((2, DEVICES, COLS)),
            pl.BlockSpec(memory_space=pl.ANY),
        ],
        out_specs=(whole((4 * LEV, LANES)), whole((4 * LEV, LANES))),
        out_shape=(f32(GCM_ROWS, LANES), f32(4 * LEV, LANES)),
        input_output_aliases={2: 0},
        compiler_params=pltpu.CompilerParams(vmem_limit_bytes=8 * MIB),
        name="home",
    )(returned, routes, gcm_next)
    return gcm_next.reshape(gcm_state.shape), stats.reshape(2, LEV, 2, LANES)


def solution(mesh):
    grid = P(None, None, "blk", "sub")
    return jax.shard_map(
        body,
        mesh=mesh,
        in_specs=(grid, P(None, None, None, ("blk", "sub")), P("blk", "sub"), P("blk", "sub"), P()),
        out_specs=(grid, grid),
        check_vma=False,
    )
```

```python
import math

import jax
import jax.numpy as jnp
from jax import lax
from jax.experimental import pallas as pl
from jax.experimental.pallas import tpu as pltpu
from jax.sharding import PartitionSpec as P

SUBSTEPS = 4
LEV = 32
NXC = 64
LANES = 128
DEVICES = 128
COLS = 256
FIELDS = 6
SUB = 8
INNER = NXC // SUB
GCM_ROWS = FIELDS * LEV * 2
CRM_CHUNK = 8
ALPHA = 0.3 * math.log2(math.e)
BETA = 1.5 * ALPHA
SHIFT = math.log2(0.5 * BETA)
MIB = 1 << 20


def pieces(x):
    first = x.astype(jnp.bfloat16)
    rest = x - first.astype(jnp.float32)
    second = rest.astype(jnp.bfloat16)
    third = (rest - second.astype(jnp.float32)).astype(jnp.bfloat16)
    return first, second, third


def select_dot(x, chosen, dims, x_first):
    total = None
    for part in pieces(x):
        pair = (part, chosen) if x_first else (chosen, part)
        term = lax.dot_general(*pair, (dims, ((), ())), preferred_element_type=jnp.float32)
        total = term if total is None else total + term
    return total


def rows_of(ref, y):
    return ref[pl.ds(y, FIELDS * LEV, stride=2), :]


def load_kernel(
    gcm_hbm, owner_hbm, branch_hbm, diffusion_hbm,
    gcm, to_core_mate, to_neighbour, owner, branch, diffusion, arrival,
):
    loads = [
        pltpu.make_async_copy(source, target, arrival.at[n])
        for n, (source, target) in enumerate(
            [(gcm_hbm, gcm), (owner_hbm, owner), (branch_hbm, branch), (diffusion_hbm, diffusion)]
        )
    ]
    for copy in loads:
        copy.start()
    for copy in loads:
        copy.wait()
    core = lax.rem(lax.axis_index("blk"), 2)
    rows = [rows_of(gcm, 0), rows_of(gcm, 1)]
    to_core_mate[...] = jnp.where(core == 0, rows[1], rows[0])
    to_neighbour[: FIELDS * LEV, :] = jnp.where(core == 0, rows[0], rows[1])
    to_neighbour[FIELDS * LEV :, :] = jnp.zeros((SUB, LANES), jnp.float32)


def edge_kernel(
    gcm, owner, branch, diffusion, to_chip_mate, to_other, routes, rates, number
):
    to_chip_mate[...] = jnp.zeros_like(to_chip_mate)
    to_other[...] = jnp.zeros_like(to_other)
    device = lax.broadcasted_iota(jnp.int32, (DEVICES, LANES), 0)
    target = jnp.concatenate(
        [(device == owner[y : y + 1, :]).astype(jnp.float32) for y in range(2)], axis=1
    )
    earlier = (
        lax.broadcasted_iota(jnp.int32, (COLS, COLS), 0)
        < lax.broadcasted_iota(jnp.int32, (COLS, COLS), 1)
    ).astype(jnp.bfloat16)
    count = jnp.dot(target.astype(jnp.bfloat16), earlier, preferred_element_type=jnp.float32)
    for slot in range(2):
        here = jnp.where(count < 0.5, 1.0 - slot, 0.0 + slot)
        routes[slot] = (target * here).astype(jnp.bfloat16)
    rates[...] = jnp.where(branch[...] == 1, 0.6, 0.2)
    for f in range(FIELDS):
        spread = jnp.broadcast_to(diffusion[f : f + 1, :], (LANES, LEV))
        number[f * LEV : (f + 1) * LEV, :] = jnp.transpose(spread)

    even = lax.rem(lax.axis_index("sub"), 2) == 0
    rows = jnp.concatenate([rows_of(gcm, 0), rows_of(gcm, 1)], axis=0)
    for part in range(GCM_ROWS // LANES):
        turned = jnp.transpose(rows[part * LANES : (part + 1) * LANES])
        first, last = turned[:1], turned[LANES - 1 :]
        to_chip_mate[part : part + 1, :] = jnp.where(even, last, first)
        to_other[part : part + 1, :] = jnp.where(even, first, last)


def early_kernel(crm_hbm, gcm, number, state, sums, partial, crm, arrival):
    loads = [
        pltpu.make_async_copy(
            crm_hbm.at[f, pl.ds(part * CRM_CHUNK, CRM_CHUNK)],
            crm.at[f, pl.ds(part * CRM_CHUNK, CRM_CHUNK)],
            arrival.at[f, part],
        )
        for f in range(2)
        for part in range(LEV // CRM_CHUNK)
    ]
    for copy in loads:
        copy.start()
    lane = lax.broadcasted_iota(jnp.int32, (FIELDS * LEV, LANES), 1)
    own = [rows_of(gcm, 0), rows_of(gcm, 1)]
    for y in range(2):
        before = jnp.where(lane == 0, 0.0, pltpu.roll(own[y], 1, axis=1))
        after = jnp.where(lane == LANES - 1, 0.0, pltpu.roll(own[y], LANES - 1, axis=1))
        around = own[1 - y] + after + before
        partial[y] = own[y] + number[...] * (around - 4.0 * own[y])

    for f, (scale, shift) in enumerate([(ALPHA, SHIFT), (BETA, 0.0)]):
        for part in range(LEV // CRM_CHUNK):
            loads[f * (LEV // CRM_CHUNK) + part].wait()

            def level(n, carry):
                k = part * CRM_CHUNK + n
                for half in range(2):
                    x = crm[f, k, :, half * LANES : (half + 1) * LANES].astype(jnp.float32)
                    x = x * scale + shift
                    total = None
                    for row in range(SUB):
                        block = x[row * INNER : (row + 1) * INNER]
                        state[f, half, pl.ds(k * NXC + row, INNER, stride=SUB), :] = block
                        total = block if total is None else total + block
                    sums[f, half, pl.ds(pl.multiple_of(k * SUB, SUB), SUB), :] = total
                return carry

            lax.fori_loop(0, CRM_CHUNK, level, 0, unroll=4)


def column_values(state, rate):
    level = lax.broadcasted_iota(jnp.int32, (LEV, LANES), 0)
    field = [state[f * LEV : (f + 1) * LEV] for f in range(FIELDS)]
    warm = ALPHA * (0.25 * field[0] + 0.2 * field[4])
    wet = BETA * (0.25 * field[1] + 0.2 * field[5])
    drift = 0.45 * jnp.tanh(field[2])
    tilt = jnp.tanh(field[3])
    rise = 0.15 * (tilt + pltpu.roll(tilt, LEV - 1, axis=0))
    rise = jnp.where(level == LEV - 1, rate, rise)
    return jnp.concatenate([warm, wet, drift, rise], axis=0)


def placed(values, routes, slot, y):
    route = routes[slot, :, pl.ds(pl.multiple_of(y * LANES, LANES), LANES)]
    return select_dot(values, route, ((1,), (1,)), False)


def inner_kernel(
    partial, number, core_mate, other, chip_mate, routes, rates, outer, done, advanced
):
    lane = lax.broadcasted_iota(jnp.int32, (FIELDS * LEV, LANES), 1)
    core = lax.rem(lax.axis_index("blk"), 2)

    def columns(ref):
        turned = jnp.transpose(ref)
        column = jnp.concatenate([turned[:, n : n + 1] for n in range(GCM_ROWS // LANES)], axis=0)
        return column[: FIELDS * LEV], column[FIELDS * LEV :]

    even = lax.rem(lax.axis_index("sub"), 2) == 0
    near, far = chip_mate[...], other[...]
    west, east = columns(jnp.where(even, far, near)), columns(jnp.where(even, near, far))
    rows = []
    for y in range(2):
        side = jnp.where(lane == 0, west[y], jnp.where(lane == LANES - 1, east[y], 0.0))
        rows.append(partial[y] + number[...] * side)
    outer[...] = jnp.where(core == 0, rows[0], rows[1])
    state = jnp.where(core == 0, rows[1], rows[0]) + number[...] * core_mate[...]
    advanced[...] = state[2 * LEV :]
    values = column_values(state, rates[pl.ds(1 - core, 1), :])
    for slot in range(2):
        done[slot] = placed(values, routes, slot, 1 - core)


def outer_kernel(
    outer, number, neighbour, routes, rates, done, inner_advanced, advanced, outgoing
):
    core = lax.rem(lax.axis_index("blk"), 2)
    state = outer[...] + number[...] * neighbour[: FIELDS * LEV, :]
    here, there = state[2 * LEV :], inner_advanced[...]
    advanced[pl.ds(0, 4 * LEV, stride=2), :] = jnp.where(core == 0, here, there)
    advanced[pl.ds(1, 4 * LEV, stride=2), :] = jnp.where(core == 0, there, here)
    values = column_values(state, rates[pl.ds(core, 1), :])
    for slot in range(2):
        outgoing[pl.ds(slot, DEVICES, stride=2), :] = done[slot] + placed(
            values, routes, slot, core
        )


def cloud_kernel(
    incoming, start, sums, advanced, outgoing, gcm_next,
    state, coef, mean, total, square, departure,
):
    leaving = pltpu.make_async_copy(
        advanced, gcm_next.at[pl.ds(2 * 2 * LEV, 4 * 2 * LEV)], departure
    )
    leaving.start()
    level = lax.broadcasted_iota(jnp.int32, (LEV, LANES), 0)
    top = level == LEV - 1
    rates = []

    def up(x):
        return pltpu.roll(x, LEV - 1, axis=0)

    def down(x):
        return pltpu.roll(x, 1, axis=0)

    def tree(parts):
        while len(parts) > 1:
            parts = [a + b for a, b in zip(parts[::2], parts[1::2])]
        return parts[0]

    def folded(ref, *lead):
        return tree(
            [ref[(*lead, pl.ds(part, LEV, stride=SUB), slice(None))] for part in range(SUB)]
        )

    for half in range(2):
        values = jnp.transpose(incoming[half * LANES : (half + 1) * LANES, :])
        rise = values[3 * LEV :]
        rates.append(rise[LEV - 1 :])
        rise = jnp.where(top, 0.0, rise)
        base = SHIFT * (1.0 - rise + down(rise))
        coef[0, half] = values[:LEV] + SHIFT - 0.75 * base
        coef[1, half] = values[LEV : 2 * LEV]
        coef[2, half] = values[2 * LEV : 3 * LEV]
        coef[3, half] = rise
        coef[7, half] = jnp.broadcast_to(rates[half], (LEV, LANES))
        for f in range(2):
            mean[f, half] = folded(sums, f, half) * (1.0 / NXC)

    def lifted(x, rise):
        flux = rise * jnp.where(rise > 0.0, x, up(x))
        return x - flux + down(flux)

    def relax(first):
        for half in range(2):
            rise, rate = coef[3, half], coef[7, half]
            now = [lifted(mean[f, half], rise) for f in range(2)]
            add = [coef[f, half] - 0.25 * now[f] for f in range(2)]
            offset = add[1]
            if not first:
                kept = lifted(mean[3, half], rise)
                owed = rate * kept
                offset = offset + (kept - owed)
                coef[4, half] = add[0] + owed
            else:
                coef[4, half] = add[0]
            mean[3, half] = offset
            coef[5, half] = -offset
            lacking = rate * offset
            coef[8, half] = lacking
            mean[0, half] = now[0] + add[0]
            mean[1, half] = now[1] + add[1]
            coef[6, half] = now[0] + add[0] - lacking

    def settle():
        for half in range(2):
            rain = folded(total, half) * (1.0 / NXC) + coef[8, half]
            mean[0, half] = mean[0, half] + rain
            mean[1, half] = mean[1, half] - rain
            mean[2, half] = mean[2, half] + rain

    def sweep(source, half, last):
        rate = jnp.broadcast_to(coef[7, half, 0:1, :], (SUB, LANES))

        def row(index, k):
            return jnp.broadcast_to(coef[index, half, k : k + 1, :], (SUB, LANES))

        def drifted(f, k, size, positive):
            cells = [
                source[f, half, k * NXC + j * SUB : k * NXC + (j + 1) * SUB, :]
                for j in range(INNER)
            ]
            before = [pltpu.roll(cells[-1], 1, axis=0)] + cells[:-1]
            after = cells[1:] + [pltpu.roll(cells[0], SUB - 1, axis=0)]
            return [
                c + size * (jnp.where(positive, b, a) - c)
                for c, b, a in zip(cells, before, after)
            ]

        def level_of(k):
            drift = row(2, k)
            size, positive = jnp.abs(drift), drift > 0.0
            return [drifted(f, k, size, positive) for f in range(2)]

        now = level_of(0)
        below = None
        for k in range(LEV):
            gain, least = row(4, k), row(5, k)
            if k < LEV - 1:
                after = level_of(k + 1)
                rise = row(3, k)
                upward = rise > 0.0
                flux = [
                    [rise * jnp.where(upward, a, b) for a, b in zip(now[f], after[f])]
                    for f in range(2)
                ]
            rained, spread = [], []
            if last:
                middle = row(6, k)
            for j in range(INNER):
                new = []
                for f in range(2):
                    x = now[f][j]
                    if k < LEV - 1:
                        x = x - flux[f][j]
                    if k > 0:
                        x = x + below[f][j]
                    new.append(x)
                temper, moisture = new
                temper = temper + gain
                rain = rate * jnp.maximum(moisture - jnp.exp2(temper), least)
                temper = temper + rain
                rained.append(rain)
                if last:
                    away = temper - middle
                    spread.append(away * away)
                else:
                    at = slice(k * NXC + j * SUB, k * NXC + (j + 1) * SUB)
                    state[0, half, at, :] = temper
                    state[1, half, at, :] = moisture - rain
            total[half, k * SUB : (k + 1) * SUB, :] = tree(rained)
            if last:
                square[half, k * SUB : (k + 1) * SUB, :] = tree(spread)
            if k < LEV - 1:
                below, now = flux, after

    def substep(source, first, last):
        relax(first)

        def half_of(half, carry):
            sweep(source, half, last)
            return carry

        lax.fori_loop(0, 2, half_of, 0)
        if not last:
            settle()

    for half in range(2):
        mean[2, half] = jnp.zeros((LEV, LANES), jnp.float32)
    substep(start, True, False)

    def middle_step(step, carry):
        substep(state, False, False)
        return carry

    lax.fori_loop(0, SUBSTEPS - 2, middle_step, 0)
    substep(state, False, True)
    settle()
    for half in range(2):
        warm, wet, rain = mean[0, half], mean[1, half], mean[2, half]
        gap = warm - coef[6, half] - coef[8, half]
        spread = folded(square, half) * (1.0 / NXC) - gap * gap
        result = [
            (warm - SHIFT) * (1.0 / ALPHA),
            wet * (1.0 / BETA),
            rain * (1.0 / BETA),
            spread * (1.0 / (ALPHA * ALPHA)),
        ]
        outgoing[half * LANES : (half + 1) * LANES, :] = jnp.transpose(
            jnp.concatenate(result, axis=0)
        )
    leaving.wait()


def home_kernel(returned, routes, begun, gcm_next, stats):
    del begun
    home = None
    for slot in range(2):
        back = returned[pl.ds(slot, DEVICES, stride=2), :]
        term = select_dot(jnp.transpose(back), routes[slot], ((1,), (0,)), True)
        home = term if home is None else home + term
    for y in range(2):
        part = home[:, y * LANES : (y + 1) * LANES]
        gcm_next[pl.ds(y, 2 * LEV, stride=2), :] = part[: 2 * LEV]
        stats[pl.ds(y, 2 * LEV, stride=2), :] = part[2 * LEV :]


def whole(shape):
    return pl.BlockSpec(shape, lambda *_: (0,) * len(shape))


def f32(*shape):
    return jax.ShapeDtypeStruct(shape, jnp.float32)


def in_hbm(x):
    return pltpu.with_memory_space_constraint(x, pltpu.HBM)


def transfer(rows):
    moved = lax.all_to_all(
        rows.reshape(DEVICES, 2, LANES), ("blk", "sub"), split_axis=0, concat_axis=0, tiled=True
    )
    return moved.reshape(COLS, LANES)


def body(gcm_state, crm_state, owner, branch, diffusion):
    gcm = gcm_state.reshape(GCM_ROWS, LANES)

    def pairs(n, first):
        ahead = [(i, (i + 1) % n) for i in range(first, n, 2)]
        return ahead + [(j, i) for i, j in ahead]

    n_blk, n_sub = lax.axis_size("blk"), lax.axis_size("sub")
    hbm = pl.BlockSpec(memory_space=pltpu.HBM)
    gcm_here, to_core_mate, to_neighbour, owner_here, branch_here, diffusion_here = pl.pallas_call(
        load_kernel,
        in_specs=[hbm] * 4,
        out_shape=(
            f32(GCM_ROWS, LANES),
            f32(FIELDS * LEV, LANES),
            f32(FIELDS * LEV + SUB, LANES),
            jax.ShapeDtypeStruct(owner.shape, owner.dtype),
            jax.ShapeDtypeStruct(branch.shape, branch.dtype),
            f32(*diffusion.shape),
        ),
        scratch_shapes=[pltpu.SemaphoreType.DMA((4,))],
        compiler_params=pltpu.CompilerParams(vmem_limit_bytes=4 * MIB),
        name="load",
    )(*map(in_hbm, (gcm, owner, branch, diffusion)))
    neighbour = lax.ppermute(to_neighbour, "blk", pairs(n_blk, 1))
    core_mate = lax.ppermute(to_core_mate, "blk", pairs(n_blk, 0))
    to_chip_mate, to_other, routes, rates, number = pl.pallas_call(
        edge_kernel,
        out_shape=(
            f32(SUB, LANES),
            f32(SUB, LANES),
            jax.ShapeDtypeStruct((2, DEVICES, COLS), jnp.bfloat16),
            f32(2, LANES),
            f32(FIELDS * LEV, LANES),
        ),
        compiler_params=pltpu.CompilerParams(vmem_limit_bytes=4 * MIB),
        name="edges",
    )(gcm_here, owner_here, branch_here, diffusion_here)
    chip_mate = lax.ppermute(to_chip_mate, "sub", pairs(n_sub, 0))
    other = lax.ppermute(to_other, "sub", pairs(n_sub, 1))
    cells = 2 * LEV * NXC * COLS
    state, sums, partial = pl.pallas_call(
        early_kernel,
        in_specs=[hbm, whole((GCM_ROWS, LANES)), whole((FIELDS * LEV, LANES))],
        out_shape=(
            f32(2, 2, LEV * NXC, LANES),
            f32(2, 2, LEV * SUB, LANES),
            f32(2, FIELDS * LEV, LANES),
        ),
        scratch_shapes=[
            pltpu.VMEM((2, LEV, NXC, COLS), jnp.bfloat16),
            pltpu.SemaphoreType.DMA((2, LEV // CRM_CHUNK)),
        ],
        compiler_params=pltpu.CompilerParams(vmem_limit_bytes=16 * MIB),
        cost_estimate=pl.CostEstimate(flops=4 * cells, bytes_accessed=6 * cells, transcendentals=0),
        name="early",
    )(in_hbm(crm_state), gcm_here, number)
    outer, done, inner_advanced = pl.pallas_call(
        inner_kernel,
        out_shape=(
            f32(FIELDS * LEV, LANES),
            f32(2, DEVICES, LANES),
            f32(4 * LEV, LANES),
        ),
        compiler_params=pltpu.CompilerParams(vmem_limit_bytes=8 * MIB),
        name="inner",
    )(partial, number, core_mate, other, chip_mate, routes, rates)
    advanced, outgoing = pl.pallas_call(
        outer_kernel,
        out_shape=(f32(4 * 2 * LEV, LANES), f32(COLS, LANES)),
        compiler_params=pltpu.CompilerParams(vmem_limit_bytes=8 * MIB),
        name="outer",
    )(outer, number, neighbour, routes, rates, done, inner_advanced)

    incoming = transfer(outgoing)
    profiles, gcm_next = pl.pallas_call(
        cloud_kernel,
        out_specs=(whole((COLS, LANES)), hbm),
        out_shape=(f32(COLS, LANES), f32(GCM_ROWS, LANES)),
        scratch_shapes=[
            pltpu.VMEM((2, 2, LEV * NXC, LANES), jnp.float32),
            pltpu.VMEM((9, 2, LEV, LANES), jnp.float32),
            pltpu.VMEM((4, 2, LEV, LANES), jnp.float32),
            pltpu.VMEM((2, LEV * SUB, LANES), jnp.float32),
            pltpu.VMEM((2, LEV * SUB, LANES), jnp.float32),
            pltpu.SemaphoreType.DMA(()),
        ],
        compiler_params=pltpu.CompilerParams(vmem_limit_bytes=12 * MIB),
        name="cloud",
    )(incoming, state, sums, advanced)
    returned = transfer(profiles)

    gcm_next, stats = pl.pallas_call(
        home_kernel,
        grid=(1,),
        in_specs=[
            whole((COLS, LANES)),
            whole((2, DEVICES, COLS)),
            pl.BlockSpec(memory_space=pl.ANY),
        ],
        out_specs=(whole((4 * LEV, LANES)), whole((4 * LEV, LANES))),
        out_shape=(f32(GCM_ROWS, LANES), f32(4 * LEV, LANES)),
        input_output_aliases={2: 0},
        compiler_params=pltpu.CompilerParams(vmem_limit_bytes=8 * MIB),
        name="home",
    )(returned, routes, gcm_next)
    return gcm_next.reshape(gcm_state.shape), stats.reshape(2, LEV, 2, LANES)


def solution(mesh):
    grid = P(None, None, "blk", "sub")
    return jax.shard_map(
        body,
        mesh=mesh,
        in_specs=(grid, P(None, None, None, ("blk", "sub")), P("blk", "sub"), P("blk", "sub"), P()),
        out_specs=(grid, grid),
        check_vma=False,
    )
```

```python
import math

import jax
import jax.numpy as jnp
from jax import lax
from jax.experimental import pallas as pl
from jax.experimental.pallas import tpu as pltpu
from jax.sharding import PartitionSpec as P

SUBSTEPS = 4
LEV = 32
NXC = 64
LANES = 128
DEVICES = 128
COLS = 256
FIELDS = 6
SUB = 8
INNER = NXC // SUB
GCM_ROWS = FIELDS * LEV * 2
CRM_CHUNK = 8
ALPHA = 0.3 * math.log2(math.e)
BETA = 1.5 * ALPHA
SHIFT = math.log2(0.5 * BETA)
MIB = 1 << 20


def pieces(x):
    first = x.astype(jnp.bfloat16)
    rest = x - first.astype(jnp.float32)
    second = rest.astype(jnp.bfloat16)
    third = (rest - second.astype(jnp.float32)).astype(jnp.bfloat16)
    return first, second, third


def select_dot(x, chosen, dims, x_first):
    total = None
    for part in pieces(x):
        pair = (part, chosen) if x_first else (chosen, part)
        term = lax.dot_general(*pair, (dims, ((), ())), preferred_element_type=jnp.float32)
        total = term if total is None else total + term
    return total


def rows_of(ref, y):
    return ref[pl.ds(y, FIELDS * LEV, stride=2), :]


def load_kernel(
    gcm_hbm, owner_hbm, branch_hbm, diffusion_hbm,
    gcm, to_core_mate, to_neighbour, owner, branch, diffusion, arrival,
):
    loads = [
        pltpu.make_async_copy(source, target, arrival.at[n])
        for n, (source, target) in enumerate(
            [(gcm_hbm, gcm), (owner_hbm, owner), (branch_hbm, branch), (diffusion_hbm, diffusion)]
        )
    ]
    for copy in loads:
        copy.start()
    for copy in loads:
        copy.wait()
    core = lax.rem(lax.axis_index("blk"), 2)
    rows = [rows_of(gcm, 0), rows_of(gcm, 1)]
    to_core_mate[...] = jnp.where(core == 0, rows[1], rows[0])
    to_neighbour[: FIELDS * LEV, :] = jnp.where(core == 0, rows[0], rows[1])
    to_neighbour[FIELDS * LEV :, :] = jnp.zeros((SUB, LANES), jnp.float32)


def edge_kernel(
    gcm, owner, branch, diffusion, to_chip_mate, to_other, routes, rates, number
):
    to_chip_mate[...] = jnp.zeros_like(to_chip_mate)
    to_other[...] = jnp.zeros_like(to_other)
    device = lax.broadcasted_iota(jnp.int32, (DEVICES, LANES), 0)
    target = jnp.concatenate(
        [(device == owner[y : y + 1, :]).astype(jnp.float32) for y in range(2)], axis=1
    )
    earlier = (
        lax.broadcasted_iota(jnp.int32, (COLS, COLS), 0)
        < lax.broadcasted_iota(jnp.int32, (COLS, COLS), 1)
    ).astype(jnp.bfloat16)
    count = jnp.dot(target.astype(jnp.bfloat16), earlier, preferred_element_type=jnp.float32)
    for slot in range(2):
        here = jnp.where(count < 0.5, 1.0 - slot, 0.0 + slot)
        routes[slot] = (target * here).astype(jnp.bfloat16)
    rates[...] = jnp.where(branch[...] == 1, 0.6, 0.2)
    for f in range(FIELDS):
        spread = jnp.broadcast_to(diffusion[f : f + 1, :], (LANES, LEV))
        number[f * LEV : (f + 1) * LEV, :] = jnp.transpose(spread)

    even = lax.rem(lax.axis_index("sub"), 2) == 0
    rows = jnp.concatenate([rows_of(gcm, 0), rows_of(gcm, 1)], axis=0)
    for part in range(GCM_ROWS // LANES):
        turned = jnp.transpose(rows[part * LANES : (part + 1) * LANES])
        first, last = turned[:1], turned[LANES - 1 :]
        to_chip_mate[part : part + 1, :] = jnp.where(even, last, first)
        to_other[part : part + 1, :] = jnp.where(even, first, last)


def tree(parts):
    while len(parts) > 1:
        parts = [a + b for a, b in zip(parts[::2], parts[1::2])]
    return parts[0]


def folded(ref, *lead):
    return tree([ref[(*lead, pl.ds(part, LEV, stride=SUB), slice(None))] for part in range(SUB)])


def early_kernel(crm_hbm, gcm, number, state, means, partial, crm, sums, arrival):
    loads = [
        pltpu.make_async_copy(
            crm_hbm.at[f, pl.ds(part * CRM_CHUNK, CRM_CHUNK)],
            crm.at[f, pl.ds(part * CRM_CHUNK, CRM_CHUNK)],
            arrival.at[f, part],
        )
        for f in range(2)
        for part in range(LEV // CRM_CHUNK)
    ]
    for copy in loads:
        copy.start()
    lane = lax.broadcasted_iota(jnp.int32, (FIELDS * LEV, LANES), 1)
    own = [rows_of(gcm, 0), rows_of(gcm, 1)]
    for y in range(2):
        before = jnp.where(lane == 0, 0.0, pltpu.roll(own[y], 1, axis=1))
        after = jnp.where(lane == LANES - 1, 0.0, pltpu.roll(own[y], LANES - 1, axis=1))
        around = own[1 - y] + after + before
        partial[y] = own[y] + number[...] * (around - 4.0 * own[y])

    for f, (scale, shift) in enumerate([(ALPHA, SHIFT), (BETA, 0.0)]):
        for part in range(LEV // CRM_CHUNK):
            loads[f * (LEV // CRM_CHUNK) + part].wait()

            def level(n, carry):
                k = part * CRM_CHUNK + n
                for half in range(2):
                    x = crm[f, k, :, half * LANES : (half + 1) * LANES].astype(jnp.float32)
                    x = x * scale + shift
                    total = None
                    for row in range(SUB):
                        block = x[row * INNER : (row + 1) * INNER]
                        state[f, half, pl.ds(k * NXC + row, INNER, stride=SUB), :] = block
                        total = block if total is None else total + block
                    sums[f, half, pl.ds(pl.multiple_of(k * SUB, SUB), SUB), :] = total
                return carry

            lax.fori_loop(0, CRM_CHUNK, level, 0, unroll=4)
    for f in range(2):
        for half in range(2):
            means[f, half] = folded(sums, f, half) * (1.0 / NXC)


def column_values(state, rate):
    level = lax.broadcasted_iota(jnp.int32, (LEV, LANES), 0)
    field = [state[f * LEV : (f + 1) * LEV] for f in range(FIELDS)]
    warm = ALPHA * (0.25 * field[0] + 0.2 * field[4])
    wet = BETA * (0.25 * field[1] + 0.2 * field[5])
    drift = 0.45 * jnp.tanh(field[2])
    tilt = jnp.tanh(field[3])
    rise = 0.15 * (tilt + pltpu.roll(tilt, LEV - 1, axis=0))
    rise = jnp.where(level == LEV - 1, rate, rise)
    return jnp.concatenate([warm, wet, drift, rise], axis=0)


def placed(values, routes, slot, y):
    route = routes[slot, :, pl.ds(pl.multiple_of(y * LANES, LANES), LANES)]
    return select_dot(values, route, ((1,), (1,)), False)


def inner_kernel(
    partial, number, core_mate, other, chip_mate, routes, rates, outer, done, advanced
):
    lane = lax.broadcasted_iota(jnp.int32, (FIELDS * LEV, LANES), 1)
    core = lax.rem(lax.axis_index("blk"), 2)

    def columns(ref):
        turned = jnp.transpose(ref)
        column = jnp.concatenate([turned[:, n : n + 1] for n in range(GCM_ROWS // LANES)], axis=0)
        return column[: FIELDS * LEV], column[FIELDS * LEV :]

    even = lax.rem(lax.axis_index("sub"), 2) == 0
    near, far = chip_mate[...], other[...]
    west, east = columns(jnp.where(even, far, near)), columns(jnp.where(even, near, far))
    rows = []
    for y in range(2):
        side = jnp.where(lane == 0, west[y], jnp.where(lane == LANES - 1, east[y], 0.0))
        rows.append(partial[y] + number[...] * side)
    outer[...] = jnp.where(core == 0, rows[0], rows[1])
    state = jnp.where(core == 0, rows[1], rows[0]) + number[...] * core_mate[...]
    advanced[...] = state[2 * LEV :]
    values = column_values(state, rates[pl.ds(1 - core, 1), :])
    for slot in range(2):
        done[slot] = placed(values, routes, slot, 1 - core)


def outer_kernel(
    outer, number, neighbour, routes, rates, done, inner_advanced, advanced, outgoing
):
    core = lax.rem(lax.axis_index("blk"), 2)
    state = outer[...] + number[...] * neighbour[: FIELDS * LEV, :]
    here, there = state[2 * LEV :], inner_advanced[...]
    advanced[pl.ds(0, 4 * LEV, stride=2), :] = jnp.where(core == 0, here, there)
    advanced[pl.ds(1, 4 * LEV, stride=2), :] = jnp.where(core == 0, there, here)
    values = column_values(state, rates[pl.ds(core, 1), :])
    for slot in range(2):
        outgoing[pl.ds(slot, DEVICES, stride=2), :] = done[slot] + placed(
            values, routes, slot, core
        )


def cloud_kernel(
    incoming, start, means, advanced, outgoing, gcm_next,
    state, coef, mean, total, square, departure,
):
    leaving = pltpu.make_async_copy(
        advanced, gcm_next.at[pl.ds(2 * 2 * LEV, 4 * 2 * LEV)], departure
    )
    leaving.start()
    level = lax.broadcasted_iota(jnp.int32, (LEV, LANES), 0)
    top = level == LEV - 1
    rates = []

    def up(x):
        return pltpu.roll(x, LEV - 1, axis=0)

    def down(x):
        return pltpu.roll(x, 1, axis=0)

    for half in range(2):
        values = jnp.transpose(incoming[half * LANES : (half + 1) * LANES, :])
        rise = values[3 * LEV :]
        rates.append(rise[LEV - 1 :])
        rise = jnp.where(top, 0.0, rise)
        base = SHIFT * (1.0 - rise + down(rise))
        coef[0, half] = values[:LEV] + SHIFT - 0.75 * base
        coef[1, half] = values[LEV : 2 * LEV]
        coef[2, half] = values[2 * LEV : 3 * LEV]
        coef[3, half] = rise
        coef[7, half] = jnp.broadcast_to(rates[half], (LEV, LANES))
        coef[9, half] = jnp.abs(coef[2, half])

    def lifted(x, rise):
        flux = rise * jnp.where(rise > 0.0, x, up(x))
        return x - flux + down(flux)

    def settled(half):
        rain = folded(total, half) * (1.0 / NXC) + coef[8, half]
        return mean[0, half] + rain, mean[1, half] - rain, mean[2, half] + rain

    def relax(first):
        for half in range(2):
            rise, rate = coef[3, half], coef[7, half]
            if first:
                before = means[0, half], means[1, half]
                mean[2, half] = jnp.zeros((LEV, LANES), jnp.float32)
            else:
                *before, mean[2, half] = settled(half)
            now = [lifted(x, rise) for x in before]
            add = [coef[f, half] - 0.25 * now[f] for f in range(2)]
            offset = add[1]
            if first:
                coef[4, half] = add[0]
            else:
                kept = lifted(mean[3, half], rise)
                owed = rate * kept
                offset = offset + (kept - owed)
                coef[4, half] = add[0] + owed
            mean[3, half] = offset
            coef[5, half] = -offset
            lacking = rate * offset
            coef[8, half] = lacking
            mean[0, half] = now[0] + add[0]
            mean[1, half] = now[1] + add[1]
            coef[6, half] = now[0] + add[0] - lacking

    def sweep(source, half, last):
        rate = jnp.broadcast_to(coef[7, half, 0:1, :], (SUB, LANES))

        def row(index, k):
            return jnp.broadcast_to(coef[index, half, k : k + 1, :], (SUB, LANES))

        def drifted(f, k, size, positive):
            cells = [
                source[f, half, k * NXC + j * SUB : k * NXC + (j + 1) * SUB, :]
                for j in range(INNER)
            ]
            before = [pltpu.roll(cells[-1], 1, axis=0)] + cells[:-1]
            after = cells[1:] + [pltpu.roll(cells[0], SUB - 1, axis=0)]
            return [
                c + size * (jnp.where(positive, b, a) - c)
                for c, b, a in zip(cells, before, after)
            ]

        def level_of(k):
            drift = row(2, k)
            size, positive = row(9, k), drift > 0.0
            return [drifted(f, k, size, positive) for f in range(2)]

        now = level_of(0)
        below = None
        for k in range(LEV):
            gain, least = row(4, k), row(5, k)
            if k < LEV - 1:
                after = level_of(k + 1)
                rise = row(3, k)
                upward = rise > 0.0
                flux = [
                    [rise * jnp.where(upward, a, b) for a, b in zip(now[f], after[f])]
                    for f in range(2)
                ]
            rained, spread = [], []
            if last:
                middle = row(6, k)
            for j in range(INNER):
                new = []
                for f in range(2):
                    x = now[f][j]
                    if k < LEV - 1:
                        x = x - flux[f][j]
                    if k > 0:
                        x = x + below[f][j]
                    new.append(x)
                temper, moisture = new
                temper = temper + gain
                rain = rate * jnp.maximum(moisture - jnp.exp2(temper), least)
                temper = temper + rain
                rained.append(rain)
                if last:
                    away = temper - middle
                    spread.append(away * away)
                else:
                    at = slice(k * NXC + j * SUB, k * NXC + (j + 1) * SUB)
                    state[0, half, at, :] = temper
                    state[1, half, at, :] = moisture - rain
            total[half, k * SUB : (k + 1) * SUB, :] = tree(rained)
            if last:
                square[half, k * SUB : (k + 1) * SUB, :] = tree(spread)
            if k < LEV - 1:
                below, now = flux, after

    def substep(source, first, last):
        relax(first)

        def half_of(half, carry):
            sweep(source, half, last)
            return carry

        lax.fori_loop(0, 2, half_of, 0)

    substep(start, True, False)

    def middle_step(step, carry):
        substep(state, False, False)
        return carry

    lax.fori_loop(0, SUBSTEPS - 2, middle_step, 0)
    substep(state, False, True)
    for half in range(2):
        warm, wet, rain = settled(half)
        gap = warm - coef[6, half] - coef[8, half]
        spread = folded(square, half) * (1.0 / NXC) - gap * gap
        result = [
            (warm - SHIFT) * (1.0 / ALPHA),
            wet * (1.0 / BETA),
            rain * (1.0 / BETA),
            spread * (1.0 / (ALPHA * ALPHA)),
        ]
        outgoing[half * LANES : (half + 1) * LANES, :] = jnp.transpose(
            jnp.concatenate(result, axis=0)
        )
    leaving.wait()


def home_kernel(returned, routes, begun, gcm_next, stats):
    del begun
    home = None
    for slot in range(2):
        back = returned[pl.ds(slot, DEVICES, stride=2), :]
        term = select_dot(jnp.transpose(back), routes[slot], ((1,), (0,)), True)
        home = term if home is None else home + term
    for y in range(2):
        part = home[:, y * LANES : (y + 1) * LANES]
        gcm_next[pl.ds(y, 2 * LEV, stride=2), :] = part[: 2 * LEV]
        stats[pl.ds(y, 2 * LEV, stride=2), :] = part[2 * LEV :]


def whole(shape):
    return pl.BlockSpec(shape, lambda *_: (0,) * len(shape))


def f32(*shape):
    return jax.ShapeDtypeStruct(shape, jnp.float32)


def in_hbm(x):
    return pltpu.with_memory_space_constraint(x, pltpu.HBM)


def transfer(rows):
    moved = lax.all_to_all(
        rows.reshape(DEVICES, 2, LANES), ("blk", "sub"), split_axis=0, concat_axis=0, tiled=True
    )
    return moved.reshape(COLS, LANES)


def body(gcm_state, crm_state, owner, branch, diffusion):
    gcm = gcm_state.reshape(GCM_ROWS, LANES)

    def pairs(n, first):
        ahead = [(i, (i + 1) % n) for i in range(first, n, 2)]
        return ahead + [(j, i) for i, j in ahead]

    n_blk, n_sub = lax.axis_size("blk"), lax.axis_size("sub")
    hbm = pl.BlockSpec(memory_space=pltpu.HBM)
    gcm_here, to_core_mate, to_neighbour, owner_here, branch_here, diffusion_here = pl.pallas_call(
        load_kernel,
        in_specs=[hbm] * 4,
        out_shape=(
            f32(GCM_ROWS, LANES),
            f32(FIELDS * LEV, LANES),
            f32(FIELDS * LEV + SUB, LANES),
            jax.ShapeDtypeStruct(owner.shape, owner.dtype),
            jax.ShapeDtypeStruct(branch.shape, branch.dtype),
            f32(*diffusion.shape),
        ),
        scratch_shapes=[pltpu.SemaphoreType.DMA((4,))],
        compiler_params=pltpu.CompilerParams(vmem_limit_bytes=4 * MIB),
        name="load",
    )(*map(in_hbm, (gcm, owner, branch, diffusion)))
    neighbour = lax.ppermute(to_neighbour, "blk", pairs(n_blk, 1))
    core_mate = lax.ppermute(to_core_mate, "blk", pairs(n_blk, 0))
    to_chip_mate, to_other, routes, rates, number = pl.pallas_call(
        edge_kernel,
        out_shape=(
            f32(SUB, LANES),
            f32(SUB, LANES),
            jax.ShapeDtypeStruct((2, DEVICES, COLS), jnp.bfloat16),
            f32(2, LANES),
            f32(FIELDS * LEV, LANES),
        ),
        compiler_params=pltpu.CompilerParams(vmem_limit_bytes=4 * MIB),
        name="edges",
    )(gcm_here, owner_here, branch_here, diffusion_here)
    chip_mate = lax.ppermute(to_chip_mate, "sub", pairs(n_sub, 0))
    other = lax.ppermute(to_other, "sub", pairs(n_sub, 1))
    cells = 2 * LEV * NXC * COLS
    state, means, partial = pl.pallas_call(
        early_kernel,
        in_specs=[hbm, whole((GCM_ROWS, LANES)), whole((FIELDS * LEV, LANES))],
        out_shape=(
            f32(2, 2, LEV * NXC, LANES),
            f32(2, 2, LEV, LANES),
            f32(2, FIELDS * LEV, LANES),
        ),
        scratch_shapes=[
            pltpu.VMEM((2, LEV, NXC, COLS), jnp.bfloat16),
            pltpu.VMEM((2, 2, LEV * SUB, LANES), jnp.float32),
            pltpu.SemaphoreType.DMA((2, LEV // CRM_CHUNK)),
        ],
        compiler_params=pltpu.CompilerParams(vmem_limit_bytes=16 * MIB),
        cost_estimate=pl.CostEstimate(flops=4 * cells, bytes_accessed=6 * cells, transcendentals=0),
        name="early",
    )(in_hbm(crm_state), gcm_here, number)
    outer, done, inner_advanced = pl.pallas_call(
        inner_kernel,
        out_shape=(
            f32(FIELDS * LEV, LANES),
            f32(2, DEVICES, LANES),
            f32(4 * LEV, LANES),
        ),
        compiler_params=pltpu.CompilerParams(vmem_limit_bytes=8 * MIB),
        name="inner",
    )(partial, number, core_mate, other, chip_mate, routes, rates)
    advanced, outgoing = pl.pallas_call(
        outer_kernel,
        out_shape=(f32(4 * 2 * LEV, LANES), f32(COLS, LANES)),
        compiler_params=pltpu.CompilerParams(vmem_limit_bytes=8 * MIB),
        name="outer",
    )(outer, number, neighbour, routes, rates, done, inner_advanced)

    incoming = transfer(outgoing)
    profiles, gcm_next = pl.pallas_call(
        cloud_kernel,
        out_specs=(whole((COLS, LANES)), hbm),
        out_shape=(f32(COLS, LANES), f32(GCM_ROWS, LANES)),
        scratch_shapes=[
            pltpu.VMEM((2, 2, LEV * NXC, LANES), jnp.float32),
            pltpu.VMEM((10, 2, LEV, LANES), jnp.float32),
            pltpu.VMEM((4, 2, LEV, LANES), jnp.float32),
            pltpu.VMEM((2, LEV * SUB, LANES), jnp.float32),
            pltpu.VMEM((2, LEV * SUB, LANES), jnp.float32),
            pltpu.SemaphoreType.DMA(()),
        ],
        compiler_params=pltpu.CompilerParams(vmem_limit_bytes=12 * MIB),
        name="cloud",
    )(incoming, state, means, advanced)
    returned = transfer(profiles)

    gcm_next, stats = pl.pallas_call(
        home_kernel,
        grid=(1,),
        in_specs=[
            whole((COLS, LANES)),
            whole((2, DEVICES, COLS)),
            pl.BlockSpec(memory_space=pl.ANY),
        ],
        out_specs=(whole((4 * LEV, LANES)), whole((4 * LEV, LANES))),
        out_shape=(f32(GCM_ROWS, LANES), f32(4 * LEV, LANES)),
        input_output_aliases={2: 0},
        compiler_params=pltpu.CompilerParams(vmem_limit_bytes=8 * MIB),
        name="home",
    )(returned, routes, gcm_next)
    return gcm_next.reshape(gcm_state.shape), stats.reshape(2, LEV, 2, LANES)


def solution(mesh):
    grid = P(None, None, "blk", "sub")
    return jax.shard_map(
        body,
        mesh=mesh,
        in_specs=(grid, P(None, None, None, ("blk", "sub")), P("blk", "sub"), P("blk", "sub"), P()),
        out_specs=(grid, grid),
        check_vma=False,
    )
```

```python
import math

import jax
import jax.numpy as jnp
from jax import lax
from jax.experimental import pallas as pl
from jax.experimental.pallas import tpu as pltpu
from jax.sharding import PartitionSpec as P

SUBSTEPS = 4
LEV = 32
NXC = 64
LANES = 128
DEVICES = 128
COLS = 256
FIELDS = 6
SUB = 8
INNER = NXC // SUB
GCM_ROWS = FIELDS * LEV * 2
CRM_CHUNK = 8
ALPHA = 0.3 * math.log2(math.e)
BETA = 1.5 * ALPHA
SHIFT = math.log2(0.5 * BETA)
MIB = 1 << 20


def pieces(x):
    first = x.astype(jnp.bfloat16)
    rest = x - first.astype(jnp.float32)
    second = rest.astype(jnp.bfloat16)
    third = (rest - second.astype(jnp.float32)).astype(jnp.bfloat16)
    return first, second, third


def select_dot(x, chosen, dims, x_first):
    total = None
    for part in pieces(x):
        pair = (part, chosen) if x_first else (chosen, part)
        term = lax.dot_general(*pair, (dims, ((), ())), preferred_element_type=jnp.float32)
        total = term if total is None else total + term
    return total


def rows_of(ref, y):
    return ref[pl.ds(y, FIELDS * LEV, stride=2), :]


def load_kernel(
    gcm_hbm, owner_hbm, branch_hbm, diffusion_hbm,
    gcm, to_neighbour, owner, branch, diffusion, arrival,
):
    loads = [
        pltpu.make_async_copy(source, target, arrival.at[n])
        for n, (source, target) in enumerate(
            [(gcm_hbm, gcm), (owner_hbm, owner), (branch_hbm, branch), (diffusion_hbm, diffusion)]
        )
    ]
    for copy in loads:
        copy.start()
    for copy in loads:
        copy.wait()
    core = lax.rem(lax.axis_index("blk"), 2)
    to_neighbour[: FIELDS * LEV, :] = jnp.where(core == 0, rows_of(gcm, 0), rows_of(gcm, 1))
    to_neighbour[FIELDS * LEV :, :] = jnp.zeros((SUB, LANES), jnp.float32)


def edge_kernel(
    gcm, owner, branch, diffusion,
    to_core_mate, to_chip_mate, to_other, routes, rates, number,
):
    to_chip_mate[...] = jnp.zeros_like(to_chip_mate)
    to_other[...] = jnp.zeros_like(to_other)
    device = lax.broadcasted_iota(jnp.int32, (DEVICES, LANES), 0)
    target = jnp.concatenate(
        [(device == owner[y : y + 1, :]).astype(jnp.float32) for y in range(2)], axis=1
    )
    earlier = (
        lax.broadcasted_iota(jnp.int32, (COLS, COLS), 0)
        < lax.broadcasted_iota(jnp.int32, (COLS, COLS), 1)
    ).astype(jnp.bfloat16)
    count = jnp.dot(target.astype(jnp.bfloat16), earlier, preferred_element_type=jnp.float32)
    for slot in range(2):
        here = jnp.where(count < 0.5, 1.0 - slot, 0.0 + slot)
        routes[slot] = (target * here).astype(jnp.bfloat16)
    rates[...] = jnp.where(branch[...] == 1, 0.6, 0.2)
    for f in range(FIELDS):
        spread = jnp.broadcast_to(diffusion[f : f + 1, :], (LANES, LEV))
        number[f * LEV : (f + 1) * LEV, :] = jnp.transpose(spread)

    even = lax.rem(lax.axis_index("sub"), 2) == 0
    pair = [rows_of(gcm, 0), rows_of(gcm, 1)]
    core = lax.rem(lax.axis_index("blk"), 2)
    to_core_mate[...] = jnp.where(core == 0, pair[1], pair[0])
    rows = jnp.concatenate(pair, axis=0)
    for part in range(GCM_ROWS // LANES):
        turned = jnp.transpose(rows[part * LANES : (part + 1) * LANES])
        first, last = turned[:1], turned[LANES - 1 :]
        to_chip_mate[part : part + 1, :] = jnp.where(even, last, first)
        to_other[part : part + 1, :] = jnp.where(even, first, last)


def tree(parts):
    while len(parts) > 1:
        parts = [a + b for a, b in zip(parts[::2], parts[1::2])]
    return parts[0]


def folded(ref, *lead):
    return tree([ref[(*lead, pl.ds(part, LEV, stride=SUB), slice(None))] for part in range(SUB)])


def early_kernel(crm_hbm, gcm, number, state, means, partial, crm, sums, arrival):
    loads = [
        pltpu.make_async_copy(
            crm_hbm.at[f, pl.ds(part * CRM_CHUNK, CRM_CHUNK)],
            crm.at[f, pl.ds(part * CRM_CHUNK, CRM_CHUNK)],
            arrival.at[f, part],
        )
        for f in range(2)
        for part in range(LEV // CRM_CHUNK)
    ]
    for copy in loads:
        copy.start()
    lane = lax.broadcasted_iota(jnp.int32, (FIELDS * LEV, LANES), 1)
    own = [rows_of(gcm, 0), rows_of(gcm, 1)]
    for y in range(2):
        before = jnp.where(lane == 0, 0.0, pltpu.roll(own[y], 1, axis=1))
        after = jnp.where(lane == LANES - 1, 0.0, pltpu.roll(own[y], LANES - 1, axis=1))
        around = own[1 - y] + after + before
        partial[y] = own[y] + number[...] * (around - 4.0 * own[y])

    for f, (scale, shift) in enumerate([(ALPHA, SHIFT), (BETA, 0.0)]):
        for part in range(LEV // CRM_CHUNK):
            loads[f * (LEV // CRM_CHUNK) + part].wait()

            def level(n, carry):
                k = part * CRM_CHUNK + n
                for half in range(2):
                    x = crm[f, k, :, half * LANES : (half + 1) * LANES].astype(jnp.float32)
                    x = x * scale + shift
                    total = None
                    for row in range(SUB):
                        block = x[row * INNER : (row + 1) * INNER]
                        state[f, half, pl.ds(k * NXC + row, INNER, stride=SUB), :] = block
                        total = block if total is None else total + block
                    sums[f, half, pl.ds(pl.multiple_of(k * SUB, SUB), SUB), :] = total
                return carry

            lax.fori_loop(0, CRM_CHUNK, level, 0, unroll=4)
    for f in range(2):
        for half in range(2):
            means[f, half] = folded(sums, f, half) * (1.0 / NXC)


def column_values(state, rate):
    level = lax.broadcasted_iota(jnp.int32, (LEV, LANES), 0)
    field = [state[f * LEV : (f + 1) * LEV] for f in range(FIELDS)]
    warm = ALPHA * (0.25 * field[0] + 0.2 * field[4])
    wet = BETA * (0.25 * field[1] + 0.2 * field[5])
    drift = 0.45 * jnp.tanh(field[2])
    tilt = jnp.tanh(field[3])
    rise = 0.15 * (tilt + pltpu.roll(tilt, LEV - 1, axis=0))
    rise = jnp.where(level == LEV - 1, rate, rise)
    return jnp.concatenate([warm, wet, drift, rise], axis=0)


def placed(values, routes, slot, y):
    route = routes[slot, :, pl.ds(pl.multiple_of(y * LANES, LANES), LANES)]
    return select_dot(values, route, ((1,), (1,)), False)


def inner_kernel(
    partial, number, core_mate, other, chip_mate, routes, rates, outer, done, advanced
):
    lane = lax.broadcasted_iota(jnp.int32, (FIELDS * LEV, LANES), 1)
    core = lax.rem(lax.axis_index("blk"), 2)

    def columns(ref):
        turned = jnp.transpose(ref)
        column = jnp.concatenate([turned[:, n : n + 1] for n in range(GCM_ROWS // LANES)], axis=0)
        return column[: FIELDS * LEV], column[FIELDS * LEV :]

    even = lax.rem(lax.axis_index("sub"), 2) == 0
    near, far = chip_mate[...], other[...]
    west, east = columns(jnp.where(even, far, near)), columns(jnp.where(even, near, far))
    rows = []
    for y in range(2):
        side = jnp.where(lane == 0, west[y], jnp.where(lane == LANES - 1, east[y], 0.0))
        rows.append(partial[y] + number[...] * side)
    outer[...] = jnp.where(core == 0, rows[0], rows[1])
    state = jnp.where(core == 0, rows[1], rows[0]) + number[...] * core_mate[...]
    advanced[...] = state[2 * LEV :]
    values = column_values(state, rates[pl.ds(1 - core, 1), :])
    for slot in range(2):
        done[slot] = placed(values, routes, slot, 1 - core)


def outer_kernel(
    outer, number, neighbour, routes, rates, done, inner_advanced, advanced, outgoing
):
    core = lax.rem(lax.axis_index("blk"), 2)
    state = outer[...] + number[...] * neighbour[: FIELDS * LEV, :]
    here, there = state[2 * LEV :], inner_advanced[...]
    advanced[pl.ds(0, 4 * LEV, stride=2), :] = jnp.where(core == 0, here, there)
    advanced[pl.ds(1, 4 * LEV, stride=2), :] = jnp.where(core == 0, there, here)
    values = column_values(state, rates[pl.ds(core, 1), :])
    for slot in range(2):
        outgoing[pl.ds(slot, DEVICES, stride=2), :] = done[slot] + placed(
            values, routes, slot, core
        )


def cloud_kernel(
    incoming, start, means, advanced, outgoing, gcm_next,
    state, coef, mean, total, square, departure,
):
    leaving = pltpu.make_async_copy(
        advanced, gcm_next.at[pl.ds(2 * 2 * LEV, 4 * 2 * LEV)], departure
    )
    leaving.start()
    level = lax.broadcasted_iota(jnp.int32, (LEV, LANES), 0)
    top = level == LEV - 1
    rates = []

    def up(x):
        return pltpu.roll(x, LEV - 1, axis=0)

    def down(x):
        return pltpu.roll(x, 1, axis=0)

    for half in range(2):
        values = jnp.transpose(incoming[half * LANES : (half + 1) * LANES, :])
        rise = values[3 * LEV :]
        rates.append(rise[LEV - 1 :])
        rise = jnp.where(top, 0.0, rise)
        base = SHIFT * (1.0 - rise + down(rise))
        coef[0, half] = values[:LEV] + SHIFT - 0.75 * base
        coef[1, half] = values[LEV : 2 * LEV]
        coef[2, half] = values[2 * LEV : 3 * LEV]
        coef[3, half] = rise
        coef[7, half] = jnp.broadcast_to(rates[half], (LEV, LANES))
        coef[9, half] = jnp.abs(coef[2, half])

    def lifted(x, rise):
        flux = rise * jnp.where(rise > 0.0, x, up(x))
        return x - flux + down(flux)

    def settled(half):
        rain = folded(total, half) * (1.0 / NXC) + coef[8, half]
        return mean[0, half] + rain, mean[1, half] - rain, mean[2, half] + rain

    def relax(first):
        for half in range(2):
            rise, rate = coef[3, half], coef[7, half]
            if first:
                before = means[0, half], means[1, half]
                mean[2, half] = jnp.zeros((LEV, LANES), jnp.float32)
            else:
                *before, mean[2, half] = settled(half)
            now = [lifted(x, rise) for x in before]
            add = [coef[f, half] - 0.25 * now[f] for f in range(2)]
            offset = add[1]
            if first:
                coef[4, half] = add[0]
            else:
                kept = lifted(mean[3, half], rise)
                owed = rate * kept
                offset = offset + (kept - owed)
                coef[4, half] = add[0] + owed
            mean[3, half] = offset
            coef[5, half] = -offset
            lacking = rate * offset
            coef[8, half] = lacking
            mean[0, half] = now[0] + add[0]
            mean[1, half] = now[1] + add[1]
            coef[6, half] = now[0] + add[0] - lacking

    def sweep(source, half, last):
        rate = jnp.broadcast_to(coef[7, half, 0:1, :], (SUB, LANES))

        def row(index, k):
            return jnp.broadcast_to(coef[index, half, k : k + 1, :], (SUB, LANES))

        def drifted(f, k, size, positive):
            cells = [
                source[f, half, k * NXC + j * SUB : k * NXC + (j + 1) * SUB, :]
                for j in range(INNER)
            ]
            before = [pltpu.roll(cells[-1], 1, axis=0)] + cells[:-1]
            after = cells[1:] + [pltpu.roll(cells[0], SUB - 1, axis=0)]
            return [
                c + size * (jnp.where(positive, b, a) - c)
                for c, b, a in zip(cells, before, after)
            ]

        def level_of(k):
            drift = row(2, k)
            size, positive = row(9, k), drift > 0.0
            return [drifted(f, k, size, positive) for f in range(2)]

        now = level_of(0)
        below = None
        for k in range(LEV):
            gain, least = row(4, k), row(5, k)
            if k < LEV - 1:
                after = level_of(k + 1)
                rise = row(3, k)
                upward = rise > 0.0
                flux = [
                    [rise * jnp.where(upward, a, b) for a, b in zip(now[f], after[f])]
                    for f in range(2)
                ]
            rained, spread = [], []
            if last:
                middle = row(6, k)
            for j in range(INNER):
                new = []
                for f in range(2):
                    x = now[f][j]
                    if k < LEV - 1:
                        x = x - flux[f][j]
                    if k > 0:
                        x = x + below[f][j]
                    new.append(x)
                temper, moisture = new
                temper = temper + gain
                rain = rate * jnp.maximum(moisture - jnp.exp2(temper), least)
                temper = temper + rain
                rained.append(rain)
                if last:
                    away = temper - middle
                    spread.append(away * away)
                else:
                    at = slice(k * NXC + j * SUB, k * NXC + (j + 1) * SUB)
                    state[0, half, at, :] = temper
                    state[1, half, at, :] = moisture - rain
            total[half, k * SUB : (k + 1) * SUB, :] = tree(rained)
            if last:
                square[half, k * SUB : (k + 1) * SUB, :] = tree(spread)
            if k < LEV - 1:
                below, now = flux, after

    def substep(source, first, last):
        relax(first)

        def half_of(half, carry):
            sweep(source, half, last)
            return carry

        lax.fori_loop(0, 2, half_of, 0)

    substep(start, True, False)

    def middle_step(step, carry):
        substep(state, False, False)
        return carry

    lax.fori_loop(0, SUBSTEPS - 2, middle_step, 0)
    substep(state, False, True)
    for half in range(2):
        warm, wet, rain = settled(half)
        gap = warm - coef[6, half] - coef[8, half]
        spread = folded(square, half) * (1.0 / NXC) - gap * gap
        result = [
            (warm - SHIFT) * (1.0 / ALPHA),
            wet * (1.0 / BETA),
            rain * (1.0 / BETA),
            spread * (1.0 / (ALPHA * ALPHA)),
        ]
        outgoing[half * LANES : (half + 1) * LANES, :] = jnp.transpose(
            jnp.concatenate(result, axis=0)
        )
    leaving.wait()


def home_kernel(returned, routes, begun, gcm_next, stats):
    del begun
    home = None
    for slot in range(2):
        back = returned[pl.ds(slot, DEVICES, stride=2), :]
        term = select_dot(jnp.transpose(back), routes[slot], ((1,), (0,)), True)
        home = term if home is None else home + term
    for y in range(2):
        part = home[:, y * LANES : (y + 1) * LANES]
        gcm_next[pl.ds(y, 2 * LEV, stride=2), :] = part[: 2 * LEV]
        stats[pl.ds(y, 2 * LEV, stride=2), :] = part[2 * LEV :]


def whole(shape):
    return pl.BlockSpec(shape, lambda *_: (0,) * len(shape))


def f32(*shape):
    return jax.ShapeDtypeStruct(shape, jnp.float32)


def in_hbm(x):
    return pltpu.with_memory_space_constraint(x, pltpu.HBM)


def transfer(rows):
    moved = lax.all_to_all(
        rows.reshape(DEVICES, 2, LANES), ("blk", "sub"), split_axis=0, concat_axis=0, tiled=True
    )
    return moved.reshape(COLS, LANES)


def body(gcm_state, crm_state, owner, branch, diffusion):
    gcm = gcm_state.reshape(GCM_ROWS, LANES)

    def pairs(n, first):
        ahead = [(i, (i + 1) % n) for i in range(first, n, 2)]
        return ahead + [(j, i) for i, j in ahead]

    n_blk, n_sub = lax.axis_size("blk"), lax.axis_size("sub")
    hbm = pl.BlockSpec(memory_space=pltpu.HBM)
    gcm_here, to_neighbour, owner_here, branch_here, diffusion_here = pl.pallas_call(
        load_kernel,
        in_specs=[hbm] * 4,
        out_shape=(
            f32(GCM_ROWS, LANES),
            f32(FIELDS * LEV + SUB, LANES),
            jax.ShapeDtypeStruct(owner.shape, owner.dtype),
            jax.ShapeDtypeStruct(branch.shape, branch.dtype),
            f32(*diffusion.shape),
        ),
        scratch_shapes=[pltpu.SemaphoreType.DMA((4,))],
        compiler_params=pltpu.CompilerParams(vmem_limit_bytes=4 * MIB),
        name="load",
    )(*map(in_hbm, (gcm, owner, branch, diffusion)))
    neighbour = lax.ppermute(to_neighbour, "blk", pairs(n_blk, 1))
    to_core_mate, to_chip_mate, to_other, routes, rates, number = pl.pallas_call(
        edge_kernel,
        out_shape=(
            f32(FIELDS * LEV, LANES),
            f32(SUB, LANES),
            f32(SUB, LANES),
            jax.ShapeDtypeStruct((2, DEVICES, COLS), jnp.bfloat16),
            f32(2, LANES),
            f32(FIELDS * LEV, LANES),
        ),
        compiler_params=pltpu.CompilerParams(vmem_limit_bytes=4 * MIB),
        name="edges",
    )(gcm_here, owner_here, branch_here, diffusion_here)
    chip_mate = lax.ppermute(to_chip_mate, "sub", pairs(n_sub, 0))
    other = lax.ppermute(to_other, "sub", pairs(n_sub, 1))
    core_mate = lax.ppermute(to_core_mate, "blk", pairs(n_blk, 0))
    cells = 2 * LEV * NXC * COLS
    state, means, partial = pl.pallas_call(
        early_kernel,
        in_specs=[hbm, whole((GCM_ROWS, LANES)), whole((FIELDS * LEV, LANES))],
        out_shape=(
            f32(2, 2, LEV * NXC, LANES),
            f32(2, 2, LEV, LANES),
            f32(2, FIELDS * LEV, LANES),
        ),
        scratch_shapes=[
            pltpu.VMEM((2, LEV, NXC, COLS), jnp.bfloat16),
            pltpu.VMEM((2, 2, LEV * SUB, LANES), jnp.float32),
            pltpu.SemaphoreType.DMA((2, LEV // CRM_CHUNK)),
        ],
        compiler_params=pltpu.CompilerParams(vmem_limit_bytes=16 * MIB),
        cost_estimate=pl.CostEstimate(flops=4 * cells, bytes_accessed=6 * cells, transcendentals=0),
        name="early",
    )(in_hbm(crm_state), gcm_here, number)
    outer, done, inner_advanced = pl.pallas_call(
        inner_kernel,
        out_shape=(
            f32(FIELDS * LEV, LANES),
            f32(2, DEVICES, LANES),
            f32(4 * LEV, LANES),
        ),
        compiler_params=pltpu.CompilerParams(vmem_limit_bytes=8 * MIB),
        name="inner",
    )(partial, number, core_mate, other, chip_mate, routes, rates)
    advanced, outgoing = pl.pallas_call(
        outer_kernel,
        out_shape=(f32(4 * 2 * LEV, LANES), f32(COLS, LANES)),
        compiler_params=pltpu.CompilerParams(vmem_limit_bytes=8 * MIB),
        name="outer",
    )(outer, number, neighbour, routes, rates, done, inner_advanced)

    incoming = transfer(outgoing)
    profiles, gcm_next = pl.pallas_call(
        cloud_kernel,
        out_specs=(whole((COLS, LANES)), hbm),
        out_shape=(f32(COLS, LANES), f32(GCM_ROWS, LANES)),
        scratch_shapes=[
            pltpu.VMEM((2, 2, LEV * NXC, LANES), jnp.float32),
            pltpu.VMEM((10, 2, LEV, LANES), jnp.float32),
            pltpu.VMEM((4, 2, LEV, LANES), jnp.float32),
            pltpu.VMEM((2, LEV * SUB, LANES), jnp.float32),
            pltpu.VMEM((2, LEV * SUB, LANES), jnp.float32),
            pltpu.SemaphoreType.DMA(()),
        ],
        compiler_params=pltpu.CompilerParams(vmem_limit_bytes=12 * MIB),
        name="cloud",
    )(incoming, state, means, advanced)
    returned = transfer(profiles)

    gcm_next, stats = pl.pallas_call(
        home_kernel,
        grid=(1,),
        in_specs=[
            whole((COLS, LANES)),
            whole((2, DEVICES, COLS)),
            pl.BlockSpec(memory_space=pl.ANY),
        ],
        out_specs=(whole((4 * LEV, LANES)), whole((4 * LEV, LANES))),
        out_shape=(f32(GCM_ROWS, LANES), f32(4 * LEV, LANES)),
        input_output_aliases={2: 0},
        compiler_params=pltpu.CompilerParams(vmem_limit_bytes=8 * MIB),
        name="home",
    )(returned, routes, gcm_next)
    return gcm_next.reshape(gcm_state.shape), stats.reshape(2, LEV, 2, LANES)


def solution(mesh):
    grid = P(None, None, "blk", "sub")
    return jax.shard_map(
        body,
        mesh=mesh,
        in_specs=(grid, P(None, None, None, ("blk", "sub")), P("blk", "sub"), P("blk", "sub"), P()),
        out_specs=(grid, grid),
        check_vma=False,
    )
```

```python
import math

import jax
import jax.numpy as jnp
from jax import lax
from jax.experimental import pallas as pl
from jax.experimental.pallas import tpu as pltpu
from jax.sharding import PartitionSpec as P

SUBSTEPS = 4
LEV = 32
NXC = 64
LANES = 128
DEVICES = 128
COLS = 256
FIELDS = 6
SUB = 8
INNER = NXC // SUB
GCM_ROWS = FIELDS * LEV * 2
CRM_CHUNK = 8
ALPHA = 0.3 * math.log2(math.e)
BETA = 1.5 * ALPHA
SHIFT = math.log2(0.5 * BETA)
MIB = 1 << 20


def pieces(x):
    first = x.astype(jnp.bfloat16)
    rest = x - first.astype(jnp.float32)
    second = rest.astype(jnp.bfloat16)
    third = (rest - second.astype(jnp.float32)).astype(jnp.bfloat16)
    return first, second, third


def select_dot(x, chosen, dims, x_first):
    total = None
    for part in pieces(x):
        pair = (part, chosen) if x_first else (chosen, part)
        term = lax.dot_general(*pair, (dims, ((), ())), preferred_element_type=jnp.float32)
        total = term if total is None else total + term
    return total


def rows_of(ref, y):
    return ref[pl.ds(y, FIELDS * LEV, stride=2), :]


def load_kernel(
    gcm_hbm, owner_hbm, branch_hbm, diffusion_hbm,
    gcm, to_neighbour, owner, branch, diffusion, arrival,
):
    step = GCM_ROWS // FIELDS
    pairs = [
        (gcm_hbm.at[pl.ds(f * step, step)], gcm.at[pl.ds(f * step, step)]) for f in range(FIELDS)
    ]
    pairs += [(owner_hbm, owner), (branch_hbm, branch), (diffusion_hbm, diffusion)]
    loads = [
        pltpu.make_async_copy(source, target, arrival.at[n])
        for n, (source, target) in enumerate(pairs)
    ]
    for copy in loads:
        copy.start()
    for copy in loads:
        copy.wait()
    core = lax.rem(lax.axis_index("blk"), 2)
    to_neighbour[: FIELDS * LEV, :] = jnp.where(core == 0, rows_of(gcm, 0), rows_of(gcm, 1))
    to_neighbour[FIELDS * LEV :, :] = jnp.zeros((SUB, LANES), jnp.float32)


def edge_kernel(
    gcm, owner, branch, diffusion,
    to_core_mate, to_chip_mate, to_other, routes, rates, number,
):
    to_chip_mate[...] = jnp.zeros_like(to_chip_mate)
    to_other[...] = jnp.zeros_like(to_other)
    device = lax.broadcasted_iota(jnp.int32, (DEVICES, LANES), 0)
    target = jnp.concatenate(
        [(device == owner[y : y + 1, :]).astype(jnp.float32) for y in range(2)], axis=1
    )
    earlier = (
        lax.broadcasted_iota(jnp.int32, (COLS, COLS), 0)
        < lax.broadcasted_iota(jnp.int32, (COLS, COLS), 1)
    ).astype(jnp.bfloat16)
    count = jnp.dot(target.astype(jnp.bfloat16), earlier, preferred_element_type=jnp.float32)
    for slot in range(2):
        here = jnp.where(count < 0.5, 1.0 - slot, 0.0 + slot)
        routes[slot] = (target * here).astype(jnp.bfloat16)
    rates[...] = jnp.where(branch[...] == 1, 0.6, 0.2)
    for f in range(FIELDS):
        spread = jnp.broadcast_to(diffusion[f : f + 1, :], (LANES, LEV))
        number[f * LEV : (f + 1) * LEV, :] = jnp.transpose(spread)

    even = lax.rem(lax.axis_index("sub"), 2) == 0
    pair = [rows_of(gcm, 0), rows_of(gcm, 1)]
    core = lax.rem(lax.axis_index("blk"), 2)
    to_core_mate[...] = jnp.where(core == 0, pair[1], pair[0])
    rows = jnp.concatenate(pair, axis=0)
    for part in range(GCM_ROWS // LANES):
        turned = jnp.transpose(rows[part * LANES : (part + 1) * LANES])
        first, last = turned[:1], turned[LANES - 1 :]
        to_chip_mate[part : part + 1, :] = jnp.where(even, last, first)
        to_other[part : part + 1, :] = jnp.where(even, first, last)


def tree(parts):
    while len(parts) > 1:
        parts = [a + b for a, b in zip(parts[::2], parts[1::2])]
    return parts[0]


def folded(ref, *lead):
    return tree([ref[(*lead, pl.ds(part, LEV, stride=SUB), slice(None))] for part in range(SUB)])


def early_kernel(crm_hbm, gcm, number, state, means, partial, crm, sums, arrival):
    loads = [
        pltpu.make_async_copy(
            crm_hbm.at[f, pl.ds(part * CRM_CHUNK, CRM_CHUNK)],
            crm.at[f, pl.ds(part * CRM_CHUNK, CRM_CHUNK)],
            arrival.at[f, part],
        )
        for f in range(2)
        for part in range(LEV // CRM_CHUNK)
    ]
    for copy in loads:
        copy.start()
    lane = lax.broadcasted_iota(jnp.int32, (FIELDS * LEV, LANES), 1)
    own = [rows_of(gcm, 0), rows_of(gcm, 1)]
    for y in range(2):
        before = jnp.where(lane == 0, 0.0, pltpu.roll(own[y], 1, axis=1))
        after = jnp.where(lane == LANES - 1, 0.0, pltpu.roll(own[y], LANES - 1, axis=1))
        around = own[1 - y] + after + before
        partial[y] = own[y] + number[...] * (around - 4.0 * own[y])

    for f, (scale, shift) in enumerate([(ALPHA, SHIFT), (BETA, 0.0)]):
        for part in range(LEV // CRM_CHUNK):
            loads[f * (LEV // CRM_CHUNK) + part].wait()

            def level(n, carry):
                k = part * CRM_CHUNK + n
                for half in range(2):
                    x = crm[f, k, :, half * LANES : (half + 1) * LANES].astype(jnp.float32)
                    x = x * scale + shift
                    total = None
                    for row in range(SUB):
                        block = x[row * INNER : (row + 1) * INNER]
                        state[f, half, pl.ds(k * NXC + row, INNER, stride=SUB), :] = block
                        total = block if total is None else total + block
                    sums[f, half, pl.ds(pl.multiple_of(k * SUB, SUB), SUB), :] = total
                return carry

            lax.fori_loop(0, CRM_CHUNK, level, 0, unroll=4)
    for f in range(2):
        for half in range(2):
            means[f, half] = folded(sums, f, half) * (1.0 / NXC)


def column_values(state, rate):
    level = lax.broadcasted_iota(jnp.int32, (LEV, LANES), 0)
    field = [state[f * LEV : (f + 1) * LEV] for f in range(FIELDS)]
    warm = ALPHA * (0.25 * field[0] + 0.2 * field[4])
    wet = BETA * (0.25 * field[1] + 0.2 * field[5])
    drift = 0.45 * jnp.tanh(field[2])
    tilt = jnp.tanh(field[3])
    rise = 0.15 * (tilt + pltpu.roll(tilt, LEV - 1, axis=0))
    rise = jnp.where(level == LEV - 1, rate, rise)
    return jnp.concatenate([warm, wet, drift, rise], axis=0)


def placed(values, routes, slot, y):
    route = routes[slot, :, pl.ds(pl.multiple_of(y * LANES, LANES), LANES)]
    return select_dot(values, route, ((1,), (1,)), False)


def inner_kernel(
    partial, number, core_mate, other, chip_mate, routes, rates, outer, done, advanced
):
    lane = lax.broadcasted_iota(jnp.int32, (FIELDS * LEV, LANES), 1)
    core = lax.rem(lax.axis_index("blk"), 2)

    def columns(ref):
        turned = jnp.transpose(ref)
        column = jnp.concatenate([turned[:, n : n + 1] for n in range(GCM_ROWS // LANES)], axis=0)
        return column[: FIELDS * LEV], column[FIELDS * LEV :]

    even = lax.rem(lax.axis_index("sub"), 2) == 0
    near, far = chip_mate[...], other[...]
    west, east = columns(jnp.where(even, far, near)), columns(jnp.where(even, near, far))
    rows = []
    for y in range(2):
        side = jnp.where(lane == 0, west[y], jnp.where(lane == LANES - 1, east[y], 0.0))
        rows.append(partial[y] + number[...] * side)
    outer[...] = jnp.where(core == 0, rows[0], rows[1])
    state = jnp.where(core == 0, rows[1], rows[0]) + number[...] * core_mate[...]
    advanced[...] = state[2 * LEV :]
    values = column_values(state, rates[pl.ds(1 - core, 1), :])
    for slot in range(2):
        done[slot] = placed(values, routes, slot, 1 - core)


def outer_kernel(
    outer, number, neighbour, routes, rates, done, inner_advanced, advanced, outgoing
):
    core = lax.rem(lax.axis_index("blk"), 2)
    state = outer[...] + number[...] * neighbour[: FIELDS * LEV, :]
    here, there = state[2 * LEV :], inner_advanced[...]
    advanced[pl.ds(0, 4 * LEV, stride=2), :] = jnp.where(core == 0, here, there)
    advanced[pl.ds(1, 4 * LEV, stride=2), :] = jnp.where(core == 0, there, here)
    values = column_values(state, rates[pl.ds(core, 1), :])
    for slot in range(2):
        outgoing[pl.ds(slot, DEVICES, stride=2), :] = done[slot] + placed(
            values, routes, slot, core
        )


def cloud_kernel(
    incoming, start, means, advanced, outgoing, gcm_next,
    state, coef, mean, total, square, departure,
):
    leaving = pltpu.make_async_copy(
        advanced, gcm_next.at[pl.ds(2 * 2 * LEV, 4 * 2 * LEV)], departure
    )
    leaving.start()
    level = lax.broadcasted_iota(jnp.int32, (LEV, LANES), 0)
    top = level == LEV - 1
    rates = []

    def up(x):
        return pltpu.roll(x, LEV - 1, axis=0)

    def down(x):
        return pltpu.roll(x, 1, axis=0)

    for half in range(2):
        values = jnp.transpose(incoming[half * LANES : (half + 1) * LANES, :])
        rise = values[3 * LEV :]
        rates.append(rise[LEV - 1 :])
        rise = jnp.where(top, 0.0, rise)
        base = SHIFT * (1.0 - rise + down(rise))
        coef[0, half] = values[:LEV] + SHIFT - 0.75 * base
        coef[1, half] = values[LEV : 2 * LEV]
        coef[2, half] = values[2 * LEV : 3 * LEV]
        coef[3, half] = rise
        coef[7, half] = jnp.broadcast_to(rates[half], (LEV, LANES))
        coef[9, half] = jnp.abs(coef[2, half])

    def lifted(x, rise):
        flux = rise * jnp.where(rise > 0.0, x, up(x))
        return x - flux + down(flux)

    def settled(half):
        rain = folded(total, half) * (1.0 / NXC) + coef[8, half]
        return mean[0, half] + rain, mean[1, half] - rain, mean[2, half] + rain

    def relax(first):
        for half in range(2):
            rise, rate = coef[3, half], coef[7, half]
            if first:
                before = means[0, half], means[1, half]
                mean[2, half] = jnp.zeros((LEV, LANES), jnp.float32)
            else:
                *before, mean[2, half] = settled(half)
            now = [lifted(x, rise) for x in before]
            add = [coef[f, half] - 0.25 * now[f] for f in range(2)]
            offset = add[1]
            if first:
                coef[4, half] = add[0]
            else:
                kept = lifted(mean[3, half], rise)
                owed = rate * kept
                offset = offset + (kept - owed)
                coef[4, half] = add[0] + owed
            mean[3, half] = offset
            coef[5, half] = -offset
            lacking = rate * offset
            coef[8, half] = lacking
            mean[0, half] = now[0] + add[0]
            mean[1, half] = now[1] + add[1]
            coef[6, half] = now[0] + add[0] - lacking

    def sweep(source, half, last):
        rate = jnp.broadcast_to(coef[7, half, 0:1, :], (SUB, LANES))

        def row(index, k):
            return jnp.broadcast_to(coef[index, half, k : k + 1, :], (SUB, LANES))

        def drifted(f, k, size, positive):
            cells = [
                source[f, half, k * NXC + j * SUB : k * NXC + (j + 1) * SUB, :]
                for j in range(INNER)
            ]
            before = [pltpu.roll(cells[-1], 1, axis=0)] + cells[:-1]
            after = cells[1:] + [pltpu.roll(cells[0], SUB - 1, axis=0)]
            return [
                c + size * (jnp.where(positive, b, a) - c)
                for c, b, a in zip(cells, before, after)
            ]

        def level_of(k):
            drift = row(2, k)
            size, positive = row(9, k), drift > 0.0
            return [drifted(f, k, size, positive) for f in range(2)]

        now = level_of(0)
        below = None
        for k in range(LEV):
            gain, least = row(4, k), row(5, k)
            if k < LEV - 1:
                after = level_of(k + 1)
                rise = row(3, k)
                upward = rise > 0.0
                flux = [
                    [rise * jnp.where(upward, a, b) for a, b in zip(now[f], after[f])]
                    for f in range(2)
                ]
            rained, spread = [], []
            if last:
                middle = row(6, k)
            for j in range(INNER):
                new = []
                for f in range(2):
                    x = now[f][j]
                    if k < LEV - 1:
                        x = x - flux[f][j]
                    if k > 0:
                        x = x + below[f][j]
                    new.append(x)
                temper, moisture = new
                temper = temper + gain
                rain = rate * jnp.maximum(moisture - jnp.exp2(temper), least)
                temper = temper + rain
                rained.append(rain)
                if last:
                    away = temper - middle
                    spread.append(away * away)
                else:
                    at = slice(k * NXC + j * SUB, k * NXC + (j + 1) * SUB)
                    state[0, half, at, :] = temper
                    state[1, half, at, :] = moisture - rain
            total[half, k * SUB : (k + 1) * SUB, :] = tree(rained)
            if last:
                square[half, k * SUB : (k + 1) * SUB, :] = tree(spread)
            if k < LEV - 1:
                below, now = flux, after

    def substep(source, first, last):
        relax(first)

        def half_of(half, carry):
            sweep(source, half, last)
            return carry

        lax.fori_loop(0, 2, half_of, 0)

    substep(start, True, False)

    def middle_step(step, carry):
        substep(state, False, False)
        return carry

    lax.fori_loop(0, SUBSTEPS - 2, middle_step, 0)
    substep(state, False, True)
    for half in range(2):
        warm, wet, rain = settled(half)
        gap = warm - coef[6, half] - coef[8, half]
        spread = folded(square, half) * (1.0 / NXC) - gap * gap
        result = [
            (warm - SHIFT) * (1.0 / ALPHA),
            wet * (1.0 / BETA),
            rain * (1.0 / BETA),
            spread * (1.0 / (ALPHA * ALPHA)),
        ]
        outgoing[half * LANES : (half + 1) * LANES, :] = jnp.transpose(
            jnp.concatenate(result, axis=0)
        )
    leaving.wait()


def home_kernel(returned, routes, begun, gcm_next, stats):
    del begun
    home = None
    for slot in range(2):
        back = returned[pl.ds(slot, DEVICES, stride=2), :]
        term = select_dot(jnp.transpose(back), routes[slot], ((1,), (0,)), True)
        home = term if home is None else home + term
    for y in range(2):
        part = home[:, y * LANES : (y + 1) * LANES]
        gcm_next[pl.ds(y, 2 * LEV, stride=2), :] = part[: 2 * LEV]
        stats[pl.ds(y, 2 * LEV, stride=2), :] = part[2 * LEV :]


def whole(shape):
    return pl.BlockSpec(shape, lambda *_: (0,) * len(shape))


def f32(*shape):
    return jax.ShapeDtypeStruct(shape, jnp.float32)


def in_hbm(x):
    return pltpu.with_memory_space_constraint(x, pltpu.HBM)


def transfer(rows):
    moved = lax.all_to_all(
        rows.reshape(DEVICES, 2, LANES), ("blk", "sub"), split_axis=0, concat_axis=0, tiled=True
    )
    return moved.reshape(COLS, LANES)


def body(gcm_state, crm_state, owner, branch, diffusion):
    gcm = gcm_state.reshape(GCM_ROWS, LANES)

    def pairs(n, first):
        ahead = [(i, (i + 1) % n) for i in range(first, n, 2)]
        return ahead + [(j, i) for i, j in ahead]

    n_blk, n_sub = lax.axis_size("blk"), lax.axis_size("sub")
    hbm = pl.BlockSpec(memory_space=pltpu.HBM)
    gcm_here, to_neighbour, owner_here, branch_here, diffusion_here = pl.pallas_call(
        load_kernel,
        in_specs=[hbm] * 4,
        out_shape=(
            f32(GCM_ROWS, LANES),
            f32(FIELDS * LEV + SUB, LANES),
            jax.ShapeDtypeStruct(owner.shape, owner.dtype),
            jax.ShapeDtypeStruct(branch.shape, branch.dtype),
            f32(*diffusion.shape),
        ),
        scratch_shapes=[pltpu.SemaphoreType.DMA((FIELDS + 3,))],
        compiler_params=pltpu.CompilerParams(vmem_limit_bytes=4 * MIB),
        name="load",
    )(*map(in_hbm, (gcm, owner, branch, diffusion)))
    neighbour = lax.ppermute(to_neighbour, "blk", pairs(n_blk, 1))
    to_core_mate, to_chip_mate, to_other, routes, rates, number = pl.pallas_call(
        edge_kernel,
        out_shape=(
            f32(FIELDS * LEV, LANES),
            f32(SUB, LANES),
            f32(SUB, LANES),
            jax.ShapeDtypeStruct((2, DEVICES, COLS), jnp.bfloat16),
            f32(2, LANES),
            f32(FIELDS * LEV, LANES),
        ),
        compiler_params=pltpu.CompilerParams(vmem_limit_bytes=4 * MIB),
        name="edges",
    )(gcm_here, owner_here, branch_here, diffusion_here)
    chip_mate = lax.ppermute(to_chip_mate, "sub", pairs(n_sub, 0))
    other = lax.ppermute(to_other, "sub", pairs(n_sub, 1))
    core_mate = lax.ppermute(to_core_mate, "blk", pairs(n_blk, 0))
    cells = 2 * LEV * NXC * COLS
    state, means, partial = pl.pallas_call(
        early_kernel,
        in_specs=[hbm, whole((GCM_ROWS, LANES)), whole((FIELDS * LEV, LANES))],
        out_shape=(
            f32(2, 2, LEV * NXC, LANES),
            f32(2, 2, LEV, LANES),
            f32(2, FIELDS * LEV, LANES),
        ),
        scratch_shapes=[
            pltpu.VMEM((2, LEV, NXC, COLS), jnp.bfloat16),
            pltpu.VMEM((2, 2, LEV * SUB, LANES), jnp.float32),
            pltpu.SemaphoreType.DMA((2, LEV // CRM_CHUNK)),
        ],
        compiler_params=pltpu.CompilerParams(vmem_limit_bytes=16 * MIB),
        cost_estimate=pl.CostEstimate(flops=4 * cells, bytes_accessed=6 * cells, transcendentals=0),
        name="early",
    )(in_hbm(crm_state), gcm_here, number)
    outer, done, inner_advanced = pl.pallas_call(
        inner_kernel,
        out_shape=(
            f32(FIELDS * LEV, LANES),
            f32(2, DEVICES, LANES),
            f32(4 * LEV, LANES),
        ),
        compiler_params=pltpu.CompilerParams(vmem_limit_bytes=8 * MIB),
        name="inner",
    )(partial, number, core_mate, other, chip_mate, routes, rates)
    advanced, outgoing = pl.pallas_call(
        outer_kernel,
        out_shape=(f32(4 * 2 * LEV, LANES), f32(COLS, LANES)),
        compiler_params=pltpu.CompilerParams(vmem_limit_bytes=8 * MIB),
        name="outer",
    )(outer, number, neighbour, routes, rates, done, inner_advanced)

    incoming = transfer(outgoing)
    profiles, gcm_next = pl.pallas_call(
        cloud_kernel,
        out_specs=(whole((COLS, LANES)), hbm),
        out_shape=(f32(COLS, LANES), f32(GCM_ROWS, LANES)),
        scratch_shapes=[
            pltpu.VMEM((2, 2, LEV * NXC, LANES), jnp.float32),
            pltpu.VMEM((10, 2, LEV, LANES), jnp.float32),
            pltpu.VMEM((4, 2, LEV, LANES), jnp.float32),
            pltpu.VMEM((2, LEV * SUB, LANES), jnp.float32),
            pltpu.VMEM((2, LEV * SUB, LANES), jnp.float32),
            pltpu.SemaphoreType.DMA(()),
        ],
        compiler_params=pltpu.CompilerParams(vmem_limit_bytes=12 * MIB),
        name="cloud",
    )(incoming, state, means, advanced)
    returned = transfer(profiles)

    gcm_next, stats = pl.pallas_call(
        home_kernel,
        grid=(1,),
        in_specs=[
            whole((COLS, LANES)),
            whole((2, DEVICES, COLS)),
            pl.BlockSpec(memory_space=pl.ANY),
        ],
        out_specs=(whole((4 * LEV, LANES)), whole((4 * LEV, LANES))),
        out_shape=(f32(GCM_ROWS, LANES), f32(4 * LEV, LANES)),
        input_output_aliases={2: 0},
        compiler_params=pltpu.CompilerParams(vmem_limit_bytes=8 * MIB),
        name="home",
    )(returned, routes, gcm_next)
    return gcm_next.reshape(gcm_state.shape), stats.reshape(2, LEV, 2, LANES)


def solution(mesh):
    grid = P(None, None, "blk", "sub")
    return jax.shard_map(
        body,
        mesh=mesh,
        in_specs=(grid, P(None, None, None, ("blk", "sub")), P("blk", "sub"), P("blk", "sub"), P()),
        out_specs=(grid, grid),
        check_vma=False,
    )
```

```python
import math

import jax
import jax.numpy as jnp
from jax import lax
from jax.experimental import pallas as pl
from jax.experimental.pallas import tpu as pltpu
from jax.sharding import PartitionSpec as P

SUBSTEPS = 4
LEV = 32
NXC = 64
LANES = 128
DEVICES = 128
COLS = 256
FIELDS = 6
SUB = 8
INNER = NXC // SUB
GCM_ROWS = FIELDS * LEV * 2
CRM_CHUNK = 8
ALPHA = 0.3 * math.log2(math.e)
BETA = 1.5 * ALPHA
SHIFT = math.log2(0.5 * BETA)
MIB = 1 << 20


def pieces(x):
    first = x.astype(jnp.bfloat16)
    rest = x - first.astype(jnp.float32)
    second = rest.astype(jnp.bfloat16)
    third = (rest - second.astype(jnp.float32)).astype(jnp.bfloat16)
    return first, second, third


def select_dot(x, chosen, dims, x_first):
    total = None
    for part in pieces(x):
        pair = (part, chosen) if x_first else (chosen, part)
        term = lax.dot_general(*pair, (dims, ((), ())), preferred_element_type=jnp.float32)
        total = term if total is None else total + term
    return total


def rows_of(ref, y):
    return ref[pl.ds(y, FIELDS * LEV, stride=2), :]


def load_kernel(
    gcm_hbm, owner_hbm, branch_hbm, diffusion_hbm,
    gcm, to_core_mate, to_neighbour, owner, branch, diffusion, arrival,
):
    step = GCM_ROWS // FIELDS
    pairs = [
        (gcm_hbm.at[pl.ds(f * step, step)], gcm.at[pl.ds(f * step, step)]) for f in range(FIELDS)
    ]
    pairs += [(owner_hbm, owner), (branch_hbm, branch), (diffusion_hbm, diffusion)]
    loads = [
        pltpu.make_async_copy(source, target, arrival.at[n])
        for n, (source, target) in enumerate(pairs)
    ]
    for copy in loads:
        copy.start()
    for copy in loads:
        copy.wait()
    core = lax.rem(lax.axis_index("blk"), 2)
    rows = [rows_of(gcm, 0), rows_of(gcm, 1)]
    to_core_mate[...] = jnp.where(core == 0, rows[1], rows[0])
    to_neighbour[: FIELDS * LEV, :] = jnp.where(core == 0, rows[0], rows[1])
    to_neighbour[FIELDS * LEV :, :] = jnp.zeros((SUB, LANES), jnp.float32)


def edge_kernel(
    gcm, owner, branch, diffusion, to_chip_mate, to_other, routes, rates, number
):
    to_chip_mate[...] = jnp.zeros_like(to_chip_mate)
    to_other[...] = jnp.zeros_like(to_other)
    device = lax.broadcasted_iota(jnp.int32, (DEVICES, LANES), 0)
    target = jnp.concatenate(
        [(device == owner[y : y + 1, :]).astype(jnp.float32) for y in range(2)], axis=1
    )
    earlier = (
        lax.broadcasted_iota(jnp.int32, (COLS, COLS), 0)
        < lax.broadcasted_iota(jnp.int32, (COLS, COLS), 1)
    ).astype(jnp.bfloat16)
    count = jnp.dot(target.astype(jnp.bfloat16), earlier, preferred_element_type=jnp.float32)
    for slot in range(2):
        here = jnp.where(count < 0.5, 1.0 - slot, 0.0 + slot)
        routes[slot] = (target * here).astype(jnp.bfloat16)
    rates[...] = jnp.where(branch[...] == 1, 0.6, 0.2)
    for f in range(FIELDS):
        spread = jnp.broadcast_to(diffusion[f : f + 1, :], (LANES, LEV))
        number[f * LEV : (f + 1) * LEV, :] = jnp.transpose(spread)

    even = lax.rem(lax.axis_index("sub"), 2) == 0
    rows = jnp.concatenate([rows_of(gcm, 0), rows_of(gcm, 1)], axis=0)
    for part in range(GCM_ROWS // LANES):
        turned = jnp.transpose(rows[part * LANES : (part + 1) * LANES])
        first, last = turned[:1], turned[LANES - 1 :]
        to_chip_mate[part : part + 1, :] = jnp.where(even, last, first)
        to_other[part : part + 1, :] = jnp.where(even, first, last)


def tree(parts):
    while len(parts) > 1:
        parts = [a + b for a, b in zip(parts[::2], parts[1::2])]
    return parts[0]


def folded(ref, *lead):
    return tree([ref[(*lead, pl.ds(part, LEV, stride=SUB), slice(None))] for part in range(SUB)])


def early_kernel(crm_hbm, gcm, number, state, means, partial, crm, sums, arrival):
    loads = [
        pltpu.make_async_copy(
            crm_hbm.at[f, pl.ds(part * CRM_CHUNK, CRM_CHUNK)],
            crm.at[f, pl.ds(part * CRM_CHUNK, CRM_CHUNK)],
            arrival.at[f, part],
        )
        for f in range(2)
        for part in range(LEV // CRM_CHUNK)
    ]
    for copy in loads:
        copy.start()
    lane = lax.broadcasted_iota(jnp.int32, (FIELDS * LEV, LANES), 1)
    own = [rows_of(gcm, 0), rows_of(gcm, 1)]
    for y in range(2):
        before = jnp.where(lane == 0, 0.0, pltpu.roll(own[y], 1, axis=1))
        after = jnp.where(lane == LANES - 1, 0.0, pltpu.roll(own[y], LANES - 1, axis=1))
        around = own[1 - y] + after + before
        partial[y] = own[y] + number[...] * (around - 4.0 * own[y])

    for f, (scale, shift) in enumerate([(ALPHA, SHIFT), (BETA, 0.0)]):
        for part in range(LEV // CRM_CHUNK):
            loads[f * (LEV // CRM_CHUNK) + part].wait()

            def level(n, carry):
                k = part * CRM_CHUNK + n
                for half in range(2):
                    x = crm[f, k, :, half * LANES : (half + 1) * LANES].astype(jnp.float32)
                    x = x * scale + shift
                    total = None
                    for row in range(SUB):
                        block = x[row * INNER : (row + 1) * INNER]
                        state[f, half, pl.ds(k * NXC + row, INNER, stride=SUB), :] = block
                        total = block if total is None else total + block
                    sums[f, half, pl.ds(pl.multiple_of(k * SUB, SUB), SUB), :] = total
                return carry

            lax.fori_loop(0, CRM_CHUNK, level, 0, unroll=4)
    for f in range(2):
        for half in range(2):
            means[f, half] = folded(sums, f, half) * (1.0 / NXC)


def column_values(state, rate):
    level = lax.broadcasted_iota(jnp.int32, (LEV, LANES), 0)
    field = [state[f * LEV : (f + 1) * LEV] for f in range(FIELDS)]
    warm = ALPHA * (0.25 * field[0] + 0.2 * field[4])
    wet = BETA * (0.25 * field[1] + 0.2 * field[5])
    drift = 0.45 * jnp.tanh(field[2])
    tilt = jnp.tanh(field[3])
    rise = 0.15 * (tilt + pltpu.roll(tilt, LEV - 1, axis=0))
    rise = jnp.where(level == LEV - 1, rate, rise)
    return jnp.concatenate([warm, wet, drift, rise], axis=0)


def placed(values, routes, slot, y):
    route = routes[slot, :, pl.ds(pl.multiple_of(y * LANES, LANES), LANES)]
    return select_dot(values, route, ((1,), (1,)), False)


def inner_kernel(
    partial, number, core_mate, other, chip_mate, routes, rates, outer, done, advanced
):
    lane = lax.broadcasted_iota(jnp.int32, (FIELDS * LEV, LANES), 1)
    core = lax.rem(lax.axis_index("blk"), 2)

    def columns(ref):
        turned = jnp.transpose(ref)
        column = jnp.concatenate([turned[:, n : n + 1] for n in range(GCM_ROWS // LANES)], axis=0)
        return column[: FIELDS * LEV], column[FIELDS * LEV :]

    even = lax.rem(lax.axis_index("sub"), 2) == 0
    near, far = chip_mate[...], other[...]
    west, east = columns(jnp.where(even, far, near)), columns(jnp.where(even, near, far))
    rows = []
    for y in range(2):
        side = jnp.where(lane == 0, west[y], jnp.where(lane == LANES - 1, east[y], 0.0))
        rows.append(partial[y] + number[...] * side)
    outer[...] = jnp.where(core == 0, rows[0], rows[1])
    state = jnp.where(core == 0, rows[1], rows[0]) + number[...] * core_mate[...]
    advanced[...] = state[2 * LEV :]
    values = column_values(state, rates[pl.ds(1 - core, 1), :])
    for slot in range(2):
        done[slot] = placed(values, routes, slot, 1 - core)


def outer_kernel(
    outer, number, neighbour, routes, rates, done, inner_advanced, advanced, outgoing
):
    core = lax.rem(lax.axis_index("blk"), 2)
    state = outer[...] + number[...] * neighbour[: FIELDS * LEV, :]
    here, there = state[2 * LEV :], inner_advanced[...]
    advanced[pl.ds(0, 4 * LEV, stride=2), :] = jnp.where(core == 0, here, there)
    advanced[pl.ds(1, 4 * LEV, stride=2), :] = jnp.where(core == 0, there, here)
    values = column_values(state, rates[pl.ds(core, 1), :])
    for slot in range(2):
        outgoing[pl.ds(slot, DEVICES, stride=2), :] = done[slot] + placed(
            values, routes, slot, core
        )


def cloud_kernel(
    incoming, start, means, advanced, outgoing, gcm_next,
    state, coef, mean, total, square, departure,
):
    leaving = pltpu.make_async_copy(
        advanced, gcm_next.at[pl.ds(2 * 2 * LEV, 4 * 2 * LEV)], departure
    )
    leaving.start()
    level = lax.broadcasted_iota(jnp.int32, (LEV, LANES), 0)
    top = level == LEV - 1
    rates = []

    def up(x):
        return pltpu.roll(x, LEV - 1, axis=0)

    def down(x):
        return pltpu.roll(x, 1, axis=0)

    for half in range(2):
        values = jnp.transpose(incoming[half * LANES : (half + 1) * LANES, :])
        rise = values[3 * LEV :]
        rates.append(rise[LEV - 1 :])
        rise = jnp.where(top, 0.0, rise)
        base = SHIFT * (1.0 - rise + down(rise))
        coef[0, half] = values[:LEV] + SHIFT - 0.75 * base
        coef[1, half] = values[LEV : 2 * LEV]
        coef[2, half] = values[2 * LEV : 3 * LEV]
        coef[3, half] = rise
        coef[7, half] = jnp.broadcast_to(rates[half], (LEV, LANES))
        coef[9, half] = jnp.abs(coef[2, half])

    def lifted(x, rise):
        flux = rise * jnp.where(rise > 0.0, x, up(x))
        return x - flux + down(flux)

    def settled(half):
        rain = folded(total, half) * (1.0 / NXC) + coef[8, half]
        return mean[0, half] + rain, mean[1, half] - rain, mean[2, half] + rain

    def relax(first):
        for half in range(2):
            rise, rate = coef[3, half], coef[7, half]
            if first:
                before = means[0, half], means[1, half]
                mean[2, half] = jnp.zeros((LEV, LANES), jnp.float32)
            else:
                *before, mean[2, half] = settled(half)
            now = [lifted(x, rise) for x in before]
            add = [coef[f, half] - 0.25 * now[f] for f in range(2)]
            offset = add[1]
            if first:
                coef[4, half] = add[0]
            else:
                kept = lifted(mean[3, half], rise)
                owed = rate * kept
                offset = offset + (kept - owed)
                coef[4, half] = add[0] + owed
            mean[3, half] = offset
            coef[5, half] = -offset
            lacking = rate * offset
            coef[8, half] = lacking
            mean[0, half] = now[0] + add[0]
            mean[1, half] = now[1] + add[1]
            coef[6, half] = now[0] + add[0] - lacking

    def sweep(source, half, last):
        rate = jnp.broadcast_to(coef[7, half, 0:1, :], (SUB, LANES))

        def row(index, k):
            return jnp.broadcast_to(coef[index, half, k : k + 1, :], (SUB, LANES))

        def drifted(f, k, size, positive):
            cells = [
                source[f, half, k * NXC + j * SUB : k * NXC + (j + 1) * SUB, :]
                for j in range(INNER)
            ]
            before = [pltpu.roll(cells[-1], 1, axis=0)] + cells[:-1]
            after = cells[1:] + [pltpu.roll(cells[0], SUB - 1, axis=0)]
            return [
                c + size * (jnp.where(positive, b, a) - c)
                for c, b, a in zip(cells, before, after)
            ]

        def level_of(k):
            drift = row(2, k)
            size, positive = row(9, k), drift > 0.0
            return [drifted(f, k, size, positive) for f in range(2)]

        now = level_of(0)
        below = None
        for k in range(LEV):
            gain, least = row(4, k), row(5, k)
            if k < LEV - 1:
                after = level_of(k + 1)
                rise = row(3, k)
                upward = rise > 0.0
                flux = [
                    [rise * jnp.where(upward, a, b) for a, b in zip(now[f], after[f])]
                    for f in range(2)
                ]
            rained, spread = [], []
            if last:
                middle = row(6, k)
            for j in range(INNER):
                new = []
                for f in range(2):
                    x = now[f][j]
                    if k < LEV - 1:
                        x = x - flux[f][j]
                    if k > 0:
                        x = x + below[f][j]
                    new.append(x)
                temper, moisture = new
                temper = temper + gain
                rain = rate * jnp.maximum(moisture - jnp.exp2(temper), least)
                temper = temper + rain
                rained.append(rain)
                if last:
                    away = temper - middle
                    spread.append(away * away)
                else:
                    at = slice(k * NXC + j * SUB, k * NXC + (j + 1) * SUB)
                    state[0, half, at, :] = temper
                    state[1, half, at, :] = moisture - rain
            total[half, k * SUB : (k + 1) * SUB, :] = tree(rained)
            if last:
                square[half, k * SUB : (k + 1) * SUB, :] = tree(spread)
            if k < LEV - 1:
                below, now = flux, after

    def substep(source, first, last):
        relax(first)

        def half_of(half, carry):
            sweep(source, half, last)
            return carry

        lax.fori_loop(0, 2, half_of, 0)

    substep(start, True, False)

    def middle_step(step, carry):
        substep(state, False, False)
        return carry

    lax.fori_loop(0, SUBSTEPS - 2, middle_step, 0)
    substep(state, False, True)
    for half in range(2):
        warm, wet, rain = settled(half)
        gap = warm - coef[6, half] - coef[8, half]
        spread = folded(square, half) * (1.0 / NXC) - gap * gap
        result = [
            (warm - SHIFT) * (1.0 / ALPHA),
            wet * (1.0 / BETA),
            rain * (1.0 / BETA),
            spread * (1.0 / (ALPHA * ALPHA)),
        ]
        outgoing[half * LANES : (half + 1) * LANES, :] = jnp.transpose(
            jnp.concatenate(result, axis=0)
        )
    leaving.wait()


def home_kernel(returned, routes, begun, gcm_next, stats):
    del begun
    home = None
    for slot in range(2):
        back = returned[pl.ds(slot, DEVICES, stride=2), :]
        term = select_dot(jnp.transpose(back), routes[slot], ((1,), (0,)), True)
        home = term if home is None else home + term
    for y in range(2):
        part = home[:, y * LANES : (y + 1) * LANES]
        gcm_next[pl.ds(y, 2 * LEV, stride=2), :] = part[: 2 * LEV]
        stats[pl.ds(y, 2 * LEV, stride=2), :] = part[2 * LEV :]


def whole(shape):
    return pl.BlockSpec(shape, lambda *_: (0,) * len(shape))


def f32(*shape):
    return jax.ShapeDtypeStruct(shape, jnp.float32)


def in_hbm(x):
    return pltpu.with_memory_space_constraint(x, pltpu.HBM)


def transfer(rows):
    moved = lax.all_to_all(
        rows.reshape(DEVICES, 2, LANES), ("blk", "sub"), split_axis=0, concat_axis=0, tiled=True
    )
    return moved.reshape(COLS, LANES)


def body(gcm_state, crm_state, owner, branch, diffusion):
    gcm = gcm_state.reshape(GCM_ROWS, LANES)

    def pairs(n, first):
        ahead = [(i, (i + 1) % n) for i in range(first, n, 2)]
        return ahead + [(j, i) for i, j in ahead]

    n_blk, n_sub = lax.axis_size("blk"), lax.axis_size("sub")
    hbm = pl.BlockSpec(memory_space=pltpu.HBM)
    gcm_here, to_core_mate, to_neighbour, owner_here, branch_here, diffusion_here = pl.pallas_call(
        load_kernel,
        in_specs=[hbm] * 4,
        out_shape=(
            f32(GCM_ROWS, LANES),
            f32(FIELDS * LEV, LANES),
            f32(FIELDS * LEV + SUB, LANES),
            jax.ShapeDtypeStruct(owner.shape, owner.dtype),
            jax.ShapeDtypeStruct(branch.shape, branch.dtype),
            f32(*diffusion.shape),
        ),
        scratch_shapes=[pltpu.SemaphoreType.DMA((FIELDS + 3,))],
        compiler_params=pltpu.CompilerParams(vmem_limit_bytes=4 * MIB),
        name="load",
    )(*map(in_hbm, (gcm, owner, branch, diffusion)))
    neighbour = lax.ppermute(to_neighbour, "blk", pairs(n_blk, 1))
    core_mate = lax.ppermute(to_core_mate, "blk", pairs(n_blk, 0))
    to_chip_mate, to_other, routes, rates, number = pl.pallas_call(
        edge_kernel,
        out_shape=(
            f32(SUB, LANES),
            f32(SUB, LANES),
            jax.ShapeDtypeStruct((2, DEVICES, COLS), jnp.bfloat16),
            f32(2, LANES),
            f32(FIELDS * LEV, LANES),
        ),
        compiler_params=pltpu.CompilerParams(vmem_limit_bytes=4 * MIB),
        name="edges",
    )(gcm_here, owner_here, branch_here, diffusion_here)
    chip_mate = lax.ppermute(to_chip_mate, "sub", pairs(n_sub, 0))
    other = lax.ppermute(to_other, "sub", pairs(n_sub, 1))
    cells = 2 * LEV * NXC * COLS
    state, means, partial = pl.pallas_call(
        early_kernel,
        in_specs=[hbm, whole((GCM_ROWS, LANES)), whole((FIELDS * LEV, LANES))],
        out_shape=(
            f32(2, 2, LEV * NXC, LANES),
            f32(2, 2, LEV, LANES),
            f32(2, FIELDS * LEV, LANES),
        ),
        scratch_shapes=[
            pltpu.VMEM((2, LEV, NXC, COLS), jnp.bfloat16),
            pltpu.VMEM((2, 2, LEV * SUB, LANES), jnp.float32),
            pltpu.SemaphoreType.DMA((2, LEV // CRM_CHUNK)),
        ],
        compiler_params=pltpu.CompilerParams(vmem_limit_bytes=16 * MIB),
        cost_estimate=pl.CostEstimate(flops=4 * cells, bytes_accessed=6 * cells, transcendentals=0),
        name="early",
    )(in_hbm(crm_state), gcm_here, number)
    outer, done, inner_advanced = pl.pallas_call(
        inner_kernel,
        out_shape=(
            f32(FIELDS * LEV, LANES),
            f32(2, DEVICES, LANES),
            f32(4 * LEV, LANES),
        ),
        compiler_params=pltpu.CompilerParams(vmem_limit_bytes=8 * MIB),
        name="inner",
    )(partial, number, core_mate, other, chip_mate, routes, rates)
    advanced, outgoing = pl.pallas_call(
        outer_kernel,
        out_shape=(f32(4 * 2 * LEV, LANES), f32(COLS, LANES)),
        compiler_params=pltpu.CompilerParams(vmem_limit_bytes=8 * MIB),
        name="outer",
    )(outer, number, neighbour, routes, rates, done, inner_advanced)

    incoming = transfer(outgoing)
    profiles, gcm_next = pl.pallas_call(
        cloud_kernel,
        out_specs=(whole((COLS, LANES)), hbm),
        out_shape=(f32(COLS, LANES), f32(GCM_ROWS, LANES)),
        scratch_shapes=[
            pltpu.VMEM((2, 2, LEV * NXC, LANES), jnp.float32),
            pltpu.VMEM((10, 2, LEV, LANES), jnp.float32),
            pltpu.VMEM((4, 2, LEV, LANES), jnp.float32),
            pltpu.VMEM((2, LEV * SUB, LANES), jnp.float32),
            pltpu.VMEM((2, LEV * SUB, LANES), jnp.float32),
            pltpu.SemaphoreType.DMA(()),
        ],
        compiler_params=pltpu.CompilerParams(vmem_limit_bytes=12 * MIB),
        name="cloud",
    )(incoming, state, means, advanced)
    returned = transfer(profiles)

    gcm_next, stats = pl.pallas_call(
        home_kernel,
        grid=(1,),
        in_specs=[
            whole((COLS, LANES)),
            whole((2, DEVICES, COLS)),
            pl.BlockSpec(memory_space=pl.ANY),
        ],
        out_specs=(whole((4 * LEV, LANES)), whole((4 * LEV, LANES))),
        out_shape=(f32(GCM_ROWS, LANES), f32(4 * LEV, LANES)),
        input_output_aliases={2: 0},
        compiler_params=pltpu.CompilerParams(vmem_limit_bytes=8 * MIB),
        name="home",
    )(returned, routes, gcm_next)
    return gcm_next.reshape(gcm_state.shape), stats.reshape(2, LEV, 2, LANES)


def solution(mesh):
    grid = P(None, None, "blk", "sub")
    return jax.shard_map(
        body,
        mesh=mesh,
        in_specs=(grid, P(None, None, None, ("blk", "sub")), P("blk", "sub"), P("blk", "sub"), P()),
        out_specs=(grid, grid),
        check_vma=False,
    )
```

```python
import math

import jax
import jax.numpy as jnp
from jax import lax
from jax.experimental import pallas as pl
from jax.experimental.pallas import tpu as pltpu
from jax.sharding import PartitionSpec as P

SUBSTEPS = 4
LEV = 32
NXC = 64
LANES = 128
DEVICES = 128
COLS = 256
FIELDS = 6
SUB = 8
INNER = NXC // SUB
GCM_ROWS = FIELDS * LEV * 2
CRM_CHUNK = 8
ALPHA = 0.3 * math.log2(math.e)
BETA = 1.5 * ALPHA
SHIFT = math.log2(0.5 * BETA)
MIB = 1 << 20


def pieces(x):
    first = x.astype(jnp.bfloat16)
    return first, (x - first.astype(jnp.float32)).astype(jnp.bfloat16)


def select_dot(x, chosen, dims, x_first):
    total = None
    for part in pieces(x):
        pair = (part, chosen) if x_first else (chosen, part)
        term = lax.dot_general(*pair, (dims, ((), ())), preferred_element_type=jnp.float32)
        total = term if total is None else total + term
    return total


def rows_of(ref, y):
    return ref[pl.ds(y, FIELDS * LEV, stride=2), :]


def load_kernel(
    gcm_hbm, owner_hbm, branch_hbm, diffusion_hbm,
    gcm, to_core_mate, to_neighbour, owner, branch, diffusion, arrival,
):
    loads = [
        pltpu.make_async_copy(source, target, arrival.at[n])
        for n, (source, target) in enumerate(
            [(gcm_hbm, gcm), (owner_hbm, owner), (branch_hbm, branch), (diffusion_hbm, diffusion)]
        )
    ]
    for copy in loads:
        copy.start()
    for copy in loads:
        copy.wait()
    core = lax.rem(lax.axis_index("blk"), 2)
    rows = [rows_of(gcm, 0), rows_of(gcm, 1)]
    to_core_mate[...] = jnp.where(core == 0, rows[1], rows[0])
    to_neighbour[: FIELDS * LEV, :] = jnp.where(core == 0, rows[0], rows[1])
    to_neighbour[FIELDS * LEV :, :] = jnp.zeros((SUB, LANES), jnp.float32)


def edge_kernel(
    gcm, owner, branch, diffusion, to_chip_mate, to_other, routes, rates, number
):
    to_chip_mate[...] = jnp.zeros_like(to_chip_mate)
    to_other[...] = jnp.zeros_like(to_other)
    device = lax.broadcasted_iota(jnp.int32, (DEVICES, LANES), 0)
    target = jnp.concatenate(
        [(device == owner[y : y + 1, :]).astype(jnp.float32) for y in range(2)], axis=1
    )
    earlier = (
        lax.broadcasted_iota(jnp.int32, (COLS, COLS), 0)
        < lax.broadcasted_iota(jnp.int32, (COLS, COLS), 1)
    ).astype(jnp.bfloat16)
    count = jnp.dot(target.astype(jnp.bfloat16), earlier, preferred_element_type=jnp.float32)
    for slot in range(2):
        here = jnp.where(count < 0.5, 1.0 - slot, 0.0 + slot)
        routes[slot] = (target * here).astype(jnp.bfloat16)
    rates[...] = jnp.where(branch[...] == 1, 0.6, 0.2)
    for f in range(FIELDS):
        spread = jnp.broadcast_to(diffusion[f : f + 1, :], (LANES, LEV))
        number[f * LEV : (f + 1) * LEV, :] = jnp.transpose(spread)

    even = lax.rem(lax.axis_index("sub"), 2) == 0
    rows = jnp.concatenate([rows_of(gcm, 0), rows_of(gcm, 1)], axis=0)
    for part in range(GCM_ROWS // LANES):
        turned = jnp.transpose(rows[part * LANES : (part + 1) * LANES])
        first, last = turned[:1], turned[LANES - 1 :]
        to_chip_mate[part : part + 1, :] = jnp.where(even, last, first)
        to_other[part : part + 1, :] = jnp.where(even, first, last)


def tree(parts):
    while len(parts) > 1:
        parts = [a + b for a, b in zip(parts[::2], parts[1::2])]
    return parts[0]


def folded(ref, *lead):
    return tree([ref[(*lead, pl.ds(part, LEV, stride=SUB), slice(None))] for part in range(SUB)])


def early_kernel(crm_hbm, gcm, number, state, means, partial, crm, sums, arrival):
    loads = [
        pltpu.make_async_copy(
            crm_hbm.at[f, pl.ds(part * CRM_CHUNK, CRM_CHUNK)],
            crm.at[f, pl.ds(part * CRM_CHUNK, CRM_CHUNK)],
            arrival.at[f, part],
        )
        for f in range(2)
        for part in range(LEV // CRM_CHUNK)
    ]
    for copy in loads:
        copy.start()
    lane = lax.broadcasted_iota(jnp.int32, (FIELDS * LEV, LANES), 1)
    own = [rows_of(gcm, 0), rows_of(gcm, 1)]
    for y in range(2):
        before = jnp.where(lane == 0, 0.0, pltpu.roll(own[y], 1, axis=1))
        after = jnp.where(lane == LANES - 1, 0.0, pltpu.roll(own[y], LANES - 1, axis=1))
        around = own[1 - y] + after + before
        partial[y] = own[y] + number[...] * (around - 4.0 * own[y])

    for f, (scale, shift) in enumerate([(ALPHA, SHIFT), (BETA, 0.0)]):
        for part in range(LEV // CRM_CHUNK):
            loads[f * (LEV // CRM_CHUNK) + part].wait()

            def level(n, carry):
                k = part * CRM_CHUNK + n
                for half in range(2):
                    x = crm[f, k, :, half * LANES : (half + 1) * LANES].astype(jnp.float32)
                    x = x * scale + shift
                    total = None
                    for row in range(SUB):
                        block = x[row * INNER : (row + 1) * INNER]
                        state[f, half, pl.ds(k * NXC + row, INNER, stride=SUB), :] = block
                        total = block if total is None else total + block
                    sums[f, half, pl.ds(pl.multiple_of(k * SUB, SUB), SUB), :] = total
                return carry

            lax.fori_loop(0, CRM_CHUNK, level, 0, unroll=4)
    for f in range(2):
        for half in range(2):
            means[f, half] = folded(sums, f, half) * (1.0 / NXC)


def column_values(state, rate):
    level = lax.broadcasted_iota(jnp.int32, (LEV, LANES), 0)
    field = [state[f * LEV : (f + 1) * LEV] for f in range(FIELDS)]
    warm = ALPHA * (0.25 * field[0] + 0.2 * field[4])
    wet = BETA * (0.25 * field[1] + 0.2 * field[5])
    drift = 0.45 * jnp.tanh(field[2])
    tilt = jnp.tanh(field[3])
    rise = 0.15 * (tilt + pltpu.roll(tilt, LEV - 1, axis=0))
    rise = jnp.where(level == LEV - 1, rate, rise)
    return jnp.concatenate([warm, wet, drift, rise], axis=0)


def placed(values, routes, slot, y):
    route = routes[slot, :, pl.ds(pl.multiple_of(y * LANES, LANES), LANES)]
    return select_dot(values, route, ((1,), (1,)), False)


def inner_kernel(
    partial, number, core_mate, other, chip_mate, routes, rates, outer, done, advanced
):
    lane = lax.broadcasted_iota(jnp.int32, (FIELDS * LEV, LANES), 1)
    core = lax.rem(lax.axis_index("blk"), 2)

    def columns(ref):
        turned = jnp.transpose(ref)
        column = jnp.concatenate([turned[:, n : n + 1] for n in range(GCM_ROWS // LANES)], axis=0)
        return column[: FIELDS * LEV], column[FIELDS * LEV :]

    even = lax.rem(lax.axis_index("sub"), 2) == 0
    near, far = chip_mate[...], other[...]
    west, east = columns(jnp.where(even, far, near)), columns(jnp.where(even, near, far))
    rows = []
    for y in range(2):
        side = jnp.where(lane == 0, west[y], jnp.where(lane == LANES - 1, east[y], 0.0))
        rows.append(partial[y] + number[...] * side)
    outer[...] = jnp.where(core == 0, rows[0], rows[1])
    state = jnp.where(core == 0, rows[1], rows[0]) + number[...] * core_mate[...]
    advanced[...] = state[2 * LEV :]
    values = column_values(state, rates[pl.ds(1 - core, 1), :])
    for slot in range(2):
        done[slot] = placed(values, routes, slot, 1 - core)


def outer_kernel(
    outer, number, neighbour, routes, rates, done, inner_advanced, advanced, outgoing
):
    core = lax.rem(lax.axis_index("blk"), 2)
    state = outer[...] + number[...] * neighbour[: FIELDS * LEV, :]
    here, there = state[2 * LEV :], inner_advanced[...]
    advanced[pl.ds(0, 4 * LEV, stride=2), :] = jnp.where(core == 0, here, there)
    advanced[pl.ds(1, 4 * LEV, stride=2), :] = jnp.where(core == 0, there, here)
    values = column_values(state, rates[pl.ds(core, 1), :])
    for slot in range(2):
        outgoing[pl.ds(slot, DEVICES, stride=2), :] = done[slot] + placed(
            values, routes, slot, core
        )


def cloud_kernel(
    incoming, start, means, advanced, outgoing, gcm_next,
    state, coef, mean, total, square, departure,
):
    leaving = pltpu.make_async_copy(
        advanced, gcm_next.at[pl.ds(2 * 2 * LEV, 4 * 2 * LEV)], departure
    )
    leaving.start()
    level = lax.broadcasted_iota(jnp.int32, (LEV, LANES), 0)
    top = level == LEV - 1
    rates = []

    def up(x):
        return pltpu.roll(x, LEV - 1, axis=0)

    def down(x):
        return pltpu.roll(x, 1, axis=0)

    for half in range(2):
        values = jnp.transpose(incoming[half * LANES : (half + 1) * LANES, :])
        rise = values[3 * LEV :]
        rates.append(rise[LEV - 1 :])
        rise = jnp.where(top, 0.0, rise)
        base = SHIFT * (1.0 - rise + down(rise))
        coef[0, half] = values[:LEV] + SHIFT - 0.75 * base
        coef[1, half] = values[LEV : 2 * LEV]
        coef[2, half] = values[2 * LEV : 3 * LEV]
        coef[3, half] = rise
        coef[7, half] = jnp.broadcast_to(rates[half], (LEV, LANES))
        coef[9, half] = jnp.abs(coef[2, half])

    def lifted(x, rise):
        flux = rise * jnp.where(rise > 0.0, x, up(x))
        return x - flux + down(flux)

    def settled(half):
        rain = folded(total, half) * (1.0 / NXC) + coef[8, half]
        return mean[0, half] + rain, mean[1, half] - rain, mean[2, half] + rain

    def relax(first):
        for half in range(2):
            rise, rate = coef[3, half], coef[7, half]
            if first:
                before = means[0, half], means[1, half]
                mean[2, half] = jnp.zeros((LEV, LANES), jnp.float32)
            else:
                *before, mean[2, half] = settled(half)
            now = [lifted(x, rise) for x in before]
            add = [coef[f, half] - 0.25 * now[f] for f in range(2)]
            offset = add[1]
            if first:
                coef[4, half] = add[0]
            else:
                kept = lifted(mean[3, half], rise)
                owed = rate * kept
                offset = offset + (kept - owed)
                coef[4, half] = add[0] + owed
            mean[3, half] = offset
            coef[5, half] = -offset
            lacking = rate * offset
            coef[8, half] = lacking
            mean[0, half] = now[0] + add[0]
            mean[1, half] = now[1] + add[1]
            coef[6, half] = now[0] + add[0] - lacking

    def sweep(source, half, last):
        rate = jnp.broadcast_to(coef[7, half, 0:1, :], (SUB, LANES))

        def row(index, k):
            return jnp.broadcast_to(coef[index, half, k : k + 1, :], (SUB, LANES))

        def drifted(f, k, size, positive):
            cells = [
                source[f, half, k * NXC + j * SUB : k * NXC + (j + 1) * SUB, :]
                for j in range(INNER)
            ]
            before = [pltpu.roll(cells[-1], 1, axis=0)] + cells[:-1]
            after = cells[1:] + [pltpu.roll(cells[0], SUB - 1, axis=0)]
            return [
                c + size * (jnp.where(positive, b, a) - c)
                for c, b, a in zip(cells, before, after)
            ]

        def level_of(k):
            drift = row(2, k)
            size, positive = row(9, k), drift > 0.0
            return [drifted(f, k, size, positive) for f in range(2)]

        now = level_of(0)
        below = None
        for k in range(LEV):
            gain, least = row(4, k), row(5, k)
            if k < LEV - 1:
                after = level_of(k + 1)
                rise = row(3, k)
                upward = rise > 0.0
                flux = [
                    [rise * jnp.where(upward, a, b) for a, b in zip(now[f], after[f])]
                    for f in range(2)
                ]
            rained, spread = [], []
            if last:
                middle = row(6, k)
            for j in range(INNER):
                new = []
                for f in range(2):
                    x = now[f][j]
                    if k < LEV - 1:
                        x = x - flux[f][j]
                    if k > 0:
                        x = x + below[f][j]
                    new.append(x)
                temper, moisture = new
                temper = temper + gain
                rain = rate * jnp.maximum(moisture - jnp.exp2(temper), least)
                temper = temper + rain
                rained.append(rain)
                if last:
                    away = temper - middle
                    spread.append(away * away)
                else:
                    at = slice(k * NXC + j * SUB, k * NXC + (j + 1) * SUB)
                    state[0, half, at, :] = temper
                    state[1, half, at, :] = moisture - rain
            total[half, k * SUB : (k + 1) * SUB, :] = tree(rained)
            if last:
                square[half, k * SUB : (k + 1) * SUB, :] = tree(spread)
            if k < LEV - 1:
                below, now = flux, after

    def substep(source, first, last):
        relax(first)

        def half_of(half, carry):
            sweep(source, half, last)
            return carry

        lax.fori_loop(0, 2, half_of, 0)

    substep(start, True, False)

    def middle_step(step, carry):
        substep(state, False, False)
        return carry

    lax.fori_loop(0, SUBSTEPS - 2, middle_step, 0)
    substep(state, False, True)
    for half in range(2):
        warm, wet, rain = settled(half)
        gap = warm - coef[6, half] - coef[8, half]
        spread = folded(square, half) * (1.0 / NXC) - gap * gap
        result = [
            (warm - SHIFT) * (1.0 / ALPHA),
            wet * (1.0 / BETA),
            rain * (1.0 / BETA),
            spread * (1.0 / (ALPHA * ALPHA)),
        ]
        outgoing[half * LANES : (half + 1) * LANES, :] = jnp.transpose(
            jnp.concatenate(result, axis=0)
        )
    leaving.wait()


def home_kernel(returned, routes, begun, gcm_next, stats):
    del begun
    home = None
    for slot in range(2):
        back = returned[pl.ds(slot, DEVICES, stride=2), :]
        term = select_dot(jnp.transpose(back), routes[slot], ((1,), (0,)), True)
        home = term if home is None else home + term
    for y in range(2):
        part = home[:, y * LANES : (y + 1) * LANES]
        gcm_next[pl.ds(y, 2 * LEV, stride=2), :] = part[: 2 * LEV]
        stats[pl.ds(y, 2 * LEV, stride=2), :] = part[2 * LEV :]


def whole(shape):
    return pl.BlockSpec(shape, lambda *_: (0,) * len(shape))


def f32(*shape):
    return jax.ShapeDtypeStruct(shape, jnp.float32)


def in_hbm(x):
    return pltpu.with_memory_space_constraint(x, pltpu.HBM)


def transfer(rows):
    moved = lax.all_to_all(
        rows.reshape(DEVICES, 2, LANES), ("blk", "sub"), split_axis=0, concat_axis=0, tiled=True
    )
    return moved.reshape(COLS, LANES)


def body(gcm_state, crm_state, owner, branch, diffusion):
    gcm = gcm_state.reshape(GCM_ROWS, LANES)

    def pairs(n, first):
        ahead = [(i, (i + 1) % n) for i in range(first, n, 2)]
        return ahead + [(j, i) for i, j in ahead]

    n_blk, n_sub = lax.axis_size("blk"), lax.axis_size("sub")
    hbm = pl.BlockSpec(memory_space=pltpu.HBM)
    gcm_here, to_core_mate, to_neighbour, owner_here, branch_here, diffusion_here = pl.pallas_call(
        load_kernel,
        in_specs=[hbm] * 4,
        out_shape=(
            f32(GCM_ROWS, LANES),
            f32(FIELDS * LEV, LANES),
            f32(FIELDS * LEV + SUB, LANES),
            jax.ShapeDtypeStruct(owner.shape, owner.dtype),
            jax.ShapeDtypeStruct(branch.shape, branch.dtype),
            f32(*diffusion.shape),
        ),
        scratch_shapes=[pltpu.SemaphoreType.DMA((4,))],
        compiler_params=pltpu.CompilerParams(vmem_limit_bytes=4 * MIB),
        name="load",
    )(*map(in_hbm, (gcm, owner, branch, diffusion)))
    neighbour = lax.ppermute(to_neighbour, "blk", pairs(n_blk, 1))
    core_mate = lax.ppermute(to_core_mate, "blk", pairs(n_blk, 0))
    to_chip_mate, to_other, routes, rates, number = pl.pallas_call(
        edge_kernel,
        out_shape=(
            f32(SUB, LANES),
            f32(SUB, LANES),
            jax.ShapeDtypeStruct((2, DEVICES, COLS), jnp.bfloat16),
            f32(2, LANES),
            f32(FIELDS * LEV, LANES),
        ),
        compiler_params=pltpu.CompilerParams(vmem_limit_bytes=4 * MIB),
        name="edges",
    )(gcm_here, owner_here, branch_here, diffusion_here)
    chip_mate = lax.ppermute(to_chip_mate, "sub", pairs(n_sub, 0))
    other = lax.ppermute(to_other, "sub", pairs(n_sub, 1))
    cells = 2 * LEV * NXC * COLS
    state, means, partial = pl.pallas_call(
        early_kernel,
        in_specs=[hbm, whole((GCM_ROWS, LANES)), whole((FIELDS * LEV, LANES))],
        out_shape=(
            f32(2, 2, LEV * NXC, LANES),
            f32(2, 2, LEV, LANES),
            f32(2, FIELDS * LEV, LANES),
        ),
        scratch_shapes=[
            pltpu.VMEM((2, LEV, NXC, COLS), jnp.bfloat16),
            pltpu.VMEM((2, 2, LEV * SUB, LANES), jnp.float32),
            pltpu.SemaphoreType.DMA((2, LEV // CRM_CHUNK)),
        ],
        compiler_params=pltpu.CompilerParams(vmem_limit_bytes=16 * MIB),
        cost_estimate=pl.CostEstimate(flops=4 * cells, bytes_accessed=6 * cells, transcendentals=0),
        name="early",
    )(in_hbm(crm_state), gcm_here, number)
    outer, done, inner_advanced = pl.pallas_call(
        inner_kernel,
        out_shape=(
            f32(FIELDS * LEV, LANES),
            f32(2, DEVICES, LANES),
            f32(4 * LEV, LANES),
        ),
        compiler_params=pltpu.CompilerParams(vmem_limit_bytes=8 * MIB),
        name="inner",
    )(partial, number, core_mate, other, chip_mate, routes, rates)
    advanced, outgoing = pl.pallas_call(
        outer_kernel,
        out_shape=(f32(4 * 2 * LEV, LANES), f32(COLS, LANES)),
        compiler_params=pltpu.CompilerParams(vmem_limit_bytes=8 * MIB),
        name="outer",
    )(outer, number, neighbour, routes, rates, done, inner_advanced)

    incoming = transfer(outgoing)
    profiles, gcm_next = pl.pallas_call(
        cloud_kernel,
        out_specs=(whole((COLS, LANES)), hbm),
        out_shape=(f32(COLS, LANES), f32(GCM_ROWS, LANES)),
        scratch_shapes=[
            pltpu.VMEM((2, 2, LEV * NXC, LANES), jnp.float32),
            pltpu.VMEM((10, 2, LEV, LANES), jnp.float32),
            pltpu.VMEM((4, 2, LEV, LANES), jnp.float32),
            pltpu.VMEM((2, LEV * SUB, LANES), jnp.float32),
            pltpu.VMEM((2, LEV * SUB, LANES), jnp.float32),
            pltpu.SemaphoreType.DMA(()),
        ],
        compiler_params=pltpu.CompilerParams(vmem_limit_bytes=12 * MIB),
        name="cloud",
    )(incoming, state, means, advanced)
    returned = transfer(profiles)

    gcm_next, stats = pl.pallas_call(
        home_kernel,
        grid=(1,),
        in_specs=[
            whole((COLS, LANES)),
            whole((2, DEVICES, COLS)),
            pl.BlockSpec(memory_space=pl.ANY),
        ],
        out_specs=(whole((4 * LEV, LANES)), whole((4 * LEV, LANES))),
        out_shape=(f32(GCM_ROWS, LANES), f32(4 * LEV, LANES)),
        input_output_aliases={2: 0},
        compiler_params=pltpu.CompilerParams(vmem_limit_bytes=8 * MIB),
        name="home",
    )(returned, routes, gcm_next)
    return gcm_next.reshape(gcm_state.shape), stats.reshape(2, LEV, 2, LANES)


def solution(mesh):
    grid = P(None, None, "blk", "sub")
    return jax.shard_map(
        body,
        mesh=mesh,
        in_specs=(grid, P(None, None, None, ("blk", "sub")), P("blk", "sub"), P("blk", "sub"), P()),
        out_specs=(grid, grid),
        check_vma=False,
    )
```
